256 devices in a mesh: space: 64 (over z, x, core), sub: 4 (over y).
Axes of the slice: x: 4, y: 4, z: 8, core: 2. Of those that a mesh axis runs over, the one named last changes fastest.
Arguments:
- trajectories: bfloat16 [300, 131072], P(None, ('space', 'sub')), may hold values from -6 to 6
- kernel_scale: bfloat16 [131072], P(('space', 'sub')), may hold values from 6.90625 to 17.25
- start_vectors: float32 [32, 131072], P(None, ('space', 'sub')), may hold values from -6 to 6
- pair_list: int32 [6144, 2], P(('space', 'sub')), may hold values from 0 to 511, as said below
Outputs:
- subspace: float32 [32, 131072], P(None, ('space', 'sub'))
The draws below stay inside these ranges and needn't reach their ends.
Inputs may be any that keep to these rules, and one draw needn't show every extreme that they name: `pair_list`: pairs in rows k * 12 * 2 to (k + 1) * 12 * 2 - 1 have their row block a in k * 2 to (k + 1) * 2 - 1, k being a device's index along space+sub. Every block appears once as (a, a). For every other pair, b lies on a device whose space index is that of a's device plus 1 to 3, modulo the size of the space axis. No pair appears twice.
All inputs are finite; a program needn't handle non-finite values.
Results may differ from the reference program's by a relative error of at most 0.0041.
Values may be sent and summed in bfloat16 or wider, within the bound.
No kernel may reach another device: no remote copies, remote signals or barrier semaphores. Data moves between devices by JAX's collectives and lax.ppermute only.
A program may use at most 64 MiB of HBM per device.

```python
import math
import jax
import jax.numpy as jnp
from jax import lax

FEAT = 300
BLOCK = 256
VECS = 32
BPD = 2
PAIRS_BLK = 12
REACH = 3
ITERS = 2
TRAJ = 131072
N_SPACE = 64
N_SUB = 4


def draw_pair_list(key, part):
    key = jax.random.fold_in(key, 7)
    device_count = N_SPACE * N_SUB
    others = (PAIRS_BLK - 1) * BPD
    candidates = BPD * BPD * REACH * N_SUB
    device_keys = jax.random.split(key, device_count)
    chosen = jax.vmap(lambda pick_key: jax.random.permutation(pick_key, candidates)[:others])(device_keys)
    device_ids = jnp.arange(device_count, dtype=jnp.int32)[:, None]
    space_at = device_ids // N_SUB
    row_pick = chosen % BPD
    rest = chosen // BPD
    col_pick = rest % BPD
    rest = rest // BPD
    sub_pick = rest % N_SUB
    hop_pick = rest // N_SUB + 1
    col_device = (space_at + hop_pick) % N_SPACE * N_SUB + sub_pick
    row_ids = device_ids * BPD + row_pick
    col_ids = col_device * BPD + col_pick
    self_ids = device_ids * BPD + jnp.arange(BPD, dtype=jnp.int32)[None, :]
    row_all = jnp.concatenate([self_ids, row_ids], 1).reshape(-1)
    col_all = jnp.concatenate([self_ids, col_ids], 1).reshape(-1)
    return jnp.stack([row_all, col_all], 1).astype(jnp.int32)


def draw_trajectories(key, part):
    key = jax.random.fold_in(key, 11)
    center_key, label_key, noise_key = jax.random.split(key, 3)
    cluster_count = 128
    labels = jax.random.randint(label_key, (TRAJ,), 0, cluster_count)
    centers = jax.random.normal(center_key, (FEAT, cluster_count), jnp.float32)
    noise = jax.random.normal(noise_key, (FEAT, TRAJ), jnp.float32)
    spread = 0.3
    picked = jnp.take(centers, labels, axis=1)
    mixed = picked * (1.0 - spread * spread) ** 0.5 + noise * spread
    return jnp.clip(mixed, -6.0, 6.0).astype(jnp.bfloat16)


def steps_of(key, extent, cuts, smallest, high):
    def one(position, parts):
        draws = jax.random.uniform(jax.random.fold_in(jax.random.fold_in(key, 6), position), (parts,), jnp.float32, smallest / len(cuts), high / len(cuts))
        return jnp.repeat(jnp.exp(draws), extent[position] // parts).reshape((-1,) + (1,) * (len(extent) - position - 1))

    factor_of = one(*cuts[0])
    for cut in cuts[1:]:
        factor_of = factor_of * one(*cut)
    return factor_of


def normal_values(rng, extent, scale, reach, shards=(), kind=jnp.bfloat16):
    result = jax.random.normal(rng, extent, jnp.float32) * scale
    if len(shards) > 0:
        result = steps_of(rng, extent, shards, -0.22, 0.18) * result
    return jnp.clip(result, min=-reach, max=reach).astype(kind)


def setup_inputs(seed: int = 0) -> dict:
    keys = jax.random.split(jax.random.key(seed), 5)
    return {
        "trajectories": draw_trajectories(jax.random.fold_in(keys[4], 71), 0),
        "kernel_scale": jnp.clip(jnp.exp(math.log(17.25) - 0.91538534 * jax.random.uniform(keys[1], (TRAJ,), jnp.float32) ** steps_of(keys[1], (TRAJ,), ((0, 256),), -0.2, 0.2)), 6.90625, 17.25).astype(jnp.bfloat16),
        "start_vectors": normal_values(keys[2], (VECS, TRAJ), 1.0, 6.0, ((1, 256),), jnp.float32),
        "pair_list": draw_pair_list(jax.random.fold_in(keys[4], 71), 0),
    }


def similarity(row_data, col_data, row_band, col_band):
    crossed = jnp.dot(row_data.T.astype(jnp.float32), col_data.astype(jnp.float32), preferred_element_type=jnp.float32)
    row_norms = lax.optimization_barrier(jnp.sum(jnp.square(row_data.astype(jnp.float32)), 0))
    col_norms = lax.optimization_barrier(jnp.sum(jnp.square(col_data.astype(jnp.float32)), 0))
    scaling = row_band.astype(jnp.float32)[:, None] * col_band.astype(jnp.float32)[None, :]
    spread = row_norms[:, None] + col_norms[None, :] - 2.0 * crossed
    return jnp.exp(-spread / scaling).astype(jnp.bfloat16)

def sweep(trajectories, kernel_scale, vectors, pair_list):
    vec_count = vectors.shape[0]

    def advance(totals, pair_item):
        row_blk = pair_item[0].astype(jnp.int32) * BLOCK
        col_blk = pair_item[1].astype(jnp.int32) * BLOCK
        row_data = lax.dynamic_slice_in_dim(trajectories, row_blk, BLOCK, 1)
        col_data = lax.dynamic_slice_in_dim(trajectories, col_blk, BLOCK, 1)
        row_band = lax.dynamic_slice_in_dim(kernel_scale, row_blk, BLOCK, 0)
        col_band = lax.dynamic_slice_in_dim(kernel_scale, col_blk, BLOCK, 0)
        weights_tile = similarity(row_data, col_data, row_band, col_band)
        left_vec = lax.dynamic_slice_in_dim(vectors, row_blk, BLOCK, 1)
        right_vec = lax.dynamic_slice_in_dim(vectors, col_blk, BLOCK, 1)
        row_term = lax.dot_general(right_vec.astype(jnp.float32), weights_tile.astype(jnp.float32), (((1,), (1,)), ((), ())), preferred_element_type=jnp.float32)
        col_term = jnp.dot(left_vec.astype(jnp.float32), weights_tile.astype(jnp.float32), preferred_element_type=jnp.float32)
        col_term = col_term * (pair_item[0] != pair_item[1]).astype(jnp.float32)
        previous = lax.dynamic_slice_in_dim(totals, row_blk, BLOCK, 1)
        totals = lax.dynamic_update_slice_in_dim(totals, previous + row_term, row_blk, 1)
        previous = lax.dynamic_slice_in_dim(totals, col_blk, BLOCK, 1)
        totals = lax.dynamic_update_slice_in_dim(totals, previous + col_term, col_blk, 1)
        return (totals, None)
    start_totals = jnp.zeros((vec_count, TRAJ), jnp.float32)
    return lax.scan(advance, start_totals, pair_list)[0]

def reference(trajectories, kernel_scale, start_vectors, pair_list):
    ones_row = jnp.ones((1, TRAJ), jnp.bfloat16)
    degree = sweep(trajectories, kernel_scale, ones_row, pair_list)[0]
    inverse_root = lax.rsqrt(degree)
    vectors = start_vectors
    for sweep_turn in range(ITERS):
        scaled = (inverse_root[None, :] * vectors).astype(jnp.bfloat16)
        image = inverse_root[None, :] * sweep(trajectories, kernel_scale, scaled, pair_list)
        gram = jnp.dot(image.astype(jnp.float32), image.T.astype(jnp.float32), precision=lax.Precision.HIGHEST, preferred_element_type=jnp.float32)
        factor = jnp.linalg.cholesky(gram)
        vectors = lax.linalg.triangular_solve(factor, image, left_side=True, lower=True)
    return vectors
```

```python
import functools

import jax
import jax.numpy as jnp
from jax import lax
from jax.experimental import pallas as pl
from jax.experimental.pallas import tpu as pltpu
from jax.sharding import PartitionSpec as P

FEAT = 300
BLOCK = 256
REACH = 3
ROWS = 304
SCALE_ROW = 300
MASK_ROW = 301
MASKED = 1e30
LOG2E = 1.4426950408889634
VMEM_LIMIT = 48 * 1024 * 1024
TRANS_B = (((1,), (1,)), ((), ()))


def shifted(value, axis, steps):
    count = lax.axis_size(axis)
    return lax.ppermute(value, axis, [((at + steps) % count, at) for at in range(count)])


def window(value):
    group = jnp.stack([value] + [shifted(value, "sub", e) for e in range(1, 4)])
    ahead = {h: shifted(group, "space", h) for h in range(1, REACH + 1)}
    behind = {h: shifted(group, "space", -h) for h in range(1, REACH + 1)}
    return group, ahead, behind


def window_relayed(value):
    group = jnp.stack([value] + [shifted(value, "sub", e) for e in range(1, 4)])
    ahead = {h: shifted(group, "space", h) for h in (1, 2)}
    behind = {h: shifted(group, "space", -h) for h in (1, 2)}
    ahead[3] = shifted(ahead[2], "space", 1)
    behind[3] = shifted(behind[2], "space", -1)
    return group, ahead, behind


def summed(value):
    for axis, stride in (("sub", 1), ("space", 1), ("space", 4), ("space", 16)):
        parts = [shifted(value, axis, stride * k) for k in range(1, 4)]
        value = (value + parts[0]) + (parts[1] + parts[2])
    return value


def squares_of(coords):
    wide = coords.astype(jnp.float32)
    return jnp.sum(wide * wide, axis=0, keepdims=True)


def degree_of(tile):
    ones = jnp.ones((8, tile.shape[1]), jnp.bfloat16)
    return lax.dot_general(ones, tile, TRANS_B, preferred_element_type=jnp.float32)


def tile_rows(lhs, rhs, row_norm, col_norm, row_rate, col_rate):
    crossed = jnp.dot(lhs, rhs, preferred_element_type=jnp.float32)
    spread = crossed - (row_norm + col_norm)
    return jnp.exp2(spread * row_rate * col_rate).astype(jnp.bfloat16)


def bias_rows(used_ref, base, step_r, step_c):
    first = lax.broadcasted_iota(jnp.int32, (1, 2 * BLOCK), 1) < BLOCK
    rows = []
    for r in range(2):
        left, right = (
            jnp.where(used_ref[base + r * step_r + c * step_c] > 0.0, 0.0, MASKED) for c in range(2)
        )
        rows.append(jnp.where(first, left, right))
    return rows


def tile_kernel(mine_ref, theirs_ref, lhs_ref, rate_ref, norm_ref, ahead_ref, behind_ref, tile_ref, degree_ref):
    at = pl.program_id(0)

    @pl.when(at == 0)
    def _():
        degree_ref[...] = jnp.zeros_like(degree_ref)

    biases = (
        bias_rows(mine_ref, at * 4, 2, 1),
        bias_rows(theirs_ref, at * 16 + lax.rem(4 - at, 4) * 4, 1, 2),
    )
    for side, data_ref in enumerate((ahead_ref, behind_ref)):
        data = data_ref[0]
        col_norm = squares_of(data[:FEAT])
        col_rate = 1.0 / data[SCALE_ROW : SCALE_ROW + 1].astype(jnp.float32)
        for r in range(2):
            rows = pl.ds(r * BLOCK, BLOCK)
            tile = tile_rows(
                lhs_ref[rows, :], data, norm_ref[rows, :], col_norm + biases[side][r], rate_ref[rows, :], col_rate
            )
            tile_ref[0, side, rows, :] = tile
            degree_ref[:, rows] += degree_of(tile)


def self_kernel(lhs_ref, rate_ref, norm_ref, own_ref, tile_ref, degree_ref):
    data = own_ref[...]
    col_norm = squares_of(data[:FEAT])
    col_rate = 1.0 / data[SCALE_ROW : SCALE_ROW + 1].astype(jnp.float32)
    first = lax.broadcasted_iota(jnp.int32, (1, 2 * BLOCK), 1) < BLOCK
    for r in range(2):
        bias = jnp.where(first == (r == 0), 0.0, MASKED)
        rows = pl.ds(r * BLOCK, BLOCK)
        tile = tile_rows(
            lhs_ref[rows, :], data, norm_ref[rows, :], col_norm + bias, rate_ref[rows, :], col_rate
        )
        tile_ref[rows, :] = tile
        degree_ref[:, rows] = degree_of(tile)


def whole(shape):
    return pl.BlockSpec(shape, lambda *at: (0,) * len(shape))


def hop_tiles(mine, theirs, lhs, rate, norm, ahead, behind):
    length = 2 * BLOCK
    slab = pl.BlockSpec((1, ROWS, length), lambda at: (at, 0, 0))
    return pl.pallas_call(
        tile_kernel,
        grid=(4,),
        in_specs=[
            pl.BlockSpec(memory_space=pltpu.SMEM),
            pl.BlockSpec(memory_space=pltpu.SMEM),
            whole(lhs.shape),
            whole(rate.shape),
            whole(norm.shape),
            slab,
            slab,
        ],
        out_specs=[
            pl.BlockSpec((1, 2, length, length), lambda at: (at, 0, 0, 0)),
            whole((8, length)),
        ],
        out_shape=[
            jax.ShapeDtypeStruct((4, 2, length, length), jnp.bfloat16),
            jax.ShapeDtypeStruct((8, length), jnp.float32),
        ],
        compiler_params=pltpu.CompilerParams(vmem_limit_bytes=VMEM_LIMIT),
        cost_estimate=pl.CostEstimate(
            flops=8 * 2 * ROWS * length * length, bytes_accessed=7 * 2**20, transcendentals=8 * length * length
        ),
    )(mine, theirs, lhs, rate, norm, ahead, behind)


def self_tiles(lhs, rate, norm, own):
    length = 2 * BLOCK
    return pl.pallas_call(
        self_kernel,
        out_shape=[
            jax.ShapeDtypeStruct((length, length), jnp.bfloat16),
            jax.ShapeDtypeStruct((8, length), jnp.float32),
        ],
        compiler_params=pltpu.CompilerParams(vmem_limit_bytes=VMEM_LIMIT),
        cost_estimate=pl.CostEstimate(
            flops=2 * ROWS * length * length, bytes_accessed=2**20, transcendentals=length * length
        ),
    )(lhs, rate, norm, own)


def gram_of(image):
    return lax.dot_general(
        image, image, TRANS_B, precision=lax.Precision.HIGHEST, preferred_element_type=jnp.float32
    )


def solved(gram, image):
    count = gram.shape[0]
    place = lax.broadcasted_iota(jnp.int32, (count, 1), 0)
    for k in range(count):
        inverse = 1.0 / jnp.sqrt(gram[k : k + 1, k : k + 1])
        gram_row = gram[k : k + 1, :] * inverse
        image_row = image[k : k + 1, :] * inverse
        column = jnp.where(place > k, gram[:, k : k + 1] * inverse, 0.0)
        gram = gram - column * gram_row
        image = jnp.where(place == k, image_row, image - column * image_row)
    return image


def weighted(vectors, tile):
    if vectors.dtype == jnp.bfloat16:
        return lax.dot_general(vectors, tile, TRANS_B, preferred_element_type=jnp.float32)
    count = vectors.shape[0]
    high = vectors.astype(jnp.bfloat16)
    low = (vectors - high.astype(jnp.float32)).astype(jnp.bfloat16)
    both = lax.dot_general(
        jnp.concatenate([high, low], 0), tile, TRANS_B, preferred_element_type=jnp.float32
    )
    return both[:count] + both[count:]


def sweep_kernel(own_ref, root_ref, self_ref, *refs):
    ahead_refs, behind_refs, tile_refs = refs[:3], refs[3:6], refs[6:9]
    image_ref, gram_ref, next_ref, total = refs[9:]
    at = pl.program_id(0)

    @pl.when(at == 0)
    def _():
        total[...] = weighted(own_ref[...], self_ref[...])

    part = None
    for ahead_ref, behind_ref, tile_ref in zip(ahead_refs, behind_refs, tile_refs):
        for side, data_ref in enumerate((ahead_ref, behind_ref)):
            term = weighted(data_ref[0], tile_ref[0, side])
            part = term if part is None else part + term
    total[...] += part

    @pl.when(at == 3)
    def _():
        image = root_ref[...] * total[...]
        image_ref[...] = image
        gram_ref[...] = gram_of(image)
        next_ref[...] = root_ref[...] * image


def sweep(own, root, self_tile, ahead, behind, tiles):
    vecs, length = own.shape
    slab = pl.BlockSpec((1, vecs, length), lambda at: (at, 0, 0))
    return pl.pallas_call(
        sweep_kernel,
        grid=(4,),
        in_specs=[whole(own.shape), whole(root.shape), whole(self_tile.shape)]
        + [slab] * 6
        + [pl.BlockSpec((1, 2, length, length), lambda at: (at, 0, 0, 0))] * 3,
        out_specs=[whole((vecs, length)), whole((vecs, vecs)), whole((vecs, length))],
        out_shape=[
            jax.ShapeDtypeStruct((vecs, length), jnp.float32),
            jax.ShapeDtypeStruct((vecs, vecs), jnp.float32),
            jax.ShapeDtypeStruct((vecs, length), jnp.float32),
        ],
        scratch_shapes=[pltpu.VMEM((vecs, length), jnp.float32)],
        compiler_params=pltpu.CompilerParams(vmem_limit_bytes=VMEM_LIMIT),
        cost_estimate=pl.CostEstimate(
            flops=25 * 2 * vecs * length * length, bytes_accessed=14 * 2**20, transcendentals=0
        ),
    )(own, root, self_tile, *[ahead[h] for h in (1, 2, 3)], *[behind[h] for h in (1, 2, 3)], *tiles)


def solve_gram_kernel(gram_ref, image_ref, solved_ref, next_ref):
    image = solved(gram_ref[...], image_ref[...])
    solved_ref[...] = image
    next_ref[...] = gram_of(image)


def solve_kernel(gram_ref, image_ref, solved_ref):
    solved_ref[...] = solved(gram_ref[...], image_ref[...])


def on_device(trajectories, kernel_scale, start_vectors, pair_list):
    length = trajectories.shape[1]
    vecs = start_vectors.shape[0]
    n_sub = lax.axis_size("sub")
    n_space = lax.axis_size("space")
    space_at = lax.axis_index("space")
    sub_at = lax.axis_index("sub")
    device = space_at * n_sub + sub_at

    row_blk = pair_list[:, 0] - device * 2
    col_dev = pair_list[:, 1] // 2
    hop = jnp.remainder(col_dev // n_sub - space_at, n_space)
    across = jnp.remainder(col_dev % n_sub - sub_at, n_sub)
    place = (((hop - 1) * 4 + across) * 2 + row_blk) * 2 + pair_list[:, 1] % 2
    place = jnp.where(hop > 0, place, -1)
    used = jnp.any(place[:, None] == jnp.arange(length, dtype=jnp.int32)[None, :], axis=0)
    payload = jnp.concatenate(
        [
            trajectories,
            kernel_scale[None, :],
            used.astype(jnp.bfloat16)[None, :],
            jnp.zeros((2, length), jnp.bfloat16),
        ],
        0,
    )

    group, ahead, behind = window_relayed(payload)

    rate = (LOG2E / kernel_scale.astype(jnp.float32))[:, None]
    norm = squares_of(trajectories).reshape(length, 1)
    lhs = jnp.concatenate(
        [trajectories.T * 2.0, jnp.zeros((length, ROWS - FEAT), jnp.bfloat16)], 1
    ).astype(jnp.bfloat16)

    mine = used[:48].astype(jnp.float32)

    def theirs_of(h):
        return behind[h][:, MASK_ROW, 16 * (h - 1) : 16 * h].astype(jnp.float32).reshape(64)

    self_tile, degree = self_tiles(lhs, rate, norm, payload)
    tiles = []
    for h in range(1, REACH + 1):
        tile, part = hop_tiles(mine[16 * (h - 1) : 16 * h], theirs_of(h), lhs, rate, norm, ahead[h], behind[h])
        tiles.append(tile)
        degree = degree + part
    root = lax.rsqrt(degree[:1])

    scaled = (root * start_vectors).astype(jnp.bfloat16)
    _, near_ahead, near_behind = window(scaled)
    image, gram, raw = sweep(scaled, root, self_tile, near_ahead, near_behind, tiles)

    gram = summed(gram)
    _, near_ahead, near_behind = window(raw)
    image, _, _ = sweep(raw, root, self_tile, near_ahead, near_behind, tiles)
    image, gram = pl.pallas_call(
        solve_gram_kernel,
        out_shape=[
            jax.ShapeDtypeStruct((vecs, length), jnp.float32),
            jax.ShapeDtypeStruct((vecs, vecs), jnp.float32),
        ],
        cost_estimate=pl.CostEstimate(flops=2**20, bytes_accessed=2**17, transcendentals=0),
    )(gram, image)
    gram = summed(gram)
    return pl.pallas_call(
        solve_kernel,
        out_shape=jax.ShapeDtypeStruct((vecs, length), jnp.float32),
        cost_estimate=pl.CostEstimate(flops=2**20, bytes_accessed=2**17, transcendentals=0),
    )(gram, image)


def solution(mesh):
    placed = (
        P(None, ("space", "sub")),
        P(("space", "sub")),
        P(None, ("space", "sub")),
        P(("space", "sub"), None),
    )
    return jax.shard_map(
        on_device, mesh=mesh, in_specs=placed, out_specs=P(None, ("space", "sub")), check_vma=False
    )
```

```python
import functools

import jax
import jax.numpy as jnp
from jax import lax
from jax.experimental import pallas as pl
from jax.experimental.pallas import tpu as pltpu
from jax.sharding import PartitionSpec as P

FEAT = 300
BLOCK = 256
LENGTH = 2 * BLOCK
REACH = 3
N_SUB = 4
ROWS = 304
SCALE_COL = 300
MASK_COL = 301
PAIRS = 4 * N_SUB
MASKED = 1e30
LOG2E = 1.4426950408889634
VMEM_LIMIT = 12 * 1024 * 1024
TRANS_B = (((1,), (1,)), ((), ()))


def shifted(value, axis, steps):
    count = lax.axis_size(axis)
    return lax.ppermute(value, axis, [((at + steps) % count, at) for at in range(count)])


def space_window(value):
    return {h: shifted(value, "space", h) for h in (1, -1, 2, -2, 3, -3)}


def groups_by(key, n_space, n_sub):
    found = {}
    for place in range(n_space * n_sub):
        found.setdefault(key(place // n_sub, place % n_sub), []).append(place)
    return list(found.values())


def summed(value):
    n_space, n_sub = lax.axis_size("space"), lax.axis_size("sub")
    shape = value.shape
    value = value.reshape(-1, 128)
    for key in (lambda s, y: (s // 4, 0), lambda s, y: (s % 4, y)):
        groups = groups_by(key, n_space, n_sub)
        sent = jnp.broadcast_to(value[None], (len(groups[0]),) + value.shape)
        value = jnp.sum(
            lax.all_to_all(sent, ("space", "sub"), 0, 0, axis_index_groups=groups), 0
        )
    return value.reshape(shape)


def whole(shape):
    return pl.BlockSpec(shape, lambda *at: (0,) * len(shape))


def column_terms(data_ref):
    wide = data_ref[:FEAT, :].astype(jnp.float32)
    norm = jnp.sum(wide * wide, axis=0, keepdims=True)
    return norm, 1.0 / data_ref[SCALE_COL : SCALE_COL + 1, :].astype(jnp.float32)


def prepare_rows(rows, lhs_ref, norm_ref, rate_ref):
    keep = lax.broadcasted_iota(jnp.int32, rows.shape, 1) < FEAT
    wide = jnp.where(keep, rows.astype(jnp.float32), 0.0)
    lhs_ref[...] = (wide + wide).astype(jnp.bfloat16)
    norm_ref[...] = jnp.sum(wide * wide, axis=1, keepdims=True)
    rate_ref[...] = LOG2E / rows[:, SCALE_COL : SCALE_COL + 1].astype(jnp.float32)


def one_tile(r, c, data_ref, lhs_ref, norm_ref, rate_ref, col_norm, col_rate):
    at_r, at_c = pl.ds(r * BLOCK, BLOCK), pl.ds(c * BLOCK, BLOCK)
    crossed = jnp.dot(lhs_ref[at_r, :], data_ref[:, at_c], preferred_element_type=jnp.float32)
    spread = crossed - (norm_ref[at_r, :] + col_norm[:, c * BLOCK : (c + 1) * BLOCK])
    power = (spread * rate_ref[at_r, :]) * col_rate[:, c * BLOCK : (c + 1) * BLOCK]
    return jnp.exp2(power).astype(jnp.bfloat16)


def row_sums(tile):
    return jnp.dot(
        tile, jnp.ones((tile.shape[1], 128), jnp.bfloat16), preferred_element_type=jnp.float32
    )


def tile_kernel(
    mine_ref, theirs_ref, rows_ref, ahead_ref, behind_ref, before_ref, tile_ref, degree_ref, lhs, norm, rate, total
):
    at = pl.program_id(0)
    prepare_rows(rows_ref[0], lhs, norm, rate)
    total[...] = jnp.zeros_like(total)
    for side, data_ref in enumerate((ahead_ref, behind_ref)):
        col_norm, col_rate = column_terms(data_ref)
        for r in range(2):
            for c in range(2):
                if side == 0:
                    listed = mine_ref[at * PAIRS + lax.rem(N_SUB - at, N_SUB) * 4 + r * 2 + c] > 0.0
                else:
                    listed = theirs_ref[at * 4 + c * 2 + r] > 0.0
                at_r, at_c = pl.ds(r * BLOCK, BLOCK), pl.ds(c * BLOCK, BLOCK)

                @pl.when(listed)
                def _():
                    tile = one_tile(r, c, data_ref, lhs, norm, rate, col_norm, col_rate)
                    tile_ref[0, side, at_r, at_c] = tile
                    total[at_r, :] += row_sums(tile)

                @pl.when(jnp.logical_not(listed))
                def _():
                    tile_ref[0, side, at_r, at_c] = jnp.zeros((BLOCK, BLOCK), jnp.bfloat16)

    degree_ref[0] = before_ref[0] + total[...].T[:8]


def hop_tiles(mine, theirs, rows, ahead, behind, before):
    return pl.pallas_call(
        tile_kernel,
        grid=(N_SUB,),
        in_specs=[
            pl.BlockSpec(memory_space=pltpu.SMEM),
            pl.BlockSpec(memory_space=pltpu.SMEM),
            pl.BlockSpec((1, LENGTH, ROWS), lambda at: (at, 0, 0)),
            whole(ahead.shape),
            whole(behind.shape),
            pl.BlockSpec((1, 8, LENGTH), lambda at: (at, 0, 0)),
        ],
        out_specs=[
            pl.BlockSpec((1, 2, LENGTH, LENGTH), lambda at: (at, 0, 0, 0)),
            pl.BlockSpec((1, 8, LENGTH), lambda at: (at, 0, 0)),
        ],
        out_shape=[
            jax.ShapeDtypeStruct((N_SUB, 2, LENGTH, LENGTH), jnp.bfloat16),
            jax.ShapeDtypeStruct((N_SUB, 8, LENGTH), jnp.float32),
        ],
        scratch_shapes=[
            pltpu.VMEM((LENGTH, ROWS), jnp.bfloat16),
            pltpu.VMEM((LENGTH, 1), jnp.float32),
            pltpu.VMEM((LENGTH, 1), jnp.float32),
            pltpu.VMEM((LENGTH, 128), jnp.float32),
        ],
        compiler_params=pltpu.CompilerParams(vmem_limit_bytes=VMEM_LIMIT),
        cost_estimate=pl.CostEstimate(
            flops=8 * 2 * ROWS * LENGTH * LENGTH,
            bytes_accessed=7 * 2**20,
            transcendentals=8 * LENGTH * LENGTH,
        ),
    )(mine, theirs, rows, ahead, behind, before)


def self_kernel(rows_ref, own_ref, tile_ref, degree_ref, lhs, norm, rate, total):
    prepare_rows(rows_ref[...], lhs, norm, rate)
    col_norm, col_rate = column_terms(own_ref)
    for r in range(2):
        at_r = pl.ds(r * BLOCK, BLOCK)
        tile = one_tile(r, r, own_ref, lhs, norm, rate, col_norm, col_rate)
        tile_ref[at_r, at_r] = tile
        tile_ref[at_r, pl.ds((1 - r) * BLOCK, BLOCK)] = jnp.zeros((BLOCK, BLOCK), jnp.bfloat16)
        total[at_r, :] = row_sums(tile)
    degree_ref[0] = total[...].T[:8]
    degree_ref[1:] = jnp.zeros((N_SUB - 1, 8, LENGTH), jnp.float32)


def self_tiles(rows, own):
    return pl.pallas_call(
        self_kernel,
        out_shape=[
            jax.ShapeDtypeStruct((LENGTH, LENGTH), jnp.bfloat16),
            jax.ShapeDtypeStruct((N_SUB, 8, LENGTH), jnp.float32),
        ],
        scratch_shapes=[
            pltpu.VMEM((LENGTH, ROWS), jnp.bfloat16),
            pltpu.VMEM((LENGTH, 1), jnp.float32),
            pltpu.VMEM((LENGTH, 1), jnp.float32),
            pltpu.VMEM((LENGTH, 128), jnp.float32),
        ],
        compiler_params=pltpu.CompilerParams(vmem_limit_bytes=VMEM_LIMIT),
        cost_estimate=pl.CostEstimate(
            flops=2 * ROWS * LENGTH * LENGTH, bytes_accessed=2**20, transcendentals=LENGTH * LENGTH
        ),
    )(rows, own)


def padded(vectors):
    vecs = vectors.shape[0]
    if vectors.dtype == jnp.bfloat16:
        parts = [vectors]
    else:
        high = vectors.astype(jnp.bfloat16)
        parts = [high, (vectors - high.astype(jnp.float32)).astype(jnp.bfloat16)]
    return jnp.concatenate(parts + [jnp.zeros((128 - len(parts) * vecs, LENGTH), jnp.bfloat16)], 0)


def sweep_kernel(parts, self_ref, *refs):
    vector_refs, tile_refs, out_refs, held = refs[:7], refs[7:10], refs[10:14], refs[14]
    vecs = vector_refs[0].shape[0]
    at = pl.program_id(0)

    @pl.when(at == 0)
    def _():
        for k in range(7):
            held[k] = padded(vector_refs[k][...])

    def product(tile, k):
        return lax.dot_general(tile, held[k], TRANS_B, preferred_element_type=jnp.float32)

    total = None
    for h, tile_ref in enumerate(tile_refs):
        for side in range(2):
            term = product(tile_ref[0, side], 1 + 2 * h + side)
            total = term if total is None else total + term

    def shaped(sums):
        turned = sums.T
        result = turned[:vecs]
        for part in range(1, parts):
            result = result + turned[part * vecs : (part + 1) * vecs]
        return result

    @pl.when(at == 0)
    def _():
        out_refs[0][...] = shaped(total + product(self_ref[...], 0))

    for k in range(1, N_SUB):

        @pl.when(at == k)
        def _(k=k):
            out_refs[k][...] = shaped(total)


def sweep(own, near, self_tile, tiles):
    vecs = own.shape[0]
    return pl.pallas_call(
        functools.partial(sweep_kernel, 1 if own.dtype == jnp.bfloat16 else 2),
        grid=(N_SUB,),
        in_specs=[whole(self_tile.shape)]
        + [whole(own.shape)] * 7
        + [pl.BlockSpec((1, 2, LENGTH, LENGTH), lambda at: (at, 0, 0, 0))] * 3,
        out_specs=[whole((vecs, LENGTH))] * 4,
        out_shape=[jax.ShapeDtypeStruct((vecs, LENGTH), jnp.float32)] * 4,
        scratch_shapes=[pltpu.VMEM((7, 128, LENGTH), jnp.bfloat16)],
        compiler_params=pltpu.CompilerParams(vmem_limit_bytes=VMEM_LIMIT),
        cost_estimate=pl.CostEstimate(
            flops=25 * 2 * 128 * LENGTH * LENGTH, bytes_accessed=14 * 2**20, transcendentals=0
        ),
    )(self_tile, own, *[near[h] for h in (1, -1, 2, -2, 3, -3)], *tiles)


def exchanged(parts):
    return [parts[0]] + [shifted(parts[e], "sub", -e) for e in range(1, N_SUB)]


def gram_of(image):
    return lax.dot_general(
        image, image, TRANS_B, precision=lax.Precision.HIGHEST, preferred_element_type=jnp.float32
    )


def solved(gram, image):
    count = gram.shape[0]
    place = lax.broadcasted_iota(jnp.int32, (count, 1), 0)
    for k in range(count):
        inverse = 1.0 / jnp.sqrt(gram[k : k + 1, k : k + 1])
        gram_row = gram[k : k + 1, :] * inverse
        image_row = image[k : k + 1, :] * inverse
        column = jnp.where(place > k, gram[:, k : k + 1] * inverse, 0.0)
        gram = gram - column * gram_row
        image = jnp.where(place == k, image_row, image - column * image_row)
    return image


def image_of(root_ref, part_refs):
    first, second, third, fourth = (part_ref[...] for part_ref in part_refs)
    return root_ref[...] * ((first + second) + (third + fourth))


def image_kernel(root_ref, *refs):
    image = image_of(root_ref, refs[:4])
    refs[4][...] = root_ref[...] * image
    refs[5][...] = gram_of(image)


def solve_gram_kernel(gram_ref, root_ref, *refs):
    image = solved(gram_ref[...], image_of(root_ref, refs[:4]))
    refs[4][...] = image
    refs[5][...] = gram_of(image)


def solve_kernel(gram_ref, image_ref, solved_ref):
    solved_ref[...] = solved(gram_ref[...], image_ref[...])


def on_device(trajectories, kernel_scale, start_vectors, pair_list):
    vecs, length = start_vectors.shape
    n_sub = lax.axis_size("sub")
    n_space = lax.axis_size("space")
    space_at = lax.axis_index("space")
    sub_at = lax.axis_index("sub")
    device = space_at * n_sub + sub_at

    row_blk = pair_list[:, 0] - device * 2
    col_dev = pair_list[:, 1] // 2
    hop = jnp.remainder(col_dev // n_sub - space_at, n_space)
    across = jnp.remainder(col_dev % n_sub - sub_at, n_sub)
    place = (((hop - 1) * n_sub + across) * 2 + row_blk) * 2 + pair_list[:, 1] % 2
    place = jnp.where(hop > 0, place, -1)
    used = jnp.any(place[:, None] == jnp.arange(length, dtype=jnp.int32)[None, :], axis=0)
    payload = jnp.concatenate(
        [
            trajectories,
            kernel_scale[None, :],
            used.astype(jnp.bfloat16)[None, :],
            jnp.zeros((ROWS - MASK_COL - 1, length), jnp.bfloat16),
        ],
        0,
    )

    members = [payload] + [shifted(payload, "sub", e) for e in range(1, N_SUB)]
    near = {h: shifted(payload, "space", h) for h in (1, -1, 2, -2)}
    near[3] = shifted(near[2], "space", 1)
    near[-3] = shifted(near[-2], "space", -1)
    rows = jnp.stack(members).transpose(0, 2, 1)
    listed = jnp.stack([member[MASK_COL, : REACH * PAIRS] for member in members]).astype(jnp.float32)

    self_tile, degree = self_tiles(payload.T, payload)
    tiles = []
    for h in range(1, REACH + 1):
        span = slice((h - 1) * PAIRS, h * PAIRS)
        mine = listed[:, span].reshape(N_SUB * PAIRS)
        theirs = near[-h][MASK_COL, span].astype(jnp.float32)
        tile, degree = hop_tiles(mine, theirs, rows, near[h], near[-h], degree)
        tiles.append(tile)
    shares = exchanged([degree[e, :1] for e in range(N_SUB)])
    root = lax.rsqrt((shares[0] + shares[1]) + (shares[2] + shares[3]))

    vector_shape = jax.ShapeDtypeStruct((vecs, length), jnp.float32)
    gram_shape = jax.ShapeDtypeStruct((vecs, vecs), jnp.float32)
    cheap = pl.CostEstimate(flops=2**20, bytes_accessed=2**17, transcendentals=0)

    scaled = (root * start_vectors).astype(jnp.bfloat16)
    shares = exchanged(sweep(scaled, space_window(scaled), self_tile, tiles))
    raw, gram = pl.pallas_call(
        image_kernel, out_shape=[vector_shape, gram_shape], cost_estimate=cheap
    )(root, *shares)

    near_raw = space_window(raw)
    gram = summed(gram)
    shares = exchanged(sweep(raw, near_raw, self_tile, tiles))
    image, gram = pl.pallas_call(
        solve_gram_kernel, out_shape=[vector_shape, gram_shape], cost_estimate=cheap
    )(gram, root, *shares)
    return pl.pallas_call(solve_kernel, out_shape=vector_shape, cost_estimate=cheap)(
        summed(gram), image
    )


def solution(mesh):
    placed = (
        P(None, ("space", "sub")),
        P(("space", "sub")),
        P(None, ("space", "sub")),
        P(("space", "sub"), None),
    )
    return jax.shard_map(
        on_device, mesh=mesh, in_specs=placed, out_specs=P(None, ("space", "sub")), check_vma=False
    )
```

```python
import functools

import jax
import jax.numpy as jnp
from jax import lax
from jax.experimental import pallas as pl
from jax.experimental.pallas import tpu as pltpu
from jax.sharding import PartitionSpec as P

FEAT = 300
BLOCK = 256
LENGTH = 2 * BLOCK
REACH = 3
N_SUB = 4
ROWS = 304
DEPTH = 320
SCALE_ROW = 300
MASK_ROW = 301
PAIRS = 4 * N_SUB
SLOTS = 48
COUNT = SLOTS - 1
NOBODY = 2 * N_SUB
UNROLL = 8
LOG2E = 1.4426950408889634
VMEM_LIMIT = 12 * 1024 * 1024
SMALL_LIMIT = 4 * 1024 * 1024
TRANS_B = (((1,), (1,)), ((), ()))


def shifted(value, axis, steps):
    count = lax.axis_size(axis)
    return lax.ppermute(value, axis, [((at + steps) % count, at) for at in range(count)])


def space_window(value):
    return {h: shifted(value, "space", h) for h in (1, 2, 3, -1, -2, -3)}


def groups_by(key, n_space, n_sub):
    found = {}
    for place in range(n_space * n_sub):
        found.setdefault(key(place // n_sub, place % n_sub), []).append(place)
    return list(found.values())


def summed(value):
    n_space, n_sub = lax.axis_size("space"), lax.axis_size("sub")
    shape = value.shape
    value = value.reshape(-1, 128)
    for key in (lambda s, y: (s // 4, 0), lambda s, y: (s % 4, y)):
        groups = groups_by(key, n_space, n_sub)
        sent = jnp.broadcast_to(value[None], (len(groups[0]),) + value.shape)
        value = jnp.sum(
            lax.all_to_all(sent, ("space", "sub"), 0, 0, axis_index_groups=groups), 0
        )
    return value.reshape(shape)


def pieces(norm):
    high = norm.astype(jnp.bfloat16).astype(jnp.float32)
    rest = norm - high
    middle = rest.astype(jnp.bfloat16).astype(jnp.float32)
    return high, middle, rest - middle


def ones_and_norms(norm, ones_at, norms_at):
    place = lax.broadcasted_iota(jnp.int32, (DEPTH - ROWS, 1), 0)
    tail = jnp.where((place >= ones_at) & (place < ones_at + 3), 1.0, 0.0)
    for k, piece in enumerate(pieces(norm)):
        tail = jnp.where(place == norms_at + k, -piece, tail)
    return tail


def rows_kernel(*refs):
    rows_ref, rate_ref = refs[N_SUB:]
    for e in range(N_SUB):
        wide = refs[e][:FEAT, :].astype(jnp.float32)
        tail = ones_and_norms(jnp.sum(wide * wide, axis=0, keepdims=True), 0, 3)
        tail = tail.astype(jnp.bfloat16)
        rate = LOG2E / refs[e][SCALE_ROW : SCALE_ROW + 1, :].astype(jnp.float32)
        below = lax.broadcasted_iota(jnp.int32, (ROWS, 1), 0) < FEAT
        twice = jnp.where(below, 2.0 * refs[e][...].astype(jnp.float32), 0.0).astype(jnp.bfloat16)
        for r in range(2):
            span = slice(r * BLOCK, (r + 1) * BLOCK)
            rows_ref[2 * e + r, :ROWS] = twice[:, span]
            rows_ref[2 * e + r, ROWS:] = tail[:, span]
            rate_ref[2 * e + r] = jnp.broadcast_to(rate[:, span], (8, BLOCK))


def row_operands(members):
    return pl.pallas_call(
        rows_kernel,
        out_shape=[
            jax.ShapeDtypeStruct((2 * N_SUB, DEPTH, BLOCK), jnp.bfloat16),
            jax.ShapeDtypeStruct((2 * N_SUB, 8, BLOCK), jnp.float32),
        ],
        compiler_params=pltpu.CompilerParams(vmem_limit_bytes=VMEM_LIMIT),
        cost_estimate=pl.CostEstimate(flops=2**22, bytes_accessed=4 * 2**20, transcendentals=0),
    )(*members)


def prepare_columns(data_ref, first, lhs, rate_ref):
    wide = data_ref[...].astype(jnp.float32)
    rate = 1.0 / wide[SCALE_ROW : SCALE_ROW + 1]
    squares = wide[:FEAT] * wide[:FEAT]
    tail = ones_and_norms(jnp.sum(squares, axis=0, keepdims=True), 3, 0)
    full = jnp.concatenate([wide, tail, jnp.zeros((384 - DEPTH, LENGTH), jnp.float32)], 0)
    turned = full.T[:, :DEPTH].astype(jnp.bfloat16)
    rate = jnp.broadcast_to(rate, (128, LENGTH)).T
    for c in range(2):
        lhs[first + c] = turned[c * BLOCK : (c + 1) * BLOCK]
        rate_ref[first + c] = rate[c * BLOCK : (c + 1) * BLOCK]


def list_pairs(mine_ref, theirs_ref, rows_ref, cols_ref, count):
    def member(e, count):
        for side in range(2):
            for r in range(2):
                for c in range(2):
                    if side == 0:
                        used = mine_ref[e * PAIRS + lax.rem(N_SUB - e, N_SUB) * 4 + r * 2 + c]
                    else:
                        used = theirs_ref[e * 4 + c * 2 + r]
                    rows_ref[count] = e * 2 + r
                    cols_ref[count] = side * 2 + c
                    count = count + jnp.where(used > 0.0, 1, 0)
        return count

    count = lax.fori_loop(0, N_SUB, member, count)
    for k in range(8):
        rows_ref[count + k] = NOBODY
        cols_ref[count + k] = 0
    rows_ref[COUNT] = count
    cols_ref[COUNT] = count
    return count


def tile_kernel(
    first, last, mine_ref, theirs_ref, blocks_ref, rate_ref, ahead_ref, behind_ref, extra_ref,
    tile_ref, rows_ref, cols_ref, sums_ref, lhs, col, even, odd, *held
):
    total = held[0] if last else sums_ref
    prepare_columns(ahead_ref, 0, lhs, col)
    prepare_columns(behind_ref, 2, lhs, col)
    count = 0
    if first:
        prepare_columns(extra_ref, 4, lhs, col)
        for r in range(2):
            rows_ref[r] = r
            cols_ref[r] = 4 + r
        count = 2
        total[...] = jnp.zeros_like(total)
    else:
        total[...] = extra_ref[...]
    count = list_pairs(mine_ref, theirs_ref, rows_ref, cols_ref, jnp.int32(count))

    def product(at):
        row = lax.min(rows_ref[at], NOBODY - 1)
        return jnp.dot(lhs[cols_ref[at]], blocks_ref[row], preferred_element_type=jnp.float32)

    def finish(crossed, at):
        row = rows_ref[at]
        rate = col[cols_ref[at]]
        rates = jnp.concatenate([rate, rate], 1) * rate_ref[lax.min(row, NOBODY - 1), :1, :]
        tile = jnp.exp2(crossed * rates).astype(jnp.bfloat16)
        tile_ref[at] = tile
        total[row] += jnp.sum(tile.astype(jnp.float32).reshape(BLOCK // 8, 8, BLOCK), axis=0)

    even[...] = product(0)

    def step(k, _):
        odd[...] = product(2 * k + 1)
        finish(even[...], 2 * k)
        even[...] = product(2 * k + 2)
        finish(odd[...], 2 * k + 1)
        return 0

    lax.fori_loop(0, lax.shift_right_logical(count + 1, 1), step, 0)
    if last:
        for e in range(N_SUB):
            for r in range(2):
                sums = jnp.sum(total[2 * e + r], axis=0, keepdims=True)
                sums_ref[e, :, pl.ds(r * BLOCK, BLOCK)] = jnp.broadcast_to(sums, (8, BLOCK))


def hop_tiles(first, last, mine, theirs, blocks, rate, ahead, behind, extra):
    smem = pl.BlockSpec(memory_space=pltpu.SMEM)
    vmem = pl.BlockSpec(memory_space=pltpu.VMEM)
    columns = 6 if first else 4
    sums = (NOBODY + 1, 8, BLOCK)
    return pl.pallas_call(
        functools.partial(tile_kernel, first, last),
        in_specs=[smem, smem] + [vmem] * 5,
        out_specs=[vmem, smem, smem, vmem],
        out_shape=[
            jax.ShapeDtypeStruct((SLOTS - 4, BLOCK, BLOCK), jnp.bfloat16),
            jax.ShapeDtypeStruct((SLOTS,), jnp.int32),
            jax.ShapeDtypeStruct((SLOTS,), jnp.int32),
            jax.ShapeDtypeStruct((N_SUB, 8, LENGTH) if last else sums, jnp.float32),
        ],
        scratch_shapes=[
            pltpu.VMEM((columns, BLOCK, DEPTH), jnp.bfloat16),
            pltpu.VMEM((columns, BLOCK, 128), jnp.float32),
            pltpu.VMEM((BLOCK, BLOCK), jnp.float32),
            pltpu.VMEM((BLOCK, BLOCK), jnp.float32),
        ]
        + ([pltpu.VMEM(sums, jnp.float32)] if last else []),
        compiler_params=pltpu.CompilerParams(vmem_limit_bytes=VMEM_LIMIT),
        cost_estimate=pl.CostEstimate(
            flops=16 * 2 * DEPTH * BLOCK * BLOCK,
            bytes_accessed=7 * 2**20,
            transcendentals=16 * BLOCK * BLOCK,
        ),
    )(mine, theirs, blocks, rate, ahead, behind, extra)


def stacked(vectors):
    if vectors.dtype == jnp.bfloat16:
        return vectors
    high = vectors.astype(jnp.bfloat16)
    return jnp.concatenate([high, (vectors - high.astype(jnp.float32)).astype(jnp.bfloat16)], 0)


def sweep_kernel(parts, order, *refs):
    list_refs, tile_refs, vector_refs = refs[:6], refs[6:9], refs[9:16]
    out_refs, held, total = refs[16:20], refs[20], refs[21]
    vecs = vector_refs[0].shape[0]
    for k in range(7):
        both = stacked(vector_refs[k][...])
        for c in range(2):
            held[2 * k + c] = both[:, c * BLOCK : (c + 1) * BLOCK]
    total[...] = jnp.zeros_like(total)

    for k, (hop, tile_ref) in enumerate(zip(order, tile_refs)):
        rows_ref, cols_ref = list_refs[2 * k], list_refs[2 * k + 1]

        def product(at, tile_ref=tile_ref, cols_ref=cols_ref, hop=hop):
            block = cols_ref[at]
            block = jnp.where(block >= 4, block - 4, block + 4 * hop - 2)
            return jnp.dot(held[block], tile_ref[at], preferred_element_type=jnp.float32)

        def step(at, _, rows_ref=rows_ref, product=product):
            terms = [product(UNROLL * at + k) for k in range(UNROLL)]
            for k in range(UNROLL):
                total[rows_ref[UNROLL * at + k]] += terms[k]
            return 0

        lax.fori_loop(0, lax.div(rows_ref[COUNT] + (UNROLL - 1), UNROLL), step, 0)

    for e in range(N_SUB):
        for r in range(2):
            result = total[2 * e + r, :vecs]
            for part in range(1, parts):
                result = result + total[2 * e + r, part * vecs : (part + 1) * vecs]
            out_refs[e][:, pl.ds(r * BLOCK, BLOCK)] = result


def sweep(own, near, order, tiles):
    vecs = own.shape[0]
    smem = pl.BlockSpec(memory_space=pltpu.SMEM)
    vmem = pl.BlockSpec(memory_space=pltpu.VMEM)
    parts = 1 if own.dtype == jnp.bfloat16 else 2
    lists = [part for tile in tiles for part in tile[1:]]
    return pl.pallas_call(
        functools.partial(sweep_kernel, parts, order),
        in_specs=[smem] * 6 + [vmem] * 10,
        out_specs=[vmem] * 4,
        out_shape=[jax.ShapeDtypeStruct((vecs, LENGTH), jnp.float32)] * 4,
        scratch_shapes=[
            pltpu.VMEM((14, parts * vecs, BLOCK), jnp.bfloat16),
            pltpu.VMEM((NOBODY + 1, parts * vecs, BLOCK), jnp.float32),
        ],
        compiler_params=pltpu.CompilerParams(vmem_limit_bytes=VMEM_LIMIT),
        cost_estimate=pl.CostEstimate(
            flops=50 * 2 * 128 * BLOCK * BLOCK, bytes_accessed=7 * 2**20, transcendentals=0
        ),
    )(*lists, *[tile[0] for tile in tiles], own, *[near[h] for h in (1, -1, 2, -2, 3, -3)])


def exchanged(parts):
    return [parts[0]] + [shifted(parts[e], "sub", -e) for e in range(1, N_SUB)]


def gram_of(image):
    return lax.dot_general(
        image, image, TRANS_B, precision=lax.Precision.HIGHEST, preferred_element_type=jnp.float32
    )


def solved(gram, image):
    count = gram.shape[0]
    place = lax.broadcasted_iota(jnp.int32, (count, 1), 0)
    across = lax.broadcasted_iota(jnp.int32, (count, count), 1)
    identity = jnp.where(across == place, 1.0, 0.0)
    joined = jnp.concatenate([gram, identity], 1)
    for k in range(count):
        column = jnp.where(place > k, joined[:, k : k + 1], 0.0)
        joined = joined - column * (joined[k : k + 1, :] * (1.0 / joined[k : k + 1, k : k + 1]))
    pivots = jnp.sum(joined[:, :count] * identity, axis=1, keepdims=True)
    inverse = joined[:, count:] / jnp.sqrt(pivots)
    return jnp.dot(
        inverse, image, precision=lax.Precision.HIGHEST, preferred_element_type=jnp.float32
    )


def image_of(root_ref, part_refs):
    first, second, third, fourth = (part_ref[...] for part_ref in part_refs)
    return root_ref[...] * ((first + second) + (third + fourth))


def image_kernel(root_ref, *refs):
    image = image_of(root_ref, refs[:4])
    refs[4][...] = root_ref[...] * image
    refs[5][...] = gram_of(image)


def solve_gram_kernel(gram_ref, root_ref, *refs):
    image = solved(gram_ref[...], image_of(root_ref, refs[:4]))
    refs[4][...] = image
    refs[5][...] = gram_of(image)


def solve_kernel(gram_ref, image_ref, solved_ref):
    solved_ref[...] = solved(gram_ref[...], image_ref[...])


def on_device(trajectories, kernel_scale, start_vectors, pair_list):
    vecs, length = start_vectors.shape
    n_sub = lax.axis_size("sub")
    n_space = lax.axis_size("space")
    space_at = lax.axis_index("space")
    sub_at = lax.axis_index("sub")
    device = space_at * n_sub + sub_at

    row_blk = pair_list[:, 0] - device * 2
    col_dev = pair_list[:, 1] // 2
    hop = jnp.remainder(col_dev // n_sub - space_at, n_space)
    across = jnp.remainder(col_dev % n_sub - sub_at, n_sub)
    place = (((hop - 1) * n_sub + across) * 2 + row_blk) * 2 + pair_list[:, 1] % 2
    place = jnp.where(hop > 0, place, -1)
    used = jnp.any(place[:, None] == jnp.arange(length, dtype=jnp.int32)[None, :], axis=0)
    payload = jnp.concatenate(
        [
            trajectories,
            kernel_scale[None, :],
            used.astype(jnp.bfloat16)[None, :],
            jnp.zeros((ROWS - MASK_ROW - 1, length), jnp.bfloat16),
        ],
        0,
    )

    members = [payload] + [shifted(payload, "sub", e) for e in range(1, N_SUB)]
    near = {h: shifted(payload, "space", h) for h in (2, -2)}
    later, near[2], near[-2] = lax.optimization_barrier((payload, near[2], near[-2]))
    for h, source in ((1, later), (-1, later), (3, near[2]), (-3, near[-2])):
        near[h] = shifted(source, "space", 1 if h > 0 else -1)
    blocks, rate = row_operands(members)
    listed = jnp.stack([member[MASK_ROW, : REACH * PAIRS] for member in members]).astype(jnp.float32)

    order = (2, 1, 3)
    tiles = []
    carried = payload
    for at, h in enumerate(order):
        span = slice((h - 1) * PAIRS, h * PAIRS)
        mine = listed[:, span].reshape(N_SUB * PAIRS)
        theirs = near[-h][MASK_ROW, span].astype(jnp.float32)
        *tile, carried = hop_tiles(
            at == 0, at == REACH - 1, mine, theirs, blocks, rate, near[h], near[-h], carried
        )
        tiles.append(tile)
    degree = carried
    shares = exchanged([degree[e, :1] for e in range(N_SUB)])
    root = lax.rsqrt((shares[0] + shares[1]) + (shares[2] + shares[3]))

    vector_shape = jax.ShapeDtypeStruct((vecs, length), jnp.float32)
    gram_shape = jax.ShapeDtypeStruct((vecs, vecs), jnp.float32)
    light = dict(
        cost_estimate=pl.CostEstimate(flops=2**20, bytes_accessed=2**17, transcendentals=0),
        compiler_params=pltpu.CompilerParams(vmem_limit_bytes=SMALL_LIMIT),
    )

    scaled = (root * start_vectors).astype(jnp.bfloat16)
    shares = exchanged(sweep(scaled, space_window(scaled), order, tiles))
    raw, gram = pl.pallas_call(
        image_kernel, out_shape=[vector_shape, gram_shape], **light
    )(root, *shares)

    near_raw = space_window(raw)
    gram = summed(gram)
    shares = exchanged(sweep(raw, near_raw, order, tiles))
    image, gram = pl.pallas_call(
        solve_gram_kernel, out_shape=[vector_shape, gram_shape], **light
    )(gram, root, *shares)
    return pl.pallas_call(solve_kernel, out_shape=vector_shape, **light)(
        summed(gram), image
    )


def solution(mesh):
    placed = (
        P(None, ("space", "sub")),
        P(("space", "sub")),
        P(None, ("space", "sub")),
        P(("space", "sub"), None),
    )
    return jax.shard_map(
        on_device, mesh=mesh, in_specs=placed, out_specs=P(None, ("space", "sub")), check_vma=False
    )
```

```python
import functools

import jax
import jax.numpy as jnp
from jax import lax
from jax.experimental import pallas as pl
from jax.experimental.pallas import tpu as pltpu
from jax.sharding import PartitionSpec as P

FEAT = 300
BLOCK = 256
LENGTH = 2 * BLOCK
REACH = 3
N_SUB = 4
ROWS = 304
DEPTH = 320
SCALE_ROW = 300
MASK_ROW = 301
PAIRS = 4 * N_SUB
SLOTS = 48
COUNT = SLOTS - 1
NOBODY = 2 * N_SUB
UNROLL = 8
STARTS = (0, 5, 9)
GROUPS = 13
LOG2E = 1.4426950408889634
VMEM_LIMIT = 12 * 1024 * 1024
SWEEP_LIMIT = 24 * 1024 * 1024
SMALL_LIMIT = 4 * 1024 * 1024
TRANS_B = (((1,), (1,)), ((), ()))


def shifted(value, axis, steps):
    count = lax.axis_size(axis)
    return lax.ppermute(value, axis, [((at + steps) % count, at) for at in range(count)])


def space_window(value):
    return {h: shifted(value, "space", h) for h in (1, 2, 3, -1, -2, -3)}


def groups_by(key, n_space, n_sub):
    found = {}
    for place in range(n_space * n_sub):
        found.setdefault(key(place // n_sub, place % n_sub), []).append(place)
    return list(found.values())


def summed(value):
    n_space, n_sub = lax.axis_size("space"), lax.axis_size("sub")
    shape = value.shape
    value = value.reshape(-1, 128)
    for key in (lambda s, y: (s // 4, 0), lambda s, y: (s % 4, y)):
        groups = groups_by(key, n_space, n_sub)
        sent = jnp.broadcast_to(value[None], (len(groups[0]),) + value.shape)
        value = jnp.sum(
            lax.all_to_all(sent, ("space", "sub"), 0, 0, axis_index_groups=groups), 0
        )
    return value.reshape(shape)


def pieces(norm):
    high = norm.astype(jnp.bfloat16).astype(jnp.float32)
    rest = norm - high
    middle = rest.astype(jnp.bfloat16).astype(jnp.float32)
    return high, middle, rest - middle


def ones_and_norms(norm, ones_at, norms_at):
    place = lax.broadcasted_iota(jnp.int32, (DEPTH - ROWS, 1), 0)
    tail = jnp.where((place >= ones_at) & (place < ones_at + 3), 1.0, 0.0)
    for k, piece in enumerate(pieces(norm)):
        tail = jnp.where(place == norms_at + k, -piece, tail)
    return tail


def rows_kernel(*refs):
    rows_ref, rate_ref = refs[N_SUB:]
    for e in range(N_SUB):
        wide = refs[e][:FEAT, :].astype(jnp.float32)
        tail = ones_and_norms(jnp.sum(wide * wide, axis=0, keepdims=True), 0, 3)
        tail = tail.astype(jnp.bfloat16)
        rate = LOG2E / refs[e][SCALE_ROW : SCALE_ROW + 1, :].astype(jnp.float32)
        below = lax.broadcasted_iota(jnp.int32, (ROWS, 1), 0) < FEAT
        twice = jnp.where(below, 2.0 * refs[e][...].astype(jnp.float32), 0.0).astype(jnp.bfloat16)
        for r in range(2):
            span = slice(r * BLOCK, (r + 1) * BLOCK)
            rows_ref[2 * e + r, :ROWS] = twice[:, span]
            rows_ref[2 * e + r, ROWS:] = tail[:, span]
            rate_ref[2 * e + r] = jnp.broadcast_to(rate[:, span], (8, BLOCK))


def row_operands(members):
    return pl.pallas_call(
        rows_kernel,
        out_shape=[
            jax.ShapeDtypeStruct((2 * N_SUB, DEPTH, BLOCK), jnp.bfloat16),
            jax.ShapeDtypeStruct((2 * N_SUB, 8, BLOCK), jnp.float32),
        ],
        compiler_params=pltpu.CompilerParams(vmem_limit_bytes=VMEM_LIMIT),
        cost_estimate=pl.CostEstimate(flops=2**22, bytes_accessed=4 * 2**20, transcendentals=0),
    )(*members)


def prepare_columns(data_ref, first, lhs, rate_ref):
    wide = data_ref[...].astype(jnp.float32)
    rate = 1.0 / wide[SCALE_ROW : SCALE_ROW + 1]
    squares = wide[:FEAT] * wide[:FEAT]
    tail = ones_and_norms(jnp.sum(squares, axis=0, keepdims=True), 3, 0)
    full = jnp.concatenate([wide, tail, jnp.zeros((384 - DEPTH, LENGTH), jnp.float32)], 0)
    turned = full.T[:, :DEPTH].astype(jnp.bfloat16)
    rate = jnp.broadcast_to(rate, (128, LENGTH)).T
    for c in range(2):
        lhs[first + c] = turned[c * BLOCK : (c + 1) * BLOCK]
        rate_ref[first + c] = rate[c * BLOCK : (c + 1) * BLOCK]


def list_pairs(mine_ref, theirs, rows_ref, cols_ref, count):
    def member(e, count):
        for side in range(2):
            for r in range(2):
                for c in range(2):
                    if side == 0:
                        used = mine_ref[e * PAIRS + lax.rem(N_SUB - e, N_SUB) * 4 + r * 2 + c]
                    else:
                        used = lax.shift_right_logical(theirs, e * 4 + c * 2 + r) & 1
                    rows_ref[count] = e * 2 + r
                    cols_ref[count] = side * 2 + c
                    count = count + used
        return count

    count = lax.fori_loop(0, N_SUB, member, count)
    for k in range(8):
        rows_ref[count + k] = NOBODY
        cols_ref[count + k] = 0
    rows_ref[COUNT] = count
    cols_ref[COUNT] = count
    return count


def tile_kernel(
    hop, first, last, mine_ref, blocks_ref, rate_ref, ahead_ref, behind_ref, extra_ref,
    tile_ref, rows_ref, cols_ref, sums_ref, lhs, col, even, odd, made, sems, *held
):
    total = held[0] if last else sums_ref
    prepare_columns(ahead_ref, 0, lhs, col)
    prepare_columns(behind_ref, 2, lhs, col)
    count = 0
    if first:
        prepare_columns(extra_ref, 4, lhs, col)
        for r in range(2):
            rows_ref[r] = r
            cols_ref[r] = 4 + r
        count = 2
        total[...] = jnp.zeros_like(total)
    else:
        total[...] = extra_ref[...]
    lane = lax.broadcasted_iota(jnp.int32, (1, 128), 1) - (hop - 1) * PAIRS
    weight = lax.shift_left(jnp.ones_like(lane), jnp.clip(lane, 0, PAIRS)).astype(jnp.float32)
    weight = jnp.where((lane >= 0) & (lane < PAIRS), weight, 0.0)
    theirs = behind_ref[MASK_ROW : MASK_ROW + 1, :128].astype(jnp.float32)
    theirs = jnp.sum(theirs * weight).astype(jnp.int32)
    count = list_pairs(mine_ref, theirs, rows_ref, cols_ref, jnp.int32(count))

    def product(at):
        row = lax.min(rows_ref[at], NOBODY - 1)
        return jnp.dot(lhs[cols_ref[at]], blocks_ref[row], preferred_element_type=jnp.float32)

    def finish(crossed, at):
        row = rows_ref[at]
        rate = col[cols_ref[at]]
        rates = jnp.concatenate([rate, rate], 1) * rate_ref[lax.min(row, NOBODY - 1), :1, :]
        tile = jnp.exp2(crossed * rates).astype(jnp.bfloat16)
        made[at] = tile
        total[row] += jnp.sum(tile.astype(jnp.float32).reshape(BLOCK // 8, 8, BLOCK), axis=0)

    even[...] = product(0)

    def step(k, _):
        odd[...] = product(2 * k + 1)
        finish(even[...], 2 * k)
        even[...] = product(2 * k + 2)
        finish(odd[...], 2 * k + 1)

        @pl.when(lax.rem(k, UNROLL // 2) == UNROLL // 2 - 1)
        def _():
            copy(lax.div(k, UNROLL // 2)).start()

        return 0

    def copy(group):
        span = pl.ds(group * UNROLL, UNROLL)
        return pltpu.make_async_copy(made.at[span], tile_ref.at[span], sems.at[group])

    steps = lax.shift_right_logical(count + 1, 1)
    lax.fori_loop(0, steps, step, 0)

    @pl.when(lax.rem(steps, UNROLL // 2) != 0)
    def _():
        copy(lax.div(steps, UNROLL // 2)).start()

    if last:
        for e in range(N_SUB):
            for r in range(2):
                sums = jnp.sum(total[2 * e + r], axis=0, keepdims=True)
                sums_ref[e, :, pl.ds(r * BLOCK, BLOCK)] = jnp.broadcast_to(sums, (8, BLOCK))

    def sent(group, _):
        copy(group).wait()
        return 0

    lax.fori_loop(0, lax.div(steps + (UNROLL // 2 - 1), UNROLL // 2), sent, 0)


def hop_tiles(hop, first, last, mine, blocks, rate, ahead, behind, extra):
    smem = pl.BlockSpec(memory_space=pltpu.SMEM)
    vmem = pl.BlockSpec(memory_space=pltpu.VMEM)
    columns = 6 if first else 4
    slots = UNROLL * (5 if first else 4)
    sums = (NOBODY + 1, 8, BLOCK)
    return pl.pallas_call(
        functools.partial(tile_kernel, hop, first, last),
        in_specs=[smem] + [vmem] * 5,
        out_specs=[pl.BlockSpec(memory_space=pl.ANY), smem, smem, vmem],
        out_shape=[
            jax.ShapeDtypeStruct((slots, BLOCK, BLOCK), jnp.bfloat16),
            jax.ShapeDtypeStruct((SLOTS,), jnp.int32),
            jax.ShapeDtypeStruct((SLOTS,), jnp.int32),
            jax.ShapeDtypeStruct((N_SUB, 8, LENGTH) if last else sums, jnp.float32),
        ],
        scratch_shapes=[
            pltpu.VMEM((columns, BLOCK, DEPTH), jnp.bfloat16),
            pltpu.VMEM((columns, BLOCK, 128), jnp.float32),
            pltpu.VMEM((BLOCK, BLOCK), jnp.float32),
            pltpu.VMEM((BLOCK, BLOCK), jnp.float32),
            pltpu.VMEM((slots, BLOCK, BLOCK), jnp.bfloat16),
            pltpu.SemaphoreType.DMA((slots // UNROLL,)),
        ]
        + ([pltpu.VMEM(sums, jnp.float32)] if last else []),
        compiler_params=pltpu.CompilerParams(vmem_limit_bytes=VMEM_LIMIT),
        cost_estimate=pl.CostEstimate(
            flops=16 * 2 * DEPTH * BLOCK * BLOCK,
            bytes_accessed=7 * 2**20,
            transcendentals=16 * BLOCK * BLOCK,
        ),
    )(mine, blocks, rate, ahead, behind, extra)


def stacked(vectors):
    if vectors.dtype == jnp.bfloat16:
        return vectors
    high = vectors.astype(jnp.bfloat16)
    return jnp.concatenate([high, (vectors - high.astype(jnp.float32)).astype(jnp.bfloat16)], 0)


def sweep_kernel(parts, order, *refs):
    list_refs, tile_refs, vector_refs = refs[:6], refs[6:9], refs[9:16]
    out_refs, (held, total, tiles, sems) = refs[16:20], refs[20:]
    vecs = vector_refs[0].shape[0]

    def copy(k, at):
        span = pl.ds(at * UNROLL, UNROLL)
        place = pl.ds((STARTS[k] + at) * UNROLL, UNROLL)
        return pltpu.make_async_copy(tile_refs[k].at[span], tiles.at[place], sems.at[STARTS[k] + at])

    groups = [lax.div(list_refs[2 * k][COUNT] + (UNROLL - 1), UNROLL) for k in range(REACH)]
    for k in range(REACH):

        def fetch(at, _, k=k):
            copy(k, at).start()
            return 0

        lax.fori_loop(0, groups[k], fetch, 0)

    for k in range(7):
        both = stacked(vector_refs[k][...])
        for c in range(2):
            held[2 * k + c] = both[:, c * BLOCK : (c + 1) * BLOCK]
    total[...] = jnp.zeros_like(total)

    for k, hop in enumerate(order):

        def step(at, _, k=k, hop=hop, rows_ref=list_refs[2 * k], cols_ref=list_refs[2 * k + 1]):
            copy(k, at).wait()
            terms = []
            for n in range(UNROLL):
                block = cols_ref[UNROLL * at + n]
                block = jnp.where(block >= 4, block - 4, block + 4 * hop - 2)
                tile = tiles[(STARTS[k] + at) * UNROLL + n]
                terms.append(jnp.dot(held[block], tile, preferred_element_type=jnp.float32))
            for n in range(UNROLL):
                total[rows_ref[UNROLL * at + n]] += terms[n]
            return 0

        lax.fori_loop(0, groups[k], step, 0)

    for e in range(N_SUB):
        for r in range(2):
            result = total[2 * e + r, :vecs]
            for part in range(1, parts):
                result = result + total[2 * e + r, part * vecs : (part + 1) * vecs]
            out_refs[e][:, pl.ds(r * BLOCK, BLOCK)] = result


def sweep(own, near, order, tiles):
    vecs = own.shape[0]
    smem = pl.BlockSpec(memory_space=pltpu.SMEM)
    vmem = pl.BlockSpec(memory_space=pltpu.VMEM)
    parts = 1 if own.dtype == jnp.bfloat16 else 2
    lists = [part for tile in tiles for part in tile[1:]]
    return pl.pallas_call(
        functools.partial(sweep_kernel, parts, order),
        in_specs=[smem] * 6 + [pl.BlockSpec(memory_space=pl.ANY)] * 3 + [vmem] * 7,
        out_specs=[vmem] * 4,
        out_shape=[jax.ShapeDtypeStruct((vecs, LENGTH), jnp.float32)] * 4,
        scratch_shapes=[
            pltpu.VMEM((14, parts * vecs, BLOCK), jnp.bfloat16),
            pltpu.VMEM((NOBODY + 1, parts * vecs, BLOCK), jnp.float32),
            pltpu.VMEM((GROUPS * UNROLL, BLOCK, BLOCK), jnp.bfloat16),
            pltpu.SemaphoreType.DMA((GROUPS,)),
        ],
        compiler_params=pltpu.CompilerParams(vmem_limit_bytes=SWEEP_LIMIT),
        cost_estimate=pl.CostEstimate(
            flops=50 * 2 * 128 * BLOCK * BLOCK, bytes_accessed=7 * 2**20, transcendentals=0
        ),
    )(*lists, *[tile[0] for tile in tiles], own, *[near[h] for h in (1, -1, 2, -2, 3, -3)])


def exchanged(parts):
    return [parts[0]] + [shifted(parts[e], "sub", -e) for e in range(1, N_SUB)]


def gram_of(image):
    return lax.dot_general(
        image, image, TRANS_B, precision=lax.Precision.HIGHEST, preferred_element_type=jnp.float32
    )


def inverse_factor(gram):
    count = gram.shape[0]
    place = lax.broadcasted_iota(jnp.int32, (count, 1), 0)
    across = lax.broadcasted_iota(jnp.int32, (count, count), 1)
    identity = jnp.where(across == place, 1.0, 0.0)
    joined = jnp.concatenate([gram, identity], 1)
    for k in range(count):
        column = jnp.where(place > k, joined[:, k : k + 1], 0.0)
        joined = joined - column * (joined[k : k + 1, :] * (1.0 / joined[k : k + 1, k : k + 1]))
    pivots = jnp.sum(joined[:, :count] * identity, axis=1, keepdims=True)
    diagonal = jnp.sum(gram * identity, axis=1, keepdims=True)
    return joined[:, count:] / jnp.sqrt(pivots), jnp.min(pivots / diagonal)


def exact_dot(left, right):
    return jnp.dot(left, right, precision=lax.Precision.HIGHEST, preferred_element_type=jnp.float32)


def image_of(root_ref, part_refs):
    first, second, third, fourth = (part_ref[...] for part_ref in part_refs)
    return root_ref[...] * ((first + second) + (third + fourth))


def image_kernel(scaled, root_ref, *refs):
    image = image_of(root_ref, refs[:4])
    refs[4][...] = root_ref[...] * image if scaled else image
    refs[5][...] = gram_of(image)


def solve_gram_kernel(gram_ref, image_ref, solved_ref, next_ref):
    image = exact_dot(inverse_factor(gram_ref[...])[0], image_ref[...])
    solved_ref[...] = image
    next_ref[...] = gram_of(image)


def solve_kernel(gram_ref, image_ref, solved_ref):
    solved_ref[...] = exact_dot(inverse_factor(gram_ref[...])[0], image_ref[...])


def solve_both_kernel(grams_ref, image_ref, solved_ref, sound_ref):
    count = image_ref.shape[0]
    first, quality = inverse_factor(grams_ref[:count])
    half = lax.dot_general(
        grams_ref[count:], first, TRANS_B, precision=lax.Precision.HIGHEST,
        preferred_element_type=jnp.float32,
    )
    second, next_quality = inverse_factor(exact_dot(first, half))
    solved_ref[...] = exact_dot(second, exact_dot(first, image_ref[...]))
    sound_ref[0] = jnp.where((quality > 0.05) & (next_quality > 0.001), 1, 0)


def on_device(trajectories, kernel_scale, start_vectors, pair_list):
    vecs, length = start_vectors.shape
    n_sub = lax.axis_size("sub")
    n_space = lax.axis_size("space")
    space_at = lax.axis_index("space")
    sub_at = lax.axis_index("sub")
    device = space_at * n_sub + sub_at

    row_blk = pair_list[:, 0] - device * 2
    col_dev = pair_list[:, 1] // 2
    hop = jnp.remainder(col_dev // n_sub - space_at, n_space)
    across = jnp.remainder(col_dev % n_sub - sub_at, n_sub)
    place = (((hop - 1) * n_sub + across) * 2 + row_blk) * 2 + pair_list[:, 1] % 2
    place = jnp.where(hop > 0, place, -1)
    used = jnp.any(place[:, None] == jnp.arange(length, dtype=jnp.int32)[None, :], axis=0)
    payload = jnp.concatenate(
        [
            trajectories,
            kernel_scale[None, :],
            used.astype(jnp.bfloat16)[None, :],
            jnp.zeros((ROWS - MASK_ROW - 1, length), jnp.bfloat16),
        ],
        0,
    )

    members = [payload] + [shifted(payload, "sub", e) for e in range(1, N_SUB)]
    near = {h: shifted(payload, "space", h) for h in (2, -2)}
    later, near[2], near[-2] = lax.optimization_barrier((payload, near[2], near[-2]))
    for h, source in ((1, later), (-1, later), (3, near[2]), (-3, near[-2])):
        near[h] = shifted(source, "space", 1 if h > 0 else -1)
    blocks, rate = row_operands(members)
    listed = jnp.stack([member[MASK_ROW, : REACH * PAIRS] for member in members]).astype(jnp.int32)

    order = (2, 1, 3)
    tiles = []
    carried = payload
    for at, h in enumerate(order):
        span = slice((h - 1) * PAIRS, h * PAIRS)
        mine = listed[:, span].reshape(N_SUB * PAIRS)
        *tile, carried = hop_tiles(
            h, at == 0, at == REACH - 1, mine, blocks, rate, near[h], near[-h], carried
        )
        tiles.append(tile)
    degree = carried
    shares = exchanged([degree[e, :1] for e in range(N_SUB)])
    root = lax.rsqrt((shares[0] + shares[1]) + (shares[2] + shares[3]))

    vector_shape = jax.ShapeDtypeStruct((vecs, length), jnp.float32)
    gram_shape = jax.ShapeDtypeStruct((vecs, vecs), jnp.float32)
    light = dict(
        cost_estimate=pl.CostEstimate(flops=2**20, bytes_accessed=2**17, transcendentals=0),
        compiler_params=pltpu.CompilerParams(vmem_limit_bytes=SMALL_LIMIT),
    )

    def imaged(parts, scaled):
        return pl.pallas_call(
            functools.partial(image_kernel, scaled), out_shape=[vector_shape, gram_shape], **light
        )(root, *exchanged(parts))

    scaled = (root * start_vectors).astype(jnp.bfloat16)
    raw, first_gram = imaged(sweep(scaled, space_window(scaled), order, tiles), True)

    image, second_gram = imaged(sweep(raw, space_window(raw), order, tiles), False)
    grams = summed(jnp.concatenate([first_gram, second_gram], 0))
    subspace, sound = pl.pallas_call(
        solve_both_kernel,
        in_specs=[pl.BlockSpec(memory_space=pltpu.VMEM)] * 2,
        out_specs=[pl.BlockSpec(memory_space=pltpu.VMEM), pl.BlockSpec(memory_space=pltpu.SMEM)],
        out_shape=[vector_shape, jax.ShapeDtypeStruct((1,), jnp.int32)],
        **light,
    )(grams, image)

    def directly():
        solved, gram = pl.pallas_call(
            solve_gram_kernel, out_shape=[vector_shape, gram_shape], **light
        )(grams[:vecs], image)
        return pl.pallas_call(solve_kernel, out_shape=vector_shape, **light)(summed(gram), solved)

    return lax.cond(sound[0] > 0, lambda: subspace, directly)


def solution(mesh):
    placed = (
        P(None, ("space", "sub")),
        P(("space", "sub")),
        P(None, ("space", "sub")),
        P(("space", "sub"), None),
    )
    return jax.shard_map(
        on_device, mesh=mesh, in_specs=placed, out_specs=P(None, ("space", "sub")), check_vma=False
    )
```

```python
import functools

import jax
import jax.numpy as jnp
from jax import lax
from jax.experimental import pallas as pl
from jax.experimental.pallas import tpu as pltpu
from jax.sharding import PartitionSpec as P

FEAT = 300
BLOCK = 256
LENGTH = 2 * BLOCK
REACH = 3
N_SUB = 4
ROWS = 304
DEPTH = 320
SCALE_ROW = 300
MASK_ROW = 301
PAIRS = 4 * N_SUB
SLOTS = 48
COUNT = SLOTS - 1
NOBODY = 2 * N_SUB
UNROLL = 8
STARTS = (0, 5, 9)
GROUPS = 13
LOG2E = 1.4426950408889634
VMEM_LIMIT = 12 * 1024 * 1024
SWEEP_LIMIT = 24 * 1024 * 1024
SMALL_LIMIT = 4 * 1024 * 1024
TRANS_B = (((1,), (1,)), ((), ()))


def shifted(value, axis, steps):
    count = lax.axis_size(axis)
    return lax.ppermute(value, axis, [((at + steps) % count, at) for at in range(count)])


def space_window(value):
    count = lax.axis_size("space")
    other = lax.ppermute(value, "space", [(at, at ^ 1) for at in range(count)])
    pair = jnp.stack([value, other])
    far = [(at, (at + (4 if at % 2 == 0 else -4)) % count) for at in range(count)]
    return value, other, shifted(pair, "space", 2), shifted(pair, "space", -2), lax.ppermute(other, "space", far)


def window_slot(hop, side):
    odd = lax.rem(lax.axis_index("space"), 2) == 1
    even_slot, odd_slot = {(1, 0): (1, 3), (1, 1): (5, 1), (2, 0): (2, 2), (2, 1): (4, 4), (3, 0): (3, 6), (3, 1): (6, 5)}[hop, side]
    return jnp.where(odd, odd_slot, even_slot)


def groups_by(key, n_space, n_sub):
    found = {}
    for place in range(n_space * n_sub):
        found.setdefault(key(place // n_sub, place % n_sub), []).append(place)
    return list(found.values())


def summed(value):
    n_space, n_sub = lax.axis_size("space"), lax.axis_size("sub")
    shape = value.shape
    value = value.reshape(-1, 128)
    for key in (lambda s, y: (s // 8, 0), lambda s, y: (s % 8, y)):
        groups = groups_by(key, n_space, n_sub)
        sent = jnp.broadcast_to(value[None], (len(groups[0]),) + value.shape)
        value = jnp.sum(
            lax.all_to_all(sent, ("space", "sub"), 0, 0, axis_index_groups=groups), 0
        )
    return value.reshape(shape)


def pieces(norm):
    high = norm.astype(jnp.bfloat16).astype(jnp.float32)
    rest = norm - high
    middle = rest.astype(jnp.bfloat16).astype(jnp.float32)
    return high, middle, rest - middle


def ones_and_norms(norm, ones_at, norms_at):
    place = lax.broadcasted_iota(jnp.int32, (DEPTH - ROWS, 1), 0)
    tail = jnp.where((place >= ones_at) & (place < ones_at + 3), 1.0, 0.0)
    for k, piece in enumerate(pieces(norm)):
        tail = jnp.where(place == norms_at + k, -piece, tail)
    return tail


def rows_kernel(*refs):
    rows_ref, rate_ref = refs[N_SUB:]
    for e in range(N_SUB):
        wide = refs[e][:FEAT, :].astype(jnp.float32)
        tail = ones_and_norms(jnp.sum(wide * wide, axis=0, keepdims=True), 0, 3)
        tail = tail.astype(jnp.bfloat16)
        rate = LOG2E / refs[e][SCALE_ROW : SCALE_ROW + 1, :].astype(jnp.float32)
        below = lax.broadcasted_iota(jnp.int32, (ROWS, 1), 0) < FEAT
        twice = jnp.where(below, 2.0 * refs[e][...].astype(jnp.float32), 0.0).astype(jnp.bfloat16)
        for r in range(2):
            span = slice(r * BLOCK, (r + 1) * BLOCK)
            rows_ref[2 * e + r, :ROWS] = twice[:, span]
            rows_ref[2 * e + r, ROWS:] = tail[:, span]
            rate_ref[2 * e + r] = jnp.broadcast_to(rate[:, span], (8, BLOCK))


def row_operands(members):
    return pl.pallas_call(
        rows_kernel,
        out_shape=[
            jax.ShapeDtypeStruct((2 * N_SUB, DEPTH, BLOCK), jnp.bfloat16),
            jax.ShapeDtypeStruct((2 * N_SUB, 8, BLOCK), jnp.float32),
        ],
        compiler_params=pltpu.CompilerParams(vmem_limit_bytes=VMEM_LIMIT),
        cost_estimate=pl.CostEstimate(flops=2**22, bytes_accessed=4 * 2**20, transcendentals=0),
    )(*members)


def prepare_columns(data_ref, first, lhs, rate_ref):
    wide = data_ref[...].astype(jnp.float32)
    rate = 1.0 / wide[SCALE_ROW : SCALE_ROW + 1]
    squares = wide[:FEAT] * wide[:FEAT]
    tail = ones_and_norms(jnp.sum(squares, axis=0, keepdims=True), 3, 0)
    full = jnp.concatenate([wide, tail, jnp.zeros((384 - DEPTH, LENGTH), jnp.float32)], 0)
    turned = full.T[:, :DEPTH].astype(jnp.bfloat16)
    rate = jnp.broadcast_to(rate, (128, LENGTH)).T
    for c in range(2):
        lhs[first + c] = turned[c * BLOCK : (c + 1) * BLOCK]
        rate_ref[first + c] = rate[c * BLOCK : (c + 1) * BLOCK]


def list_pairs(mine_ref, theirs, rows_ref, cols_ref, count):
    def member(e, count):
        for side in range(2):
            for r in range(2):
                for c in range(2):
                    if side == 0:
                        used = mine_ref[e * PAIRS + lax.rem(N_SUB - e, N_SUB) * 4 + r * 2 + c]
                    else:
                        used = lax.shift_right_logical(theirs, e * 4 + c * 2 + r) & 1
                    rows_ref[count] = e * 2 + r
                    cols_ref[count] = side * 2 + c
                    count = count + used
        return count

    count = lax.fori_loop(0, N_SUB, member, count)
    for k in range(8):
        rows_ref[count + k] = NOBODY
        cols_ref[count + k] = 0
    rows_ref[COUNT] = count
    cols_ref[COUNT] = count
    return count


def tile_kernel(
    hop, first, last, mine_ref, blocks_ref, rate_ref, ahead_ref, behind_ref, extra_ref,
    tile_ref, rows_ref, cols_ref, sums_ref, lhs, col, even, odd, made, sems, *held
):
    total = held[0] if last else sums_ref
    prepare_columns(ahead_ref, 0, lhs, col)
    prepare_columns(behind_ref, 2, lhs, col)
    count = 0
    if first:
        prepare_columns(extra_ref, 4, lhs, col)
        for r in range(2):
            rows_ref[r] = r
            cols_ref[r] = 4 + r
        count = 2
        total[...] = jnp.zeros_like(total)
    else:
        total[...] = extra_ref[...]
    lane = lax.broadcasted_iota(jnp.int32, (1, 128), 1) - (hop - 1) * PAIRS
    weight = lax.shift_left(jnp.ones_like(lane), jnp.clip(lane, 0, PAIRS)).astype(jnp.float32)
    weight = jnp.where((lane >= 0) & (lane < PAIRS), weight, 0.0)
    theirs = behind_ref[MASK_ROW : MASK_ROW + 1, :128].astype(jnp.float32)
    theirs = jnp.sum(theirs * weight).astype(jnp.int32)
    count = list_pairs(mine_ref, theirs, rows_ref, cols_ref, jnp.int32(count))

    def product(at):
        row = lax.min(rows_ref[at], NOBODY - 1)
        return jnp.dot(lhs[cols_ref[at]], blocks_ref[row], preferred_element_type=jnp.float32)

    def finish(crossed, at):
        row = rows_ref[at]
        rate = col[cols_ref[at]]
        rates = jnp.concatenate([rate, rate], 1) * rate_ref[lax.min(row, NOBODY - 1), :1, :]
        tile = jnp.exp2(crossed * rates).astype(jnp.bfloat16)
        made[at] = tile
        total[row] += jnp.sum(tile.astype(jnp.float32).reshape(BLOCK // 8, 8, BLOCK), axis=0)

    even[...] = product(0)

    def step(k, _):
        odd[...] = product(2 * k + 1)
        finish(even[...], 2 * k)
        even[...] = product(2 * k + 2)
        finish(odd[...], 2 * k + 1)

        @pl.when(lax.rem(k, UNROLL // 2) == UNROLL // 2 - 1)
        def _():
            copy(lax.div(k, UNROLL // 2)).start()

        return 0

    def copy(group):
        span = pl.ds(group * UNROLL, UNROLL)
        return pltpu.make_async_copy(made.at[span], tile_ref.at[span], sems.at[group])

    steps = lax.shift_right_logical(count + 1, 1)
    lax.fori_loop(0, steps, step, 0)

    @pl.when(lax.rem(steps, UNROLL // 2) != 0)
    def _():
        copy(lax.div(steps, UNROLL // 2)).start()

    if last:
        for e in range(N_SUB):
            for r in range(2):
                sums = jnp.sum(total[2 * e + r], axis=0, keepdims=True)
                sums_ref[e, :, pl.ds(r * BLOCK, BLOCK)] = jnp.broadcast_to(sums, (8, BLOCK))

    def sent(group, _):
        copy(group).wait()
        return 0

    lax.fori_loop(0, lax.div(steps + (UNROLL // 2 - 1), UNROLL // 2), sent, 0)


def hop_tiles(hop, first, last, mine, blocks, rate, ahead, behind, extra):
    smem = pl.BlockSpec(memory_space=pltpu.SMEM)
    vmem = pl.BlockSpec(memory_space=pltpu.VMEM)
    columns = 6 if first else 4
    slots = UNROLL * (5 if first else 4)
    sums = (NOBODY + 1, 8, BLOCK)
    return pl.pallas_call(
        functools.partial(tile_kernel, hop, first, last),
        in_specs=[smem] + [vmem] * 5,
        out_specs=[pl.BlockSpec(memory_space=pl.ANY), smem, smem, vmem],
        out_shape=[
            jax.ShapeDtypeStruct((slots, BLOCK, BLOCK), jnp.bfloat16),
            jax.ShapeDtypeStruct((SLOTS,), jnp.int32),
            jax.ShapeDtypeStruct((SLOTS,), jnp.int32),
            jax.ShapeDtypeStruct((N_SUB, 8, LENGTH) if last else sums, jnp.float32),
        ],
        scratch_shapes=[
            pltpu.VMEM((columns, BLOCK, DEPTH), jnp.bfloat16),
            pltpu.VMEM((columns, BLOCK, 128), jnp.float32),
            pltpu.VMEM((BLOCK, BLOCK), jnp.float32),
            pltpu.VMEM((BLOCK, BLOCK), jnp.float32),
            pltpu.VMEM((slots, BLOCK, BLOCK), jnp.bfloat16),
            pltpu.SemaphoreType.DMA((slots // UNROLL,)),
        ]
        + ([pltpu.VMEM(sums, jnp.float32)] if last else []),
        compiler_params=pltpu.CompilerParams(vmem_limit_bytes=VMEM_LIMIT),
        cost_estimate=pl.CostEstimate(
            flops=16 * 2 * DEPTH * BLOCK * BLOCK,
            bytes_accessed=7 * 2**20,
            transcendentals=16 * BLOCK * BLOCK,
        ),
    )(mine, blocks, rate, ahead, behind, extra)


def stacked(vectors):
    if vectors.dtype == jnp.bfloat16:
        return vectors
    high = vectors.astype(jnp.bfloat16)
    return jnp.concatenate([high, (vectors - high.astype(jnp.float32)).astype(jnp.bfloat16)], 0)


def sweep_kernel(parts, order, *refs):
    list_refs, tile_refs, vector_refs = refs[:6], refs[6:9], refs[9:14]
    out_refs, (held, total, tiles, sems) = refs[14:18], refs[18:]
    vecs = vector_refs[0].shape[0]

    def copy(k, at):
        span = pl.ds(at * UNROLL, UNROLL)
        place = pl.ds((STARTS[k] + at) * UNROLL, UNROLL)
        return pltpu.make_async_copy(tile_refs[k].at[span], tiles.at[place], sems.at[STARTS[k] + at])

    groups = [lax.div(list_refs[2 * k][COUNT] + (UNROLL - 1), UNROLL) for k in range(REACH)]
    for k in range(REACH):

        def fetch(at, _, k=k):
            copy(k, at).start()
            return 0

        lax.fori_loop(0, groups[k], fetch, 0)

    own, other, ahead, behind, far = vector_refs
    for k, vectors in enumerate(
        (own[...], other[...], ahead[0], ahead[1], behind[0], behind[1], far[...])
    ):
        both = stacked(vectors)
        for c in range(2):
            held[2 * k + c] = both[:, c * BLOCK : (c + 1) * BLOCK]
    total[...] = jnp.zeros_like(total)

    for k, hop in enumerate(order):
        slots = [window_slot(hop, side) for side in range(2)]

        def step(at, _, k=k, slots=slots, rows_ref=list_refs[2 * k], cols_ref=list_refs[2 * k + 1]):
            copy(k, at).wait()
            terms = []
            for n in range(UNROLL):
                block = cols_ref[UNROLL * at + n]
                slot = jnp.where(block >= 4, 0, jnp.where(block >= 2, slots[1], slots[0]))
                block = 2 * slot + (block & 1)
                tile = tiles[(STARTS[k] + at) * UNROLL + n]
                terms.append(jnp.dot(held[block], tile, preferred_element_type=jnp.float32))
            for n in range(UNROLL):
                total[rows_ref[UNROLL * at + n]] += terms[n]
            return 0

        lax.fori_loop(0, groups[k], step, 0)

    for e in range(N_SUB):
        for r in range(2):
            result = total[2 * e + r, :vecs]
            for part in range(1, parts):
                result = result + total[2 * e + r, part * vecs : (part + 1) * vecs]
            out_refs[e][:, pl.ds(r * BLOCK, BLOCK)] = result


def sweep(near, order, tiles):
    own = near[0]
    vecs = own.shape[0]
    smem = pl.BlockSpec(memory_space=pltpu.SMEM)
    vmem = pl.BlockSpec(memory_space=pltpu.VMEM)
    parts = 1 if own.dtype == jnp.bfloat16 else 2
    lists = [part for tile in tiles for part in tile[1:]]
    return pl.pallas_call(
        functools.partial(sweep_kernel, parts, order),
        in_specs=[smem] * 6 + [pl.BlockSpec(memory_space=pl.ANY)] * 3 + [vmem] * 5,
        out_specs=[vmem] * 4,
        out_shape=[jax.ShapeDtypeStruct((vecs, LENGTH), jnp.float32)] * 4,
        scratch_shapes=[
            pltpu.VMEM((14, parts * vecs, BLOCK), jnp.bfloat16),
            pltpu.VMEM((NOBODY + 1, parts * vecs, BLOCK), jnp.float32),
            pltpu.VMEM((GROUPS * UNROLL, BLOCK, BLOCK), jnp.bfloat16),
            pltpu.SemaphoreType.DMA((GROUPS,)),
        ],
        compiler_params=pltpu.CompilerParams(vmem_limit_bytes=SWEEP_LIMIT),
        cost_estimate=pl.CostEstimate(
            flops=50 * 2 * 128 * BLOCK * BLOCK, bytes_accessed=7 * 2**20, transcendentals=0
        ),
    )(*lists, *[tile[0] for tile in tiles], *near)


def exchanged(parts):
    return [parts[0]] + [shifted(parts[e], "sub", -e) for e in range(1, N_SUB)]


def gram_of(image):
    return lax.dot_general(
        image, image, TRANS_B, precision=lax.Precision.HIGHEST, preferred_element_type=jnp.float32
    )


def inverse_factor(gram):
    count = gram.shape[0]
    place = lax.broadcasted_iota(jnp.int32, (count, 1), 0)
    across = lax.broadcasted_iota(jnp.int32, (count, count), 1)
    identity = jnp.where(across == place, 1.0, 0.0)
    joined = jnp.concatenate([gram, identity], 1)
    for k in range(count):
        column = jnp.where(place > k, joined[:, k : k + 1], 0.0)
        joined = joined - column * (joined[k : k + 1, :] * (1.0 / joined[k : k + 1, k : k + 1]))
    pivots = jnp.sum(joined[:, :count] * identity, axis=1, keepdims=True)
    diagonal = jnp.sum(gram * identity, axis=1, keepdims=True)
    return joined[:, count:] / jnp.sqrt(pivots), jnp.min(pivots / diagonal)


def exact_dot(left, right):
    return jnp.dot(left, right, precision=lax.Precision.HIGHEST, preferred_element_type=jnp.float32)


def image_of(root_ref, part_refs):
    first, second, third, fourth = (part_ref[...] for part_ref in part_refs)
    return root_ref[...] * ((first + second) + (third + fourth))


def image_kernel(scaled, root_ref, *refs):
    image = image_of(root_ref, refs[:4])
    refs[4][...] = root_ref[...] * image if scaled else image
    refs[5][...] = gram_of(image)


def solve_gram_kernel(gram_ref, image_ref, solved_ref, next_ref):
    image = exact_dot(inverse_factor(gram_ref[...])[0], image_ref[...])
    solved_ref[...] = image
    next_ref[...] = gram_of(image)


def solve_kernel(gram_ref, image_ref, solved_ref):
    solved_ref[...] = exact_dot(inverse_factor(gram_ref[...])[0], image_ref[...])


def solve_both_kernel(grams_ref, image_ref, solved_ref, sound_ref):
    count = image_ref.shape[0]
    first, quality = inverse_factor(grams_ref[:count])
    half = lax.dot_general(
        grams_ref[count:], first, TRANS_B, precision=lax.Precision.HIGHEST,
        preferred_element_type=jnp.float32,
    )
    second, next_quality = inverse_factor(exact_dot(first, half))
    solved_ref[...] = exact_dot(second, exact_dot(first, image_ref[...]))
    sound_ref[0] = jnp.where((quality > 0.05) & (next_quality > 0.001), 1, 0)


def payload_kernel(pairs_ref, data_ref, scale_ref, payload_ref):
    n_space, n_sub = lax.axis_size("space"), lax.axis_size("sub")
    space_at, sub_at = lax.axis_index("space"), lax.axis_index("sub")
    lane = lax.broadcasted_iota(jnp.int32, (1, LENGTH), 1)
    used = jnp.zeros((1, LENGTH), jnp.float32)
    for k in range(pairs_ref.shape[0]):
        row, col = pairs_ref[k, 0], pairs_ref[k, 1]
        device = lax.shift_right_logical(col, 1)
        hop = lax.rem(lax.div(device, n_sub) - space_at + n_space, n_space)
        across = lax.rem(lax.rem(device, n_sub) - sub_at + n_sub, n_sub)
        place = (((hop - 1) * n_sub + across) * 2 + (row & 1)) * 2 + (col & 1)
        used = jnp.where((lane == place) & (hop > 0), 1.0, used)
    payload_ref[: ROWS - 16] = data_ref[: ROWS - 16]
    payload_ref[ROWS - 16 :] = jnp.concatenate(
        [
            data_ref[ROWS - 16 : FEAT].astype(jnp.float32),
            scale_ref[...].astype(jnp.float32),
            used,
            jnp.zeros((ROWS - MASK_ROW - 1, LENGTH), jnp.float32),
        ],
        0,
    ).astype(jnp.bfloat16)


def on_device(trajectories, kernel_scale, start_vectors, pair_list):
    vecs, length = start_vectors.shape
    light = dict(
        cost_estimate=pl.CostEstimate(flops=2**20, bytes_accessed=2**17, transcendentals=0),
        compiler_params=pltpu.CompilerParams(vmem_limit_bytes=SMALL_LIMIT),
    )

    payload = pl.pallas_call(
        payload_kernel,
        in_specs=[pl.BlockSpec(memory_space=pltpu.SMEM)] + [pl.BlockSpec(memory_space=pltpu.VMEM)] * 2,
        out_shape=jax.ShapeDtypeStruct((ROWS, length), jnp.bfloat16),
        **light,
    )(pair_list, trajectories, kernel_scale[None, :])

    members = [payload] + [shifted(payload, "sub", e) for e in range(1, N_SUB)]
    near = {h: shifted(payload, "space", h) for h in (2, -2)}
    later, near[2], near[-2] = lax.optimization_barrier((payload, near[2], near[-2]))
    for h, source in ((1, later), (-1, later), (3, near[2]), (-3, near[-2])):
        near[h] = shifted(source, "space", 1 if h > 0 else -1)
    blocks, rate = row_operands(members)
    listed = jnp.stack([member[MASK_ROW, : REACH * PAIRS] for member in members]).astype(jnp.int32)

    order = (2, 1, 3)
    tiles = []
    carried = payload
    for at, h in enumerate(order):
        span = slice((h - 1) * PAIRS, h * PAIRS)
        mine = listed[:, span].reshape(N_SUB * PAIRS)
        *tile, carried = hop_tiles(
            h, at == 0, at == REACH - 1, mine, blocks, rate, near[h], near[-h], carried
        )
        tiles.append(tile)
    degree = carried
    shares = exchanged([degree[e, :1] for e in range(N_SUB)])
    root = lax.rsqrt((shares[0] + shares[1]) + (shares[2] + shares[3]))

    vector_shape = jax.ShapeDtypeStruct((vecs, length), jnp.float32)
    gram_shape = jax.ShapeDtypeStruct((vecs, vecs), jnp.float32)
    def imaged(parts, scaled):
        return pl.pallas_call(
            functools.partial(image_kernel, scaled), out_shape=[vector_shape, gram_shape], **light
        )(root, *exchanged(parts))

    scaled = (root * start_vectors).astype(jnp.bfloat16)
    raw, first_gram = imaged(sweep(space_window(scaled), order, tiles), True)

    image, second_gram = imaged(sweep(space_window(raw), order, tiles), False)
    grams = summed(jnp.concatenate([first_gram, second_gram], 0))
    subspace, sound = pl.pallas_call(
        solve_both_kernel,
        in_specs=[pl.BlockSpec(memory_space=pltpu.VMEM)] * 2,
        out_specs=[pl.BlockSpec(memory_space=pltpu.VMEM), pl.BlockSpec(memory_space=pltpu.SMEM)],
        out_shape=[vector_shape, jax.ShapeDtypeStruct((1,), jnp.int32)],
        **light,
    )(grams, image)

    def directly():
        solved, gram = pl.pallas_call(
            solve_gram_kernel, out_shape=[vector_shape, gram_shape], **light
        )(grams[:vecs], image)
        return pl.pallas_call(solve_kernel, out_shape=vector_shape, **light)(summed(gram), solved)

    return lax.cond(sound[0] > 0, lambda: subspace, directly)


def solution(mesh):
    placed = (
        P(None, ("space", "sub")),
        P(("space", "sub")),
        P(None, ("space", "sub")),
        P(("space", "sub"), None),
    )
    return jax.shard_map(
        on_device, mesh=mesh, in_specs=placed, out_specs=P(None, ("space", "sub")), check_vma=False
    )
```

```python
import functools

import jax
import jax.numpy as jnp
from jax import lax
from jax.experimental import pallas as pl
from jax.experimental.pallas import tpu as pltpu
from jax.sharding import PartitionSpec as P

FEAT = 300
BLOCK = 256
LENGTH = 2 * BLOCK
REACH = 3
N_SUB = 4
ROWS = 304
DEPTH = 320
SCALE_ROW = 300
MASK_ROW = 301
PAIRS = 4 * N_SUB
SLOTS = 80
COUNT = SLOTS - 1
NOBODY = 2 * N_SUB
UNROLL = 8
HALF = UNROLL // 2
HOPS = ((2,), (1, 3))
STARTS = (0, 5)
GROUPS = 13
LOG2E = 1.4426950408889634
VMEM_LIMIT = 24 * 1024 * 1024
SWEEP_LIMIT = 24 * 1024 * 1024
SMALL_LIMIT = 4 * 1024 * 1024
TRANS_B = (((1,), (1,)), ((), ()))


def shifted(value, axis, steps):
    count = lax.axis_size(axis)
    return lax.ppermute(value, axis, [((at + steps) % count, at) for at in range(count)])


def space_window(value):
    count = lax.axis_size("space")
    swap = [(at, at ^ 1) for at in range(count)]
    far = [(at, (at + (3 if at % 2 else -3)) % count) for at in range(count)]
    other, far = lax.ppermute(value, "space", swap), lax.ppermute(value, "space", far)
    beside = jnp.stack([shifted(value, "space", 2), shifted(value, "space", -2)])
    return value, other, beside, lax.ppermute(beside, "space", swap), far


def window_slot(hop, side):
    odd = lax.rem(lax.axis_index("space"), 2) == 1
    even_slot, odd_slot = {(1, 0): (1, 3), (1, 1): (5, 1), (2, 0): (2, 2), (2, 1): (4, 4), (3, 0): (3, 6), (3, 1): (6, 5)}[hop, side]
    return jnp.where(odd, odd_slot, even_slot)


def groups_by(key, n_space, n_sub):
    found = {}
    for place in range(n_space * n_sub):
        found.setdefault(key(place // n_sub, place % n_sub), []).append(place)
    return list(found.values())


def summed(value):
    n_space, n_sub = lax.axis_size("space"), lax.axis_size("sub")
    shape = value.shape
    value = value.reshape(-1, 128)
    for key in (lambda s, y: (s // 8, 0), lambda s, y: (s % 8, y)):
        groups = groups_by(key, n_space, n_sub)
        sent = jnp.broadcast_to(value[None], (len(groups[0]),) + value.shape)
        value = jnp.sum(
            lax.all_to_all(sent, ("space", "sub"), 0, 0, axis_index_groups=groups), 0
        )
    return value.reshape(shape)


def pieces(norm):
    high = norm.astype(jnp.bfloat16).astype(jnp.float32)
    rest = norm - high
    middle = rest.astype(jnp.bfloat16).astype(jnp.float32)
    return high, middle, rest - middle


def ones_and_norms(norm, ones_at, norms_at):
    place = lax.broadcasted_iota(jnp.int32, (DEPTH - ROWS, 1), 0)
    tail = jnp.where((place >= ones_at) & (place < ones_at + 3), 1.0, 0.0)
    for k, piece in enumerate(pieces(norm)):
        tail = jnp.where(place == norms_at + k, -piece, tail)
    return tail


def rows_kernel(*refs):
    rows_ref, rate_ref = refs[N_SUB:]
    for e in range(N_SUB):
        wide = refs[e][:FEAT, :].astype(jnp.float32)
        tail = ones_and_norms(jnp.sum(wide * wide, axis=0, keepdims=True), 0, 3)
        tail = tail.astype(jnp.bfloat16)
        rate = LOG2E / refs[e][SCALE_ROW : SCALE_ROW + 1, :].astype(jnp.float32)
        below = lax.broadcasted_iota(jnp.int32, (ROWS, 1), 0) < FEAT
        twice = jnp.where(below, 2.0 * refs[e][...].astype(jnp.float32), 0.0).astype(jnp.bfloat16)
        for r in range(2):
            span = slice(r * BLOCK, (r + 1) * BLOCK)
            rows_ref[2 * e + r, :ROWS] = twice[:, span]
            rows_ref[2 * e + r, ROWS:] = tail[:, span]
            rate_ref[2 * e + r] = jnp.broadcast_to(rate[:, span], (8, BLOCK))


def row_operands(members):
    return pl.pallas_call(
        rows_kernel,
        out_shape=[
            jax.ShapeDtypeStruct((2 * N_SUB, DEPTH, BLOCK), jnp.bfloat16),
            jax.ShapeDtypeStruct((2 * N_SUB, 8, BLOCK), jnp.float32),
        ],
        compiler_params=pltpu.CompilerParams(vmem_limit_bytes=VMEM_LIMIT),
        cost_estimate=pl.CostEstimate(flops=2**22, bytes_accessed=4 * 2**20, transcendentals=0),
    )(*members)


def prepare_columns(data_ref, first, lhs, rate_ref):
    wide = data_ref[...].astype(jnp.float32)
    rate = 1.0 / wide[SCALE_ROW : SCALE_ROW + 1]
    squares = wide[:FEAT] * wide[:FEAT]
    tail = ones_and_norms(jnp.sum(squares, axis=0, keepdims=True), 3, 0)
    full = jnp.concatenate([wide, tail, jnp.zeros((384 - DEPTH, LENGTH), jnp.float32)], 0)
    turned = full.T[:, :DEPTH].astype(jnp.bfloat16)
    rate = jnp.broadcast_to(rate, (128, LENGTH)).T
    for c in range(2):
        lhs[first + c] = turned[c * BLOCK : (c + 1) * BLOCK]
        rate_ref[first + c] = rate[c * BLOCK : (c + 1) * BLOCK]


def list_pairs(hops, mine_ref, theirs, rows_ref, cols_ref, count):
    def member(e, count):
        for k, bits in enumerate(theirs):
            for side in range(2):
                for r in range(2):
                    for c in range(2):
                        if side == 0:
                            place = lax.rem(N_SUB - e, N_SUB) * 4 + r * 2 + c
                            used = mine_ref[(e * REACH + hops[k] - 1) * PAIRS + place]
                        else:
                            used = lax.shift_right_logical(bits, e * 4 + c * 2 + r) & 1
                        rows_ref[count] = e * 2 + r
                        cols_ref[count] = k * 4 + side * 2 + c
                        count = count + used
        return count

    count = lax.fori_loop(0, N_SUB, member, count)
    for k in range(UNROLL + HALF):
        rows_ref[count + k] = NOBODY
        cols_ref[count + k] = 0
    rows_ref[COUNT] = count
    cols_ref[COUNT] = count
    return count


def listed_behind(data_ref, hop):
    lane = lax.broadcasted_iota(jnp.int32, (1, 128), 1) - (hop - 1) * PAIRS
    weight = lax.shift_left(jnp.ones_like(lane), jnp.clip(lane, 0, PAIRS)).astype(jnp.float32)
    weight = jnp.where((lane >= 0) & (lane < PAIRS), weight, 0.0)
    used = data_ref[MASK_ROW : MASK_ROW + 1, :128].astype(jnp.float32)
    return jnp.sum(used * weight).astype(jnp.int32)


def tile_kernel(hops, first, last, mine_ref, blocks_ref, rate_ref, *refs):
    window_refs, extra_ref, refs = refs[: 2 * len(hops)], refs[2 * len(hops)], refs[2 * len(hops) + 1 :]
    tile_ref, rows_ref, cols_ref, sums_ref, lhs, col, even, odd, made, sems, *held = refs
    total = held[0] if last else sums_ref
    for k, window_ref in enumerate(window_refs):
        prepare_columns(window_ref, 2 * k, lhs, col)
    count = 0
    if first:
        prepare_columns(extra_ref, 4 * len(hops), lhs, col)
        for r in range(2):
            rows_ref[r] = r
            cols_ref[r] = 4 * len(hops) + r
        count = 2
        total[...] = jnp.zeros_like(total)
    else:
        total[...] = extra_ref[...]
    theirs = [listed_behind(window_refs[2 * k + 1], hop) for k, hop in enumerate(hops)]
    count = list_pairs(hops, mine_ref, theirs, rows_ref, cols_ref, jnp.int32(count))

    def products(buffer, base):
        for n in range(HALF):
            row = lax.min(rows_ref[base + n], NOBODY - 1)
            buffer[n] = jnp.dot(
                lhs[cols_ref[base + n]], blocks_ref[row], preferred_element_type=jnp.float32
            )

    def finish(buffer, base):
        for n in range(HALF):
            at = base + n
            row = rows_ref[at]
            rate = col[cols_ref[at]]
            rates = jnp.concatenate([rate, rate], 1) * rate_ref[lax.min(row, NOBODY - 1), :1, :]
            tile = jnp.exp2(buffer[n] * rates).astype(jnp.bfloat16)
            made[at] = tile
            total[row] += jnp.sum(tile.astype(jnp.float32).reshape(BLOCK // 8, 8, BLOCK), axis=0)

    def copy(group):
        span = pl.ds(group * UNROLL, UNROLL)
        return pltpu.make_async_copy(made.at[span], tile_ref.at[span], sems.at[group])

    products(even, 0)

    def step(group, _):
        products(odd, UNROLL * group + HALF)
        finish(even, UNROLL * group)
        products(even, UNROLL * group + UNROLL)
        finish(odd, UNROLL * group + HALF)
        copy(group).start()
        return 0

    groups = lax.div(count + (UNROLL - 1), UNROLL)
    lax.fori_loop(0, groups, step, 0)
    if last:
        for e in range(N_SUB):
            for r in range(2):
                sums = jnp.sum(total[2 * e + r], axis=0, keepdims=True)
                sums_ref[e, :, pl.ds(r * BLOCK, BLOCK)] = jnp.broadcast_to(sums, (8, BLOCK))

    def sent(group, _):
        copy(group).wait()
        return 0

    lax.fori_loop(0, groups, sent, 0)


def hop_tiles(hops, first, last, mine, blocks, rate, windows, extra):
    smem = pl.BlockSpec(memory_space=pltpu.SMEM)
    vmem = pl.BlockSpec(memory_space=pltpu.VMEM)
    columns = 4 * len(hops) + (2 if first else 0)
    slots = 2 * len(hops) * PAIRS + (UNROLL if first else 0)
    sums = (NOBODY + 1, 8, BLOCK)
    return pl.pallas_call(
        functools.partial(tile_kernel, hops, first, last),
        in_specs=[smem] + [vmem] * (3 + len(windows)),
        out_specs=[pl.BlockSpec(memory_space=pl.ANY), smem, smem, vmem],
        out_shape=[
            jax.ShapeDtypeStruct((slots, BLOCK, BLOCK), jnp.bfloat16),
            jax.ShapeDtypeStruct((SLOTS,), jnp.int32),
            jax.ShapeDtypeStruct((SLOTS,), jnp.int32),
            jax.ShapeDtypeStruct((N_SUB, 8, LENGTH) if last else sums, jnp.float32),
        ],
        scratch_shapes=[
            pltpu.VMEM((columns, BLOCK, DEPTH), jnp.bfloat16),
            pltpu.VMEM((columns, BLOCK, 128), jnp.float32),
            pltpu.VMEM((HALF, BLOCK, BLOCK), jnp.float32),
            pltpu.VMEM((HALF, BLOCK, BLOCK), jnp.float32),
            pltpu.VMEM((slots, BLOCK, BLOCK), jnp.bfloat16),
            pltpu.SemaphoreType.DMA((slots // UNROLL,)),
        ]
        + ([pltpu.VMEM(sums, jnp.float32)] if last else []),
        compiler_params=pltpu.CompilerParams(vmem_limit_bytes=VMEM_LIMIT),
        cost_estimate=pl.CostEstimate(
            flops=16 * len(hops) * 2 * DEPTH * BLOCK * BLOCK,
            bytes_accessed=7 * 2**20,
            transcendentals=16 * len(hops) * BLOCK * BLOCK,
        ),
    )(mine, blocks, rate, *windows, extra)


def stacked(vectors):
    if vectors.dtype == jnp.bfloat16:
        return vectors
    high = vectors.astype(jnp.bfloat16)
    return jnp.concatenate([high, (vectors - high.astype(jnp.float32)).astype(jnp.bfloat16)], 0)


def sweep_kernel(parts, *refs):
    list_refs, tile_refs, vector_refs = refs[:4], refs[4:6], refs[6:11]
    out_refs, (held, total, tiles, sems) = refs[11:15], refs[15:]
    vecs = vector_refs[0].shape[0]

    def copy(k, at):
        span = pl.ds(at * UNROLL, UNROLL)
        place = pl.ds((STARTS[k] + at) * UNROLL, UNROLL)
        return pltpu.make_async_copy(tile_refs[k].at[span], tiles.at[place], sems.at[STARTS[k] + at])

    groups = [lax.div(list_refs[2 * k][COUNT] + (UNROLL - 1), UNROLL) for k in range(len(HOPS))]
    for k in range(len(HOPS)):

        def fetch(at, _, k=k):
            copy(k, at).start()
            return 0

        lax.fori_loop(0, groups[k], fetch, 0)

    own, other, beside, swapped, far = vector_refs
    for k, vectors in enumerate(
        (own[...], other[...], beside[0], swapped[0], beside[1], swapped[1], far[...])
    ):
        both = stacked(vectors)
        for c in range(2):
            held[2 * k + c] = both[:, c * BLOCK : (c + 1) * BLOCK]
    total[...] = jnp.zeros_like(total)

    for k, hops in enumerate(HOPS):
        slots = [window_slot(hop, side) for hop in hops for side in range(2)]

        def step(at, _, k=k, slots=slots, rows_ref=list_refs[2 * k], cols_ref=list_refs[2 * k + 1]):
            copy(k, at).wait()
            terms = []
            for n in range(UNROLL):
                block = cols_ref[UNROLL * at + n]
                slot = 0
                for at_slot, found in enumerate(slots):
                    slot = jnp.where(lax.shift_right_logical(block, 1) == at_slot, found, slot)
                block = 2 * slot + (block & 1)
                tile = tiles[(STARTS[k] + at) * UNROLL + n]
                terms.append(jnp.dot(held[block], tile, preferred_element_type=jnp.float32))
            for n in range(UNROLL):
                total[rows_ref[UNROLL * at + n]] += terms[n]
            return 0

        lax.fori_loop(0, groups[k], step, 0)

    for e in range(N_SUB):
        for r in range(2):
            result = total[2 * e + r, :vecs]
            for part in range(1, parts):
                result = result + total[2 * e + r, part * vecs : (part + 1) * vecs]
            out_refs[e][:, pl.ds(r * BLOCK, BLOCK)] = result


def sweep(near, tiles):
    own = near[0]
    vecs = own.shape[0]
    smem = pl.BlockSpec(memory_space=pltpu.SMEM)
    vmem = pl.BlockSpec(memory_space=pltpu.VMEM)
    parts = 1 if own.dtype == jnp.bfloat16 else 2
    lists = [part for tile in tiles for part in tile[1:]]
    return pl.pallas_call(
        functools.partial(sweep_kernel, parts),
        in_specs=[smem] * 4 + [pl.BlockSpec(memory_space=pl.ANY)] * 2 + [vmem] * 5,
        out_specs=[vmem] * 4,
        out_shape=[jax.ShapeDtypeStruct((vecs, LENGTH), jnp.float32)] * 4,
        scratch_shapes=[
            pltpu.VMEM((14, parts * vecs, BLOCK), jnp.bfloat16),
            pltpu.VMEM((NOBODY + 1, parts * vecs, BLOCK), jnp.float32),
            pltpu.VMEM((GROUPS * UNROLL, BLOCK, BLOCK), jnp.bfloat16),
            pltpu.SemaphoreType.DMA((GROUPS,)),
        ],
        compiler_params=pltpu.CompilerParams(vmem_limit_bytes=SWEEP_LIMIT),
        cost_estimate=pl.CostEstimate(
            flops=50 * 2 * 128 * BLOCK * BLOCK, bytes_accessed=7 * 2**20, transcendentals=0
        ),
    )(*lists, *[tile[0] for tile in tiles], *near)


def exchanged(parts):
    return [parts[0]] + [shifted(parts[e], "sub", -e) for e in range(1, N_SUB)]


def gram_of(image):
    return lax.dot_general(
        image, image, TRANS_B, precision=lax.Precision.HIGHEST, preferred_element_type=jnp.float32
    )


def inverse_factor(gram):
    count = gram.shape[0]
    place = lax.broadcasted_iota(jnp.int32, (count, 1), 0)
    across = lax.broadcasted_iota(jnp.int32, (count, count), 1)
    identity = jnp.where(across == place, 1.0, 0.0)
    joined = jnp.concatenate([gram, identity], 1)
    for k in range(count):
        column = jnp.where(place > k, joined[:, k : k + 1], 0.0)
        joined = joined - column * (joined[k : k + 1, :] * (1.0 / joined[k : k + 1, k : k + 1]))
    pivots = jnp.sum(joined[:, :count] * identity, axis=1, keepdims=True)
    diagonal = jnp.sum(gram * identity, axis=1, keepdims=True)
    return joined[:, count:] / jnp.sqrt(pivots), jnp.min(pivots / diagonal)


def exact_dot(left, right):
    return jnp.dot(left, right, precision=lax.Precision.HIGHEST, preferred_element_type=jnp.float32)


def image_of(root_ref, part_refs):
    first, second, third, fourth = (part_ref[...] for part_ref in part_refs)
    return root_ref[...] * ((first + second) + (third + fourth))


def image_kernel(scaled, root_ref, *refs):
    image = image_of(root_ref, refs[:4])
    refs[4][...] = root_ref[...] * image if scaled else image
    refs[5][...] = gram_of(image)


def solve_gram_kernel(gram_ref, image_ref, solved_ref, next_ref):
    image = exact_dot(inverse_factor(gram_ref[...])[0], image_ref[...])
    solved_ref[...] = image
    next_ref[...] = gram_of(image)


def solve_kernel(gram_ref, image_ref, solved_ref):
    solved_ref[...] = exact_dot(inverse_factor(gram_ref[...])[0], image_ref[...])


def solve_both_kernel(grams_ref, image_ref, solved_ref, sound_ref):
    count = image_ref.shape[0]
    first, quality = inverse_factor(grams_ref[:count])
    half = lax.dot_general(
        grams_ref[count:], first, TRANS_B, precision=lax.Precision.HIGHEST,
        preferred_element_type=jnp.float32,
    )
    second, next_quality = inverse_factor(exact_dot(first, half))
    solved_ref[...] = exact_dot(second, exact_dot(first, image_ref[...]))
    sound_ref[0] = jnp.where((quality > 0.05) & (next_quality > 0.001), 1, 0)


def payload_kernel(pairs_ref, data_ref, scale_ref, payload_ref):
    n_space, n_sub = lax.axis_size("space"), lax.axis_size("sub")
    space_at, sub_at = lax.axis_index("space"), lax.axis_index("sub")
    lane = lax.broadcasted_iota(jnp.int32, (1, LENGTH), 1)
    used = jnp.zeros((1, LENGTH), jnp.float32)
    for k in range(pairs_ref.shape[0]):
        row, col = pairs_ref[k, 0], pairs_ref[k, 1]
        device = lax.shift_right_logical(col, 1)
        hop = lax.rem(lax.div(device, n_sub) - space_at + n_space, n_space)
        across = lax.rem(lax.rem(device, n_sub) - sub_at + n_sub, n_sub)
        place = (((hop - 1) * n_sub + across) * 2 + (row & 1)) * 2 + (col & 1)
        used = jnp.where((lane == place) & (hop > 0), 1.0, used)
    payload_ref[: ROWS - 16] = data_ref[: ROWS - 16]
    payload_ref[ROWS - 16 :] = jnp.concatenate(
        [
            data_ref[ROWS - 16 : FEAT].astype(jnp.float32),
            scale_ref[...].astype(jnp.float32),
            used,
            jnp.zeros((ROWS - MASK_ROW - 1, LENGTH), jnp.float32),
        ],
        0,
    ).astype(jnp.bfloat16)


def on_device(trajectories, kernel_scale, start_vectors, pair_list):
    vecs, length = start_vectors.shape
    light = dict(
        cost_estimate=pl.CostEstimate(flops=2**20, bytes_accessed=2**17, transcendentals=0),
        compiler_params=pltpu.CompilerParams(vmem_limit_bytes=SMALL_LIMIT),
    )

    payload = pl.pallas_call(
        payload_kernel,
        in_specs=[pl.BlockSpec(memory_space=pltpu.SMEM)] + [pl.BlockSpec(memory_space=pltpu.VMEM)] * 2,
        out_shape=jax.ShapeDtypeStruct((ROWS, length), jnp.bfloat16),
        **light,
    )(pair_list, trajectories, kernel_scale[None, :])

    members = [payload] + [shifted(payload, "sub", e) for e in range(1, N_SUB)]
    near = {h: shifted(payload, "space", h) for h in (2, -2)}
    later, near[2], near[-2] = lax.optimization_barrier((payload, near[2], near[-2]))
    for h, source in ((1, later), (-1, later), (3, near[2]), (-3, near[-2])):
        near[h] = shifted(source, "space", 1 if h > 0 else -1)
    blocks, rate = row_operands(members)
    listed = jnp.stack([member[MASK_ROW, : REACH * PAIRS] for member in members]).astype(jnp.int32)
    listed = listed.reshape(N_SUB * REACH * PAIRS)

    tiles = []
    carried = payload
    for at, hops in enumerate(HOPS):
        windows = [near[side * h] for h in hops for side in (1, -1)]
        *tile, carried = hop_tiles(
            hops, at == 0, at == len(HOPS) - 1, listed, blocks, rate, windows, carried
        )
        tiles.append(tile)
    degree = carried
    shares = exchanged([degree[e, :1] for e in range(N_SUB)])
    root = lax.rsqrt((shares[0] + shares[1]) + (shares[2] + shares[3]))

    vector_shape = jax.ShapeDtypeStruct((vecs, length), jnp.float32)
    gram_shape = jax.ShapeDtypeStruct((vecs, vecs), jnp.float32)
    def imaged(parts, scaled):
        return pl.pallas_call(
            functools.partial(image_kernel, scaled), out_shape=[vector_shape, gram_shape], **light
        )(root, *exchanged(parts))

    scaled = (root * start_vectors).astype(jnp.bfloat16)
    raw, first_gram = imaged(sweep(space_window(scaled), tiles), True)

    image, second_gram = imaged(sweep(space_window(raw), tiles), False)
    grams = summed(jnp.concatenate([first_gram, second_gram], 0))
    subspace, sound = pl.pallas_call(
        solve_both_kernel,
        in_specs=[pl.BlockSpec(memory_space=pltpu.VMEM)] * 2,
        out_specs=[pl.BlockSpec(memory_space=pltpu.VMEM), pl.BlockSpec(memory_space=pltpu.SMEM)],
        out_shape=[vector_shape, jax.ShapeDtypeStruct((1,), jnp.int32)],
        **light,
    )(grams, image)

    def directly():
        solved, gram = pl.pallas_call(
            solve_gram_kernel, out_shape=[vector_shape, gram_shape], **light
        )(grams[:vecs], image)
        return pl.pallas_call(solve_kernel, out_shape=vector_shape, **light)(summed(gram), solved)

    return lax.cond(sound[0] > 0, lambda: subspace, directly)


def solution(mesh):
    placed = (
        P(None, ("space", "sub")),
        P(("space", "sub")),
        P(None, ("space", "sub")),
        P(("space", "sub"), None),
    )
    return jax.shard_map(
        on_device, mesh=mesh, in_specs=placed, out_specs=P(None, ("space", "sub")), check_vma=False
    )
```

```python
import functools

import jax
import jax.numpy as jnp
from jax import lax
from jax.experimental import pallas as pl
from jax.experimental.pallas import tpu as pltpu
from jax.sharding import PartitionSpec as P

FEAT = 300
BLOCK = 256
LENGTH = 2 * BLOCK
REACH = 3
N_SUB = 4
ROWS = 304
DEPTH = 320
SCALE_ROW = 300
MASK_ROW = 301
PAIRS = 4 * N_SUB
SLOTS = 80
COUNT = SLOTS - 1
NOBODY = 2 * N_SUB
UNROLL = 8
AT_ONCE = 16
HALF = UNROLL // 2
HOPS = ((2,), (1, 3))
STARTS = (0, 5)
GROUPS = 13
LOG2E = 1.4426950408889634
VMEM_LIMIT = 24 * 1024 * 1024
SWEEP_LIMIT = 24 * 1024 * 1024
SMALL_LIMIT = 4 * 1024 * 1024
TRANS_B = (((1,), (1,)), ((), ()))


def shifted(value, axis, steps):
    count = lax.axis_size(axis)
    return lax.ppermute(value, axis, [((at + steps) % count, at) for at in range(count)])


def space_window(value):
    count = lax.axis_size("space")
    swap = [(at, at ^ 1) for at in range(count)]
    far = [(at, (at + (3 if at % 2 else -3)) % count) for at in range(count)]
    other, far, ahead, behind = lax.optimization_barrier(
        (
            lax.ppermute(value, "space", swap),
            lax.ppermute(value, "space", far),
            shifted(value, "space", 2),
            shifted(value, "space", -2),
        )
    )
    beside = jnp.stack([ahead, behind])
    return value, other, beside, lax.ppermute(beside, "space", swap), far


def window_slot(hop, side):
    odd = lax.rem(lax.axis_index("space"), 2) == 1
    even_slot, odd_slot = {(1, 0): (1, 3), (1, 1): (5, 1), (2, 0): (2, 2), (2, 1): (4, 4), (3, 0): (3, 6), (3, 1): (6, 5)}[hop, side]
    return jnp.where(odd, odd_slot, even_slot)


def groups_by(key, n_space, n_sub):
    found = {}
    for place in range(n_space * n_sub):
        found.setdefault(key(place // n_sub, place % n_sub), []).append(place)
    return list(found.values())


def summed(value):
    n_space, n_sub = lax.axis_size("space"), lax.axis_size("sub")
    shape = value.shape
    value = value.reshape(-1, 128)
    for key in (lambda s, y: (s // 8, 0), lambda s, y: (s % 8, y)):
        groups = groups_by(key, n_space, n_sub)
        sent = jnp.broadcast_to(value[None], (len(groups[0]),) + value.shape)
        value = jnp.sum(
            lax.all_to_all(sent, ("space", "sub"), 0, 0, axis_index_groups=groups), 0
        )
    return value.reshape(shape)


def pieces(norm):
    high = norm.astype(jnp.bfloat16).astype(jnp.float32)
    rest = norm - high
    middle = rest.astype(jnp.bfloat16).astype(jnp.float32)
    return high, middle, rest - middle


def ones_and_norms(norm, ones_at, norms_at):
    place = lax.broadcasted_iota(jnp.int32, (DEPTH - ROWS, 1), 0)
    tail = jnp.where((place >= ones_at) & (place < ones_at + 3), 1.0, 0.0)
    for k, piece in enumerate(pieces(norm)):
        tail = jnp.where(place == norms_at + k, -piece, tail)
    return tail


def rows_kernel(*refs):
    rows_ref, rate_ref = refs[N_SUB:]
    for e in range(N_SUB):
        wide = refs[e][:FEAT, :].astype(jnp.float32)
        tail = ones_and_norms(jnp.sum(wide * wide, axis=0, keepdims=True), 0, 3)
        tail = tail.astype(jnp.bfloat16)
        rate = LOG2E / refs[e][SCALE_ROW : SCALE_ROW + 1, :].astype(jnp.float32)
        below = lax.broadcasted_iota(jnp.int32, (ROWS, 1), 0) < FEAT
        twice = jnp.where(below, 2.0 * refs[e][...].astype(jnp.float32), 0.0).astype(jnp.bfloat16)
        for r in range(2):
            span = slice(r * BLOCK, (r + 1) * BLOCK)
            rows_ref[2 * e + r, :ROWS] = twice[:, span]
            rows_ref[2 * e + r, ROWS:] = tail[:, span]
            rate_ref[2 * e + r] = jnp.broadcast_to(rate[:, span], (8, BLOCK))


def row_operands(members):
    return pl.pallas_call(
        rows_kernel,
        out_shape=[
            jax.ShapeDtypeStruct((2 * N_SUB, DEPTH, BLOCK), jnp.bfloat16),
            jax.ShapeDtypeStruct((2 * N_SUB, 8, BLOCK), jnp.float32),
        ],
        compiler_params=pltpu.CompilerParams(vmem_limit_bytes=VMEM_LIMIT),
        cost_estimate=pl.CostEstimate(flops=2**22, bytes_accessed=4 * 2**20, transcendentals=0),
    )(*members)


def prepare_columns(data_ref, first, lhs, rate_ref):
    wide = data_ref[...].astype(jnp.float32)
    rate = 1.0 / wide[SCALE_ROW : SCALE_ROW + 1]
    squares = wide[:FEAT] * wide[:FEAT]
    tail = ones_and_norms(jnp.sum(squares, axis=0, keepdims=True), 3, 0)
    full = jnp.concatenate([wide, tail, jnp.zeros((384 - DEPTH, LENGTH), jnp.float32)], 0)
    turned = full.T[:, :DEPTH].astype(jnp.bfloat16)
    rate = jnp.broadcast_to(rate, (128, LENGTH)).T
    for c in range(2):
        lhs[first + c] = turned[c * BLOCK : (c + 1) * BLOCK]
        rate_ref[first + c] = rate[c * BLOCK : (c + 1) * BLOCK]


def list_pairs(hops, mine_ref, theirs, rows_ref, cols_ref, count):
    def member(e, count):
        for k, bits in enumerate(theirs):
            for side in range(2):
                for r in range(2):
                    for c in range(2):
                        if side == 0:
                            place = lax.rem(N_SUB - e, N_SUB) * 4 + r * 2 + c
                            used = mine_ref[(e * REACH + hops[k] - 1) * PAIRS + place]
                        else:
                            used = lax.shift_right_logical(bits, e * 4 + c * 2 + r) & 1
                        rows_ref[count] = e * 2 + r
                        cols_ref[count] = k * 4 + side * 2 + c
                        count = count + used
        return count

    count = lax.fori_loop(0, N_SUB, member, count)
    for k in range(UNROLL + HALF):
        rows_ref[count + k] = NOBODY
        cols_ref[count + k] = 0
    rows_ref[COUNT] = count
    cols_ref[COUNT] = count
    return count


def listed_behind(data_ref, hop):
    lane = lax.broadcasted_iota(jnp.int32, (1, 128), 1) - (hop - 1) * PAIRS
    weight = lax.shift_left(jnp.ones_like(lane), jnp.clip(lane, 0, PAIRS)).astype(jnp.float32)
    weight = jnp.where((lane >= 0) & (lane < PAIRS), weight, 0.0)
    used = data_ref[MASK_ROW : MASK_ROW + 1, :128].astype(jnp.float32)
    return jnp.sum(used * weight).astype(jnp.int32)


def tile_kernel(hops, first, last, mine_ref, blocks_ref, rate_ref, *refs):
    window_refs, extra_ref, refs = refs[: 2 * len(hops)], refs[2 * len(hops)], refs[2 * len(hops) + 1 :]
    tile_ref, rows_ref, cols_ref, sums_ref, lhs, col, even, odd, made, sems, *held = refs
    total = held[0] if last else sums_ref
    for k, window_ref in enumerate(window_refs):
        prepare_columns(window_ref, 2 * k, lhs, col)
    count = 0
    if first:
        prepare_columns(extra_ref, 4 * len(hops), lhs, col)
        for r in range(2):
            rows_ref[r] = r
            cols_ref[r] = 4 * len(hops) + r
        count = 2
        total[...] = jnp.zeros_like(total)
    else:
        total[...] = extra_ref[...]
    theirs = [listed_behind(window_refs[2 * k + 1], hop) for k, hop in enumerate(hops)]
    count = list_pairs(hops, mine_ref, theirs, rows_ref, cols_ref, jnp.int32(count))

    def products(buffer, base):
        for n in range(HALF):
            row = lax.min(rows_ref[base + n], NOBODY - 1)
            buffer[n] = jnp.dot(
                lhs[cols_ref[base + n]], blocks_ref[row], preferred_element_type=jnp.float32
            )

    def finish(buffer, base):
        for n in range(HALF):
            at = base + n
            row = rows_ref[at]
            rate = col[cols_ref[at]]
            rates = jnp.concatenate([rate, rate], 1) * rate_ref[lax.min(row, NOBODY - 1), :1, :]
            tile = jnp.exp2(buffer[n] * rates).astype(jnp.bfloat16)
            made[at] = tile
            total[row] += jnp.sum(tile.astype(jnp.float32).reshape(BLOCK // 8, 8, BLOCK), axis=0)

    def copy(group):
        span = pl.ds(group * UNROLL, UNROLL)
        return pltpu.make_async_copy(made.at[span], tile_ref.at[span], sems.at[group])

    products(even, 0)

    def step(group, _):
        products(odd, UNROLL * group + HALF)
        finish(even, UNROLL * group)
        products(even, UNROLL * group + UNROLL)
        finish(odd, UNROLL * group + HALF)
        copy(group).start()
        return 0

    groups = lax.div(count + (UNROLL - 1), UNROLL)
    lax.fori_loop(0, groups, step, 0)
    if last:
        for e in range(N_SUB):
            for r in range(2):
                sums = jnp.sum(total[2 * e + r], axis=0, keepdims=True)
                sums_ref[e, :, pl.ds(r * BLOCK, BLOCK)] = jnp.broadcast_to(sums, (8, BLOCK))

    def sent(group, _):
        copy(group).wait()
        return 0

    lax.fori_loop(0, groups, sent, 0)


def hop_tiles(hops, first, last, mine, blocks, rate, windows, extra):
    smem = pl.BlockSpec(memory_space=pltpu.SMEM)
    vmem = pl.BlockSpec(memory_space=pltpu.VMEM)
    columns = 4 * len(hops) + (2 if first else 0)
    slots = 2 * len(hops) * PAIRS + (UNROLL if first else 0)
    sums = (NOBODY + 1, 8, BLOCK)
    return pl.pallas_call(
        functools.partial(tile_kernel, hops, first, last),
        in_specs=[smem] + [vmem] * (3 + len(windows)),
        out_specs=[pl.BlockSpec(memory_space=pl.ANY), smem, smem, vmem],
        out_shape=[
            jax.ShapeDtypeStruct((slots, BLOCK, BLOCK), jnp.bfloat16),
            jax.ShapeDtypeStruct((SLOTS,), jnp.int32),
            jax.ShapeDtypeStruct((SLOTS,), jnp.int32),
            jax.ShapeDtypeStruct((N_SUB, 8, LENGTH) if last else sums, jnp.float32),
        ],
        scratch_shapes=[
            pltpu.VMEM((columns, BLOCK, DEPTH), jnp.bfloat16),
            pltpu.VMEM((columns, BLOCK, 128), jnp.float32),
            pltpu.VMEM((HALF, BLOCK, BLOCK), jnp.float32),
            pltpu.VMEM((HALF, BLOCK, BLOCK), jnp.float32),
            pltpu.VMEM((slots, BLOCK, BLOCK), jnp.bfloat16),
            pltpu.SemaphoreType.DMA((slots // UNROLL,)),
        ]
        + ([pltpu.VMEM(sums, jnp.float32)] if last else []),
        compiler_params=pltpu.CompilerParams(vmem_limit_bytes=VMEM_LIMIT),
        cost_estimate=pl.CostEstimate(
            flops=16 * len(hops) * 2 * DEPTH * BLOCK * BLOCK,
            bytes_accessed=7 * 2**20,
            transcendentals=16 * len(hops) * BLOCK * BLOCK,
        ),
    )(mine, blocks, rate, *windows, extra)


def stacked(vectors):
    if vectors.dtype == jnp.bfloat16:
        return vectors
    high = vectors.astype(jnp.bfloat16)
    return jnp.concatenate([high, (vectors - high.astype(jnp.float32)).astype(jnp.bfloat16)], 0)


def sweep_kernel(parts, *refs):
    list_refs, tile_refs, vector_refs = refs[:4], refs[4:6], refs[6:11]
    out_refs, (held, total, tiles, sems) = refs[11:15], refs[15:]
    vecs = vector_refs[0].shape[0]

    def copy(k, at):
        span = pl.ds(at * UNROLL, UNROLL)
        place = pl.ds((STARTS[k] + at) * UNROLL, UNROLL)
        return pltpu.make_async_copy(tile_refs[k].at[span], tiles.at[place], sems.at[STARTS[k] + at])

    groups = [lax.div(list_refs[2 * k][COUNT] + (UNROLL - 1), UNROLL) for k in range(len(HOPS))]
    for k in range(len(HOPS)):

        def fetch(at, _, k=k):
            copy(k, at).start()
            return 0

        lax.fori_loop(0, groups[k], fetch, 0)

    own, other, beside, swapped, far = vector_refs
    for k, vectors in enumerate(
        (own[...], other[...], beside[0], swapped[0], beside[1], swapped[1], far[...])
    ):
        both = stacked(vectors)
        for c in range(2):
            held[2 * k + c] = both[:, c * BLOCK : (c + 1) * BLOCK]
    total[...] = jnp.zeros_like(total)

    for k, hops in enumerate(HOPS):
        slots = [window_slot(hop, side) for hop in hops for side in range(2)]

        def step(at, _, k=k, slots=slots, rows_ref=list_refs[2 * k], cols_ref=list_refs[2 * k + 1]):
            copy(k, at).wait()
            terms = []
            for n in range(UNROLL):
                block = cols_ref[UNROLL * at + n]
                slot = 0
                for at_slot, found in enumerate(slots):
                    slot = jnp.where(lax.shift_right_logical(block, 1) == at_slot, found, slot)
                block = 2 * slot + (block & 1)
                tile = tiles[(STARTS[k] + at) * UNROLL + n]
                terms.append(jnp.dot(held[block], tile, preferred_element_type=jnp.float32))
            for n in range(UNROLL):
                total[rows_ref[UNROLL * at + n]] += terms[n]
            return 0

        lax.fori_loop(0, groups[k], step, 0)

    for e in range(N_SUB):
        for r in range(2):
            result = total[2 * e + r, :vecs]
            for part in range(1, parts):
                result = result + total[2 * e + r, part * vecs : (part + 1) * vecs]
            out_refs[e][:, pl.ds(r * BLOCK, BLOCK)] = result


def sweep(near, tiles):
    own = near[0]
    vecs = own.shape[0]
    smem = pl.BlockSpec(memory_space=pltpu.SMEM)
    vmem = pl.BlockSpec(memory_space=pltpu.VMEM)
    parts = 1 if own.dtype == jnp.bfloat16 else 2
    lists = [part for tile in tiles for part in tile[1:]]
    return pl.pallas_call(
        functools.partial(sweep_kernel, parts),
        in_specs=[smem] * 4 + [pl.BlockSpec(memory_space=pl.ANY)] * 2 + [vmem] * 5,
        out_specs=[vmem] * 4,
        out_shape=[jax.ShapeDtypeStruct((vecs, LENGTH), jnp.float32)] * 4,
        scratch_shapes=[
            pltpu.VMEM((14, parts * vecs, BLOCK), jnp.bfloat16),
            pltpu.VMEM((NOBODY + 1, parts * vecs, BLOCK), jnp.float32),
            pltpu.VMEM((GROUPS * UNROLL, BLOCK, BLOCK), jnp.bfloat16),
            pltpu.SemaphoreType.DMA((GROUPS,)),
        ],
        compiler_params=pltpu.CompilerParams(vmem_limit_bytes=SWEEP_LIMIT),
        cost_estimate=pl.CostEstimate(
            flops=50 * 2 * 128 * BLOCK * BLOCK, bytes_accessed=7 * 2**20, transcendentals=0
        ),
    )(*lists, *[tile[0] for tile in tiles], *near)


def exchanged(parts):
    return [parts[0]] + [shifted(parts[e], "sub", -e) for e in range(1, N_SUB)]


def gram_of(image):
    return lax.dot_general(
        image, image, TRANS_B, precision=lax.Precision.HIGHEST, preferred_element_type=jnp.float32
    )


def inverse_factor(gram):
    count = gram.shape[0]
    place = lax.broadcasted_iota(jnp.int32, (count, 1), 0)
    across = lax.broadcasted_iota(jnp.int32, (count, count), 1)
    identity = jnp.where(across == place, 1.0, 0.0)
    joined = jnp.concatenate([gram, identity], 1)
    for k in range(0, count, AT_ONCE):
        columns = [
            jnp.broadcast_to(joined[:, k + n : k + n + 1], joined.shape) for n in range(AT_ONCE)
        ]
        rows = [joined[k + n : k + n + 1, :] for n in range(AT_ONCE)]
        for n in range(AT_ONCE):
            at = slice(k + n, k + n + 1)
            factor = jnp.where(place > k + n, columns[n] * (1.0 / columns[n][at]), 0.0)
            for m in range(n + 1, AT_ONCE):
                columns[m] = columns[m] - factor * columns[m][at]
                rows[m] = rows[m] - factor[k + m : k + m + 1] * rows[n]
            joined = joined - factor * rows[n]
    pivots = jnp.sum(joined[:, :count] * identity, axis=1, keepdims=True)
    diagonal = jnp.sum(gram * identity, axis=1, keepdims=True)
    return joined[:, count:] / jnp.sqrt(pivots), jnp.min(pivots / diagonal)


def exact_dot(left, right):
    return jnp.dot(left, right, precision=lax.Precision.HIGHEST, preferred_element_type=jnp.float32)


def image_of(root_ref, part_refs):
    first, second, third, fourth = (part_ref[...] for part_ref in part_refs)
    return root_ref[...] * ((first + second) + (third + fourth))


def image_kernel(scaled, root_ref, *refs):
    image = image_of(root_ref, refs[:4])
    refs[4][...] = root_ref[...] * image if scaled else image
    refs[5][...] = gram_of(image)


def solve_gram_kernel(gram_ref, image_ref, solved_ref, next_ref):
    image = exact_dot(inverse_factor(gram_ref[...])[0], image_ref[...])
    solved_ref[...] = image
    next_ref[...] = gram_of(image)


def solve_kernel(gram_ref, image_ref, solved_ref):
    solved_ref[...] = exact_dot(inverse_factor(gram_ref[...])[0], image_ref[...])


def solve_both_kernel(grams_ref, image_ref, solved_ref, sound_ref):
    count = image_ref.shape[0]
    first, quality = inverse_factor(grams_ref[:count])
    half = lax.dot_general(
        grams_ref[count:], first, TRANS_B, precision=lax.Precision.HIGHEST,
        preferred_element_type=jnp.float32,
    )
    second, next_quality = inverse_factor(exact_dot(first, half))
    solved_ref[...] = exact_dot(second, exact_dot(first, image_ref[...]))
    sound_ref[0] = jnp.where((quality > 0.05) & (next_quality > 0.001), 1, 0)


def payload_kernel(pairs_ref, data_ref, scale_ref, payload_ref):
    n_space, n_sub = lax.axis_size("space"), lax.axis_size("sub")
    space_at, sub_at = lax.axis_index("space"), lax.axis_index("sub")
    lane = lax.broadcasted_iota(jnp.int32, (1, LENGTH), 1)
    used = jnp.zeros((1, LENGTH), jnp.float32)
    for k in range(pairs_ref.shape[1]):
        row, col = pairs_ref[0, k], pairs_ref[1, k]
        device = lax.shift_right_logical(col, 1)
        hop = lax.rem(lax.div(device, n_sub) - space_at + n_space, n_space)
        across = lax.rem(lax.rem(device, n_sub) - sub_at + n_sub, n_sub)
        place = (((hop - 1) * n_sub + across) * 2 + (row & 1)) * 2 + (col & 1)
        used = jnp.where((lane == place) & (hop > 0), 1.0, used)
    payload_ref[: ROWS - 16] = data_ref[: ROWS - 16]
    payload_ref[ROWS - 16 :] = jnp.concatenate(
        [
            data_ref[ROWS - 16 : FEAT].astype(jnp.float32),
            scale_ref[...].astype(jnp.float32).reshape(1, LENGTH),
            used,
            jnp.zeros((ROWS - MASK_ROW - 1, LENGTH), jnp.float32),
        ],
        0,
    ).astype(jnp.bfloat16)


def on_device(trajectories, kernel_scale, start_vectors, pair_list):
    vecs, length = start_vectors.shape
    light = dict(
        cost_estimate=pl.CostEstimate(flops=2**20, bytes_accessed=2**17, transcendentals=0),
        compiler_params=pltpu.CompilerParams(vmem_limit_bytes=SMALL_LIMIT),
    )

    payload = pl.pallas_call(
        payload_kernel,
        in_specs=[pl.BlockSpec(memory_space=pltpu.SMEM)] + [pl.BlockSpec(memory_space=pltpu.VMEM)] * 2,
        out_shape=jax.ShapeDtypeStruct((ROWS, length), jnp.bfloat16),
        **light,
    )(pair_list.T, trajectories, kernel_scale)

    members = [payload] + [shifted(payload, "sub", e) for e in range(1, N_SUB)]
    near = {h: shifted(payload, "space", h) for h in (2, -2)}
    later, near[2], near[-2] = lax.optimization_barrier((payload, near[2], near[-2]))
    for h, source in ((1, later), (-1, later), (3, near[2]), (-3, near[-2])):
        near[h] = shifted(source, "space", 1 if h > 0 else -1)
    blocks, rate = row_operands(members)
    listed = jnp.stack([member[MASK_ROW, : REACH * PAIRS] for member in members]).astype(jnp.int32)
    listed = listed.reshape(N_SUB * REACH * PAIRS)

    tiles = []
    carried = payload
    for at, hops in enumerate(HOPS):
        windows = [near[side * h] for h in hops for side in (1, -1)]
        *tile, carried = hop_tiles(
            hops, at == 0, at == len(HOPS) - 1, listed, blocks, rate, windows, carried
        )
        tiles.append(tile)
    degree = carried
    shares = exchanged([degree[e, :1] for e in range(N_SUB)])
    root = lax.rsqrt((shares[0] + shares[1]) + (shares[2] + shares[3]))

    vector_shape = jax.ShapeDtypeStruct((vecs, length), jnp.float32)
    gram_shape = jax.ShapeDtypeStruct((vecs, vecs), jnp.float32)
    def imaged(parts, scaled):
        return pl.pallas_call(
            functools.partial(image_kernel, scaled), out_shape=[vector_shape, gram_shape], **light
        )(root, *exchanged(parts))

    scaled = (root * start_vectors).astype(jnp.bfloat16)
    raw, first_gram = imaged(sweep(space_window(scaled), tiles), True)

    image, second_gram = imaged(sweep(space_window(raw), tiles), False)
    grams = summed(jnp.concatenate([first_gram, second_gram], 0))
    subspace, sound = pl.pallas_call(
        solve_both_kernel,
        in_specs=[pl.BlockSpec(memory_space=pltpu.VMEM)] * 2,
        out_specs=[pl.BlockSpec(memory_space=pltpu.VMEM), pl.BlockSpec(memory_space=pltpu.SMEM)],
        out_shape=[vector_shape, jax.ShapeDtypeStruct((1,), jnp.int32)],
        **light,
    )(grams, image)

    def directly():
        solved, gram = pl.pallas_call(
            solve_gram_kernel, out_shape=[vector_shape, gram_shape], **light
        )(grams[:vecs], image)
        return pl.pallas_call(solve_kernel, out_shape=vector_shape, **light)(summed(gram), solved)

    return lax.cond(sound[0] > 0, lambda: subspace, directly)


def solution(mesh):
    placed = (
        P(None, ("space", "sub")),
        P(("space", "sub")),
        P(None, ("space", "sub")),
        P(("space", "sub"), None),
    )
    return jax.shard_map(
        on_device, mesh=mesh, in_specs=placed, out_specs=P(None, ("space", "sub")), check_vma=False
    )
```

```python
import functools

import jax
import jax.numpy as jnp
from jax import lax
from jax.experimental import pallas as pl
from jax.experimental.pallas import tpu as pltpu
from jax.sharding import PartitionSpec as P

FEAT = 300
BLOCK = 256
LENGTH = 2 * BLOCK
REACH = 3
N_SUB = 4
ROWS = 304
DEPTH = 320
SCALE_ROW = 300
MASK_ROW = 301
PAIRS = 4 * N_SUB
SLOTS = 80
COUNT = SLOTS - 1
NOBODY = 2 * N_SUB
UNROLL = 8
AT_ONCE = 16
HALF = UNROLL // 2
HOPS = ((2,), (1, 3))
STARTS = (0, 5)
GROUPS = 13
LOG2E = 1.4426950408889634
VMEM_LIMIT = 24 * 1024 * 1024
SWEEP_LIMIT = 24 * 1024 * 1024
SMALL_LIMIT = 4 * 1024 * 1024
TRANS_B = (((1,), (1,)), ((), ()))


def shifted(value, axis, steps):
    count = lax.axis_size(axis)
    return lax.ppermute(value, axis, [((at + steps) % count, at) for at in range(count)])


def space_window(value):
    count = lax.axis_size("space")
    swap = [(at, at ^ 1) for at in range(count)]
    far = [(at, (at + (3 if at % 2 else -3)) % count) for at in range(count)]
    far, ahead, behind = lax.optimization_barrier(
        (
            lax.ppermute(value, "space", far),
            shifted(value, "space", 2),
            shifted(value, "space", -2),
        )
    )
    held = jnp.stack([value, ahead, behind])
    return held, lax.ppermute(held, "space", swap), far


def window_slot(hop, side):
    odd = lax.rem(lax.axis_index("space"), 2) == 1
    even_slot, odd_slot = {(1, 0): (1, 3), (1, 1): (5, 1), (2, 0): (2, 2), (2, 1): (4, 4), (3, 0): (3, 6), (3, 1): (6, 5)}[hop, side]
    return jnp.where(odd, odd_slot, even_slot)


def groups_by(key, n_space, n_sub):
    found = {}
    for place in range(n_space * n_sub):
        found.setdefault(key(place // n_sub, place % n_sub), []).append(place)
    return list(found.values())


def summed(value):
    n_space, n_sub = lax.axis_size("space"), lax.axis_size("sub")
    shape = value.shape
    value = value.reshape(-1, 128)
    for key in (lambda s, y: (s // 8, 0), lambda s, y: (s % 8, y)):
        groups = groups_by(key, n_space, n_sub)
        sent = jnp.broadcast_to(value[None], (len(groups[0]),) + value.shape)
        value = jnp.sum(
            lax.all_to_all(sent, ("space", "sub"), 0, 0, axis_index_groups=groups), 0
        )
    return value.reshape(shape)


def pieces(norm):
    high = norm.astype(jnp.bfloat16).astype(jnp.float32)
    rest = norm - high
    middle = rest.astype(jnp.bfloat16).astype(jnp.float32)
    return high, middle, rest - middle


def ones_and_norms(norm, ones_at, norms_at):
    place = lax.broadcasted_iota(jnp.int32, (DEPTH - ROWS, 1), 0)
    tail = jnp.where((place >= ones_at) & (place < ones_at + 3), 1.0, 0.0)
    for k, piece in enumerate(pieces(norm)):
        tail = jnp.where(place == norms_at + k, -piece, tail)
    return tail


def rows_kernel(*refs):
    rows_ref, rate_ref = refs[N_SUB:]
    for e in range(N_SUB):
        wide = refs[e][:FEAT, :].astype(jnp.float32)
        tail = ones_and_norms(jnp.sum(wide * wide, axis=0, keepdims=True), 0, 3)
        tail = tail.astype(jnp.bfloat16)
        rate = LOG2E / refs[e][SCALE_ROW : SCALE_ROW + 1, :].astype(jnp.float32)
        below = lax.broadcasted_iota(jnp.int32, (ROWS, 1), 0) < FEAT
        twice = jnp.where(below, 2.0 * refs[e][...].astype(jnp.float32), 0.0).astype(jnp.bfloat16)
        for r in range(2):
            span = slice(r * BLOCK, (r + 1) * BLOCK)
            rows_ref[2 * e + r, :ROWS] = twice[:, span]
            rows_ref[2 * e + r, ROWS:] = tail[:, span]
            rate_ref[2 * e + r] = jnp.broadcast_to(rate[:, span], (8, BLOCK))


def row_operands(members):
    return pl.pallas_call(
        rows_kernel,
        out_shape=[
            jax.ShapeDtypeStruct((2 * N_SUB, DEPTH, BLOCK), jnp.bfloat16),
            jax.ShapeDtypeStruct((2 * N_SUB, 8, BLOCK), jnp.float32),
        ],
        compiler_params=pltpu.CompilerParams(vmem_limit_bytes=VMEM_LIMIT),
        cost_estimate=pl.CostEstimate(flops=2**22, bytes_accessed=4 * 2**20, transcendentals=0),
    )(*members)


def prepare_columns(data_ref, first, lhs, rate_ref):
    wide = data_ref[...].astype(jnp.float32)
    rate = 1.0 / wide[SCALE_ROW : SCALE_ROW + 1]
    squares = wide[:FEAT] * wide[:FEAT]
    tail = ones_and_norms(jnp.sum(squares, axis=0, keepdims=True), 3, 0)
    full = jnp.concatenate([wide, tail, jnp.zeros((384 - DEPTH, LENGTH), jnp.float32)], 0)
    turned = full.T[:, :DEPTH].astype(jnp.bfloat16)
    rate = jnp.broadcast_to(rate, (128, LENGTH)).T
    for c in range(2):
        lhs[first + c] = turned[c * BLOCK : (c + 1) * BLOCK]
        rate_ref[first + c] = rate[c * BLOCK : (c + 1) * BLOCK]


def list_pairs(hops, mine_ref, theirs, rows_ref, cols_ref, count):
    def member(e, count):
        for k, bits in enumerate(theirs):
            for side in range(2):
                for r in range(2):
                    for c in range(2):
                        if side == 0:
                            place = lax.rem(N_SUB - e, N_SUB) * 4 + r * 2 + c
                            used = mine_ref[(e * REACH + hops[k] - 1) * PAIRS + place]
                        else:
                            used = lax.shift_right_logical(bits, e * 4 + c * 2 + r) & 1
                        rows_ref[count] = e * 2 + r
                        cols_ref[count] = k * 4 + side * 2 + c
                        count = count + used
        return count

    count = lax.fori_loop(0, N_SUB, member, count)
    for k in range(UNROLL + HALF):
        rows_ref[count + k] = NOBODY
        cols_ref[count + k] = 0
    rows_ref[COUNT] = count
    cols_ref[COUNT] = count
    return count


def listed_behind(data_ref, hop):
    lane = lax.broadcasted_iota(jnp.int32, (1, 128), 1) - (hop - 1) * PAIRS
    weight = lax.shift_left(jnp.ones_like(lane), jnp.clip(lane, 0, PAIRS)).astype(jnp.float32)
    weight = jnp.where((lane >= 0) & (lane < PAIRS), weight, 0.0)
    used = data_ref[MASK_ROW : MASK_ROW + 1, :128].astype(jnp.float32)
    return jnp.sum(used * weight).astype(jnp.int32)


def tile_kernel(hops, first, last, mine_ref, blocks_ref, rate_ref, *refs):
    window_refs, extra_ref, refs = refs[: 2 * len(hops)], refs[2 * len(hops)], refs[2 * len(hops) + 1 :]
    tile_ref, rows_ref, cols_ref, sums_ref, lhs, col, even, odd, made, sems, *held = refs
    total = held[0] if last else sums_ref
    for k, window_ref in enumerate(window_refs):
        prepare_columns(window_ref, 2 * k, lhs, col)
    count = 0
    if first:
        prepare_columns(extra_ref, 4 * len(hops), lhs, col)
        for r in range(2):
            rows_ref[r] = r
            cols_ref[r] = 4 * len(hops) + r
        count = 2
        total[...] = jnp.zeros_like(total)
    else:
        total[...] = extra_ref[...]
    theirs = [listed_behind(window_refs[2 * k + 1], hop) for k, hop in enumerate(hops)]
    count = list_pairs(hops, mine_ref, theirs, rows_ref, cols_ref, jnp.int32(count))

    def products(buffer, base):
        for n in range(HALF):
            row = lax.min(rows_ref[base + n], NOBODY - 1)
            buffer[n] = jnp.dot(
                lhs[cols_ref[base + n]], blocks_ref[row], preferred_element_type=jnp.float32
            )

    def finish(buffer, base):
        for n in range(HALF):
            at = base + n
            row = rows_ref[at]
            rate = col[cols_ref[at]]
            rates = jnp.concatenate([rate, rate], 1) * rate_ref[lax.min(row, NOBODY - 1), :1, :]
            tile = jnp.exp2(buffer[n] * rates).astype(jnp.bfloat16)
            made[at] = tile
            total[row] += jnp.sum(tile.astype(jnp.float32).reshape(BLOCK // 8, 8, BLOCK), axis=0)

    def copy(group):
        span = pl.ds(group * UNROLL, UNROLL)
        return pltpu.make_async_copy(made.at[span], tile_ref.at[span], sems.at[group])

    products(even, 0)

    def step(group, _):
        products(odd, UNROLL * group + HALF)
        finish(even, UNROLL * group)
        products(even, UNROLL * group + UNROLL)
        finish(odd, UNROLL * group + HALF)
        copy(group).start()
        return 0

    groups = lax.div(count + (UNROLL - 1), UNROLL)
    lax.fori_loop(0, groups, step, 0)
    if last:
        for e in range(N_SUB):
            for r in range(2):
                sums = jnp.sum(total[2 * e + r], axis=0, keepdims=True)
                sums_ref[e, :, pl.ds(r * BLOCK, BLOCK)] = jnp.broadcast_to(sums, (8, BLOCK))

    def sent(group, _):
        copy(group).wait()
        return 0

    lax.fori_loop(0, groups, sent, 0)


def hop_tiles(hops, first, last, mine, blocks, rate, windows, extra):
    smem = pl.BlockSpec(memory_space=pltpu.SMEM)
    vmem = pl.BlockSpec(memory_space=pltpu.VMEM)
    columns = 4 * len(hops) + (2 if first else 0)
    slots = 2 * len(hops) * PAIRS + (UNROLL if first else 0)
    sums = (NOBODY + 1, 8, BLOCK)
    return pl.pallas_call(
        functools.partial(tile_kernel, hops, first, last),
        in_specs=[smem] + [vmem] * (3 + len(windows)),
        out_specs=[pl.BlockSpec(memory_space=pl.ANY), smem, smem, vmem],
        out_shape=[
            jax.ShapeDtypeStruct((slots, BLOCK, BLOCK), jnp.bfloat16),
            jax.ShapeDtypeStruct((SLOTS,), jnp.int32),
            jax.ShapeDtypeStruct((SLOTS,), jnp.int32),
            jax.ShapeDtypeStruct((N_SUB, 8, LENGTH) if last else sums, jnp.float32),
        ],
        scratch_shapes=[
            pltpu.VMEM((columns, BLOCK, DEPTH), jnp.bfloat16),
            pltpu.VMEM((columns, BLOCK, 128), jnp.float32),
            pltpu.VMEM((HALF, BLOCK, BLOCK), jnp.float32),
            pltpu.VMEM((HALF, BLOCK, BLOCK), jnp.float32),
            pltpu.VMEM((slots, BLOCK, BLOCK), jnp.bfloat16),
            pltpu.SemaphoreType.DMA((slots // UNROLL,)),
        ]
        + ([pltpu.VMEM(sums, jnp.float32)] if last else []),
        compiler_params=pltpu.CompilerParams(vmem_limit_bytes=VMEM_LIMIT),
        cost_estimate=pl.CostEstimate(
            flops=16 * len(hops) * 2 * DEPTH * BLOCK * BLOCK,
            bytes_accessed=7 * 2**20,
            transcendentals=16 * len(hops) * BLOCK * BLOCK,
        ),
    )(mine, blocks, rate, *windows, extra)


def stacked(vectors):
    if vectors.dtype == jnp.bfloat16:
        return vectors
    high = vectors.astype(jnp.bfloat16)
    return jnp.concatenate([high, (vectors - high.astype(jnp.float32)).astype(jnp.bfloat16)], 0)


def sweep_kernel(parts, *refs):
    list_refs, tile_refs, vector_refs = refs[:4], refs[4:6], refs[6:9]
    out_refs, (held, total, tiles, sems) = refs[9:13], refs[13:]
    vecs = vector_refs[0].shape[1]

    def copy(k, at):
        span = pl.ds(at * UNROLL, UNROLL)
        place = pl.ds((STARTS[k] + at) * UNROLL, UNROLL)
        return pltpu.make_async_copy(tile_refs[k].at[span], tiles.at[place], sems.at[STARTS[k] + at])

    groups = [lax.div(list_refs[2 * k][COUNT] + (UNROLL - 1), UNROLL) for k in range(len(HOPS))]
    for k in range(len(HOPS)):

        def fetch(at, _, k=k):
            copy(k, at).start()
            return 0

        lax.fori_loop(0, groups[k], fetch, 0)

    here, there, far = vector_refs
    for k, vectors in enumerate(
        (here[0], there[0], here[1], there[1], here[2], there[2], far[...])
    ):
        both = stacked(vectors)
        for c in range(2):
            held[2 * k + c] = both[:, c * BLOCK : (c + 1) * BLOCK]
    total[...] = jnp.zeros_like(total)

    for k, hops in enumerate(HOPS):
        slots = [window_slot(hop, side) for hop in hops for side in range(2)]

        def step(at, _, k=k, slots=slots, rows_ref=list_refs[2 * k], cols_ref=list_refs[2 * k + 1]):
            copy(k, at).wait()
            terms = []
            for n in range(UNROLL):
                block = cols_ref[UNROLL * at + n]
                slot = 0
                for at_slot, found in enumerate(slots):
                    slot = jnp.where(lax.shift_right_logical(block, 1) == at_slot, found, slot)
                block = 2 * slot + (block & 1)
                tile = tiles[(STARTS[k] + at) * UNROLL + n]
                terms.append(jnp.dot(held[block], tile, preferred_element_type=jnp.float32))
            for n in range(UNROLL):
                total[rows_ref[UNROLL * at + n]] += terms[n]
            return 0

        lax.fori_loop(0, groups[k], step, 0)

    for e in range(N_SUB):
        for r in range(2):
            result = total[2 * e + r, :vecs]
            for part in range(1, parts):
                result = result + total[2 * e + r, part * vecs : (part + 1) * vecs]
            out_refs[e][:, pl.ds(r * BLOCK, BLOCK)] = result


def sweep(near, tiles):
    own = near[0]
    vecs = own.shape[1]
    smem = pl.BlockSpec(memory_space=pltpu.SMEM)
    vmem = pl.BlockSpec(memory_space=pltpu.VMEM)
    parts = 1 if own.dtype == jnp.bfloat16 else 2
    lists = [part for tile in tiles for part in tile[1:]]
    return pl.pallas_call(
        functools.partial(sweep_kernel, parts),
        in_specs=[smem] * 4 + [pl.BlockSpec(memory_space=pl.ANY)] * 2 + [vmem] * 3,
        out_specs=[vmem] * 4,
        out_shape=[jax.ShapeDtypeStruct((vecs, LENGTH), jnp.float32)] * 4,
        scratch_shapes=[
            pltpu.VMEM((14, parts * vecs, BLOCK), jnp.bfloat16),
            pltpu.VMEM((NOBODY + 1, parts * vecs, BLOCK), jnp.float32),
            pltpu.VMEM((GROUPS * UNROLL, BLOCK, BLOCK), jnp.bfloat16),
            pltpu.SemaphoreType.DMA((GROUPS,)),
        ],
        compiler_params=pltpu.CompilerParams(vmem_limit_bytes=SWEEP_LIMIT),
        cost_estimate=pl.CostEstimate(
            flops=50 * 2 * 128 * BLOCK * BLOCK, bytes_accessed=7 * 2**20, transcendentals=0
        ),
    )(*lists, *[tile[0] for tile in tiles], *near)


def exchanged(parts):
    return [parts[0]] + [shifted(parts[e], "sub", -e) for e in range(1, N_SUB)]


def gram_of(image):
    return lax.dot_general(
        image, image, TRANS_B, precision=lax.Precision.HIGHEST, preferred_element_type=jnp.float32
    )


def inverse_factor(gram):
    count = gram.shape[0]
    place = lax.broadcasted_iota(jnp.int32, (count, 1), 0)
    across = lax.broadcasted_iota(jnp.int32, (count, count), 1)
    identity = jnp.where(across == place, 1.0, 0.0)
    joined = jnp.concatenate([gram, identity], 1)
    for k in range(0, count, AT_ONCE):
        columns = [
            jnp.broadcast_to(joined[:, k + n : k + n + 1], joined.shape) for n in range(AT_ONCE)
        ]
        rows = [joined[k + n : k + n + 1, :] for n in range(AT_ONCE)]
        for n in range(AT_ONCE):
            at = slice(k + n, k + n + 1)
            factor = jnp.where(place > k + n, columns[n] * (1.0 / columns[n][at]), 0.0)
            for m in range(n + 1, AT_ONCE):
                columns[m] = columns[m] - factor * columns[m][at]
                rows[m] = rows[m] - factor[k + m : k + m + 1] * rows[n]
            joined = joined - factor * rows[n]
    pivots = jnp.sum(joined[:, :count] * identity, axis=1, keepdims=True)
    diagonal = jnp.sum(gram * identity, axis=1, keepdims=True)
    return joined[:, count:] / jnp.sqrt(pivots), jnp.min(pivots / diagonal)


def exact_dot(left, right):
    return jnp.dot(left, right, precision=lax.Precision.HIGHEST, preferred_element_type=jnp.float32)


def image_of(root_ref, part_refs):
    first, second, third, fourth = (part_ref[...] for part_ref in part_refs)
    return root_ref[...] * ((first + second) + (third + fourth))


def image_kernel(scaled, root_ref, *refs):
    image = image_of(root_ref, refs[:4])
    refs[4][...] = root_ref[...] * image if scaled else image
    refs[5][...] = gram_of(image)


def solve_gram_kernel(gram_ref, image_ref, solved_ref, next_ref):
    image = exact_dot(inverse_factor(gram_ref[...])[0], image_ref[...])
    solved_ref[...] = image
    next_ref[...] = gram_of(image)


def solve_kernel(gram_ref, image_ref, solved_ref):
    solved_ref[...] = exact_dot(inverse_factor(gram_ref[...])[0], image_ref[...])


def solve_both_kernel(grams_ref, image_ref, solved_ref, sound_ref):
    count = image_ref.shape[0]
    first, quality = inverse_factor(grams_ref[:count])
    half = lax.dot_general(
        grams_ref[count:], first, TRANS_B, precision=lax.Precision.HIGHEST,
        preferred_element_type=jnp.float32,
    )
    second, next_quality = inverse_factor(exact_dot(first, half))
    solved_ref[...] = exact_dot(second, exact_dot(first, image_ref[...]))
    sound_ref[0] = jnp.where((quality > 0.05) & (next_quality > 0.001), 1, 0)


def payload_kernel(pairs_ref, data_ref, scale_ref, payload_ref):
    n_space, n_sub = lax.axis_size("space"), lax.axis_size("sub")
    space_at, sub_at = lax.axis_index("space"), lax.axis_index("sub")
    lane = lax.broadcasted_iota(jnp.int32, (1, LENGTH), 1)
    used = jnp.zeros((1, LENGTH), jnp.float32)
    for k in range(pairs_ref.shape[1]):
        row, col = pairs_ref[0, k], pairs_ref[1, k]
        device = lax.shift_right_logical(col, 1)
        hop = lax.rem(lax.div(device, n_sub) - space_at + n_space, n_space)
        across = lax.rem(lax.rem(device, n_sub) - sub_at + n_sub, n_sub)
        place = (((hop - 1) * n_sub + across) * 2 + (row & 1)) * 2 + (col & 1)
        used = jnp.where((lane == place) & (hop > 0), 1.0, used)
    payload_ref[: ROWS - 16] = data_ref[: ROWS - 16]
    payload_ref[ROWS - 16 :] = jnp.concatenate(
        [
            data_ref[ROWS - 16 : FEAT].astype(jnp.float32),
            scale_ref[...].astype(jnp.float32).reshape(1, LENGTH),
            used,
            jnp.zeros((ROWS - MASK_ROW - 1, LENGTH), jnp.float32),
        ],
        0,
    ).astype(jnp.bfloat16)


def on_device(trajectories, kernel_scale, start_vectors, pair_list):
    vecs, length = start_vectors.shape
    light = dict(
        cost_estimate=pl.CostEstimate(flops=2**20, bytes_accessed=2**17, transcendentals=0),
        compiler_params=pltpu.CompilerParams(vmem_limit_bytes=SMALL_LIMIT),
    )

    payload = pl.pallas_call(
        payload_kernel,
        in_specs=[pl.BlockSpec(memory_space=pltpu.SMEM)] + [pl.BlockSpec(memory_space=pltpu.VMEM)] * 2,
        out_shape=jax.ShapeDtypeStruct((ROWS, length), jnp.bfloat16),
        **light,
    )(pair_list.T, trajectories, kernel_scale)

    members = [payload] + [shifted(payload, "sub", e) for e in range(1, N_SUB)]
    near = {h: shifted(payload, "space", h) for h in (2, -2)}
    later, near[2], near[-2] = lax.optimization_barrier((payload, near[2], near[-2]))
    for h, source in ((1, later), (-1, later), (3, near[2]), (-3, near[-2])):
        near[h] = shifted(source, "space", 1 if h > 0 else -1)
    blocks, rate = row_operands(members)
    listed = jnp.stack([member[MASK_ROW, : REACH * PAIRS] for member in members]).astype(jnp.int32)
    listed = listed.reshape(N_SUB * REACH * PAIRS)

    tiles = []
    carried = payload
    for at, hops in enumerate(HOPS):
        windows = [near[side * h] for h in hops for side in (1, -1)]
        *tile, carried = hop_tiles(
            hops, at == 0, at == len(HOPS) - 1, listed, blocks, rate, windows, carried
        )
        tiles.append(tile)
    degree = carried
    shares = exchanged([degree[e, :1] for e in range(N_SUB)])
    root = lax.rsqrt((shares[0] + shares[1]) + (shares[2] + shares[3]))

    vector_shape = jax.ShapeDtypeStruct((vecs, length), jnp.float32)
    gram_shape = jax.ShapeDtypeStruct((vecs, vecs), jnp.float32)
    def imaged(parts, scaled):
        return pl.pallas_call(
            functools.partial(image_kernel, scaled), out_shape=[vector_shape, gram_shape], **light
        )(root, *exchanged(parts))

    scaled = (root * start_vectors).astype(jnp.bfloat16)
    raw, first_gram = imaged(sweep(space_window(scaled), tiles), True)

    image, second_gram = imaged(sweep(space_window(raw), tiles), False)
    grams = summed(jnp.concatenate([first_gram, second_gram], 0))
    subspace, sound = pl.pallas_call(
        solve_both_kernel,
        in_specs=[pl.BlockSpec(memory_space=pltpu.VMEM)] * 2,
        out_specs=[pl.BlockSpec(memory_space=pltpu.VMEM), pl.BlockSpec(memory_space=pltpu.SMEM)],
        out_shape=[vector_shape, jax.ShapeDtypeStruct((1,), jnp.int32)],
        **light,
    )(grams, image)

    def directly():
        solved, gram = pl.pallas_call(
            solve_gram_kernel, out_shape=[vector_shape, gram_shape], **light
        )(grams[:vecs], image)
        return pl.pallas_call(solve_kernel, out_shape=vector_shape, **light)(summed(gram), solved)

    return lax.cond(sound[0] > 0, lambda: subspace, directly)


def solution(mesh):
    placed = (
        P(None, ("space", "sub")),
        P(("space", "sub")),
        P(None, ("space", "sub")),
        P(("space", "sub"), None),
    )
    return jax.shard_map(
        on_device, mesh=mesh, in_specs=placed, out_specs=P(None, ("space", "sub")), check_vma=False
    )
```

```python
import functools

import jax
import jax.numpy as jnp
from jax import lax
from jax.experimental import pallas as pl
from jax.experimental.pallas import tpu as pltpu
from jax.sharding import PartitionSpec as P

FEAT = 300
BLOCK = 256
LENGTH = 2 * BLOCK
REACH = 3
N_SUB = 4
ROWS = 304
DEPTH = 320
SCALE_ROW = 300
MASK_ROW = 301
PAIRS = 4 * N_SUB
SLOTS = 80
COUNT = SLOTS - 1
NOBODY = 2 * N_SUB
UNROLL = 8
AT_ONCE = 16
HALF = UNROLL // 2
WINDOWS = (((2, 2), (-2, -2)), ((1, -1), (3, 1), (-1, -3), (-3, 3)))
PLACES = ((2, 4, 0), (1, 3, 5, 6))
WIDE = 320
STARTS = (0, 5)
GROUPS = 13
LOG2E = 1.4426950408889634
VMEM_LIMIT = 24 * 1024 * 1024
SWEEP_LIMIT = 24 * 1024 * 1024
SMALL_LIMIT = 4 * 1024 * 1024
TRANS_B = (((1,), (1,)), ((), ()))


def shifted(value, axis, steps):
    count = lax.axis_size(axis)
    return lax.ppermute(value, axis, [((at + steps) % count, at) for at in range(count)])


def far_pairs(count):
    return [(at, (at + (3 if at % 2 else -3)) % count) for at in range(count)]


def swapped(value):
    return lax.ppermute(value, "space", [(at, at ^ 1) for at in range(lax.axis_size("space"))])


def space_window(value):
    far, ahead, behind = lax.optimization_barrier(
        (
            lax.ppermute(value, "space", far_pairs(lax.axis_size("space"))),
            shifted(value, "space", 2),
            shifted(value, "space", -2),
        )
    )
    here = jnp.stack([value, ahead, behind])
    return here, swapped(here), far


def groups_by(key, n_space, n_sub):
    found = {}
    for place in range(n_space * n_sub):
        found.setdefault(key(place // n_sub, place % n_sub), []).append(place)
    return list(found.values())


def summed(value):
    n_space, n_sub = lax.axis_size("space"), lax.axis_size("sub")
    shape = value.shape
    value = value.reshape(-1, 128)
    for key in (lambda s, y: (s // 8, 0), lambda s, y: (s % 8, y)):
        groups = groups_by(key, n_space, n_sub)
        sent = jnp.broadcast_to(value[None], (len(groups[0]),) + value.shape)
        value = jnp.sum(
            lax.all_to_all(sent, ("space", "sub"), 0, 0, axis_index_groups=groups), 0
        )
    return value.reshape(shape)


def pieces(norm):
    high = norm.astype(jnp.bfloat16).astype(jnp.float32)
    rest = norm - high
    middle = rest.astype(jnp.bfloat16).astype(jnp.float32)
    return high, middle, rest - middle


def ones_and_norms(norm, ones_at, norms_at):
    place = lax.broadcasted_iota(jnp.int32, (DEPTH - ROWS, 1), 0)
    tail = jnp.where((place >= ones_at) & (place < ones_at + 3), 1.0, 0.0)
    for k, piece in enumerate(pieces(norm)):
        tail = jnp.where(place == norms_at + k, -piece, tail)
    return tail


def rows_kernel(*refs):
    rows_ref, rate_ref = refs[N_SUB:]
    for e in range(N_SUB):
        wide = refs[e][:FEAT, :].astype(jnp.float32)
        tail = ones_and_norms(jnp.sum(wide * wide, axis=0, keepdims=True), 0, 3)
        tail = tail.astype(jnp.bfloat16)
        rate = LOG2E / refs[e][SCALE_ROW : SCALE_ROW + 1, :].astype(jnp.float32)
        below = lax.broadcasted_iota(jnp.int32, (ROWS, 1), 0) < FEAT
        twice = jnp.where(below, 2.0 * refs[e][:ROWS, :].astype(jnp.float32), 0.0).astype(jnp.bfloat16)
        for r in range(2):
            span = slice(r * BLOCK, (r + 1) * BLOCK)
            rows_ref[2 * e + r, :ROWS] = twice[:, span]
            rows_ref[2 * e + r, ROWS:] = tail[:, span]
            rate_ref[2 * e + r] = jnp.broadcast_to(rate[:, span], (8, BLOCK))


def row_operands(members):
    return pl.pallas_call(
        rows_kernel,
        out_shape=[
            jax.ShapeDtypeStruct((2 * N_SUB, DEPTH, BLOCK), jnp.bfloat16),
            jax.ShapeDtypeStruct((2 * N_SUB, 8, BLOCK), jnp.float32),
        ],
        compiler_params=pltpu.CompilerParams(vmem_limit_bytes=VMEM_LIMIT),
        cost_estimate=pl.CostEstimate(flops=2**22, bytes_accessed=4 * 2**20, transcendentals=0),
    )(*members)


def prepare_columns(data_ref, first, lhs, rate_ref):
    wide = data_ref[...].astype(jnp.float32)
    rate = 1.0 / wide[SCALE_ROW : SCALE_ROW + 1]
    squares = wide[:FEAT] * wide[:FEAT]
    tail = ones_and_norms(jnp.sum(squares, axis=0, keepdims=True), 3, 0)
    full = jnp.concatenate([wide, tail, jnp.zeros((384 - DEPTH, LENGTH), jnp.float32)], 0)
    turned = full.T[:, :DEPTH].astype(jnp.bfloat16)
    rate = jnp.broadcast_to(rate, (128, LENGTH)).T
    for c in range(2):
        lhs[first + c] = turned[c * BLOCK : (c + 1) * BLOCK]
        rate_ref[first + c] = rate[c * BLOCK : (c + 1) * BLOCK]


def list_pairs(hops, mine_ref, theirs, rows_ref, cols_ref, count):
    def member(e, count):
        for k, (hop, bits) in enumerate(zip(hops, theirs)):
            base = (e * REACH + lax.abs(hop) - 1) * PAIRS + lax.rem(N_SUB - e, N_SUB) * 4
            for r in range(2):
                for c in range(2):
                    behind = lax.shift_right_logical(bits, e * 4 + c * 2 + r) & 1
                    used = jnp.where(hop > 0, mine_ref[base + r * 2 + c], behind)
                    rows_ref[count] = e * 2 + r
                    cols_ref[count] = k * 2 + c
                    count = count + used
        return count

    count = lax.fori_loop(0, N_SUB, member, count)
    for k in range(UNROLL + HALF):
        rows_ref[count + k] = NOBODY
        cols_ref[count + k] = 0
    rows_ref[COUNT] = count
    cols_ref[COUNT] = count
    return count


def listed_behind(data_ref, hop):
    lane = lax.broadcasted_iota(jnp.int32, (1, 128), 1) - (lax.abs(hop) - 1) * PAIRS
    weight = lax.shift_left(jnp.ones_like(lane), jnp.clip(lane, 0, PAIRS)).astype(jnp.float32)
    weight = jnp.where((lane >= 0) & (lane < PAIRS), weight, 0.0)
    used = data_ref[MASK_ROW : MASK_ROW + 1, :128].astype(jnp.float32)
    return jnp.sum(used * weight).astype(jnp.int32)


def tile_kernel(windows, first, last, mine_ref, blocks_ref, rate_ref, *refs):
    ahead_ref, behind_ref, extra_ref, refs = *refs[:3], refs[3:]
    window_refs = [ahead_ref, behind_ref]
    if not first:
        window_refs = [ahead_ref.at[k] for k in range(3)] + [behind_ref]
    odd_place = lax.rem(lax.axis_index("space"), 2) == 1
    hops = [jnp.where(odd_place, odd_hop, even_hop) for even_hop, odd_hop in windows]
    tile_ref, rows_ref, cols_ref, sums_ref, lhs, col, even, odd, made, sems, *held = refs
    total = held[0] if last else sums_ref
    for k, window_ref in enumerate(window_refs):
        prepare_columns(window_ref, 2 * k, lhs, col)
    count = 0
    if first:
        prepare_columns(extra_ref, 2 * len(hops), lhs, col)
        for r in range(2):
            rows_ref[r] = r
            cols_ref[r] = 2 * len(hops) + r
        count = 2
        total[...] = jnp.zeros_like(total)
    else:
        total[...] = extra_ref[...]
    theirs = [listed_behind(ref, hop) for ref, hop in zip(window_refs, hops)]
    count = list_pairs(hops, mine_ref, theirs, rows_ref, cols_ref, jnp.int32(count))

    def products(buffer, base):
        for n in range(HALF):
            row = lax.min(rows_ref[base + n], NOBODY - 1)
            buffer[n] = jnp.dot(
                lhs[cols_ref[base + n]], blocks_ref[row], preferred_element_type=jnp.float32
            )

    def finish(buffer, base):
        for n in range(HALF):
            at = base + n
            row = rows_ref[at]
            rate = col[cols_ref[at]]
            rates = jnp.concatenate([rate, rate], 1) * rate_ref[lax.min(row, NOBODY - 1), :1, :]
            tile = jnp.exp2(buffer[n] * rates).astype(jnp.bfloat16)
            made[at] = tile
            total[row] += jnp.sum(tile.astype(jnp.float32).reshape(BLOCK // 8, 8, BLOCK), axis=0)

    def copy(group):
        span = pl.ds(group * UNROLL, UNROLL)
        return pltpu.make_async_copy(made.at[span], tile_ref.at[span], sems.at[group])

    products(even, 0)

    def step(group, _):
        products(odd, UNROLL * group + HALF)
        finish(even, UNROLL * group)
        products(even, UNROLL * group + UNROLL)
        finish(odd, UNROLL * group + HALF)
        copy(group).start()
        return 0

    groups = lax.div(count + (UNROLL - 1), UNROLL)
    lax.fori_loop(0, groups, step, 0)
    if last:
        for e in range(N_SUB):
            for r in range(2):
                sums = jnp.sum(total[2 * e + r], axis=0, keepdims=True)
                sums_ref[e, :, pl.ds(r * BLOCK, BLOCK)] = jnp.broadcast_to(sums, (8, BLOCK))

    def sent(group, _):
        copy(group).wait()
        return 0

    lax.fori_loop(0, groups, sent, 0)


def hop_tiles(windows, first, last, mine, blocks, rate, ahead, behind, extra):
    smem = pl.BlockSpec(memory_space=pltpu.SMEM)
    vmem = pl.BlockSpec(memory_space=pltpu.VMEM)
    columns = 2 * len(windows) + (2 if first else 0)
    slots = len(windows) * PAIRS + (UNROLL if first else 0)
    sums = (NOBODY + 1, 8, BLOCK)
    return pl.pallas_call(
        functools.partial(tile_kernel, windows, first, last),
        in_specs=[smem] + [vmem] * 5,
        out_specs=[pl.BlockSpec(memory_space=pl.ANY), smem, smem, vmem],
        out_shape=[
            jax.ShapeDtypeStruct((slots, BLOCK, BLOCK), jnp.bfloat16),
            jax.ShapeDtypeStruct((SLOTS,), jnp.int32),
            jax.ShapeDtypeStruct((SLOTS,), jnp.int32),
            jax.ShapeDtypeStruct((N_SUB, 8, LENGTH) if last else sums, jnp.float32),
        ],
        scratch_shapes=[
            pltpu.VMEM((columns, BLOCK, DEPTH), jnp.bfloat16),
            pltpu.VMEM((columns, BLOCK, 128), jnp.float32),
            pltpu.VMEM((HALF, BLOCK, BLOCK), jnp.float32),
            pltpu.VMEM((HALF, BLOCK, BLOCK), jnp.float32),
            pltpu.VMEM((slots, BLOCK, BLOCK), jnp.bfloat16),
            pltpu.SemaphoreType.DMA((slots // UNROLL,)),
        ]
        + ([pltpu.VMEM(sums, jnp.float32)] if last else []),
        compiler_params=pltpu.CompilerParams(vmem_limit_bytes=VMEM_LIMIT),
        cost_estimate=pl.CostEstimate(
            flops=8 * len(windows) * 2 * DEPTH * BLOCK * BLOCK,
            bytes_accessed=7 * 2**20,
            transcendentals=8 * len(windows) * BLOCK * BLOCK,
        ),
    )(mine, blocks, rate, ahead, behind, extra)


def stacked(vectors):
    if vectors.dtype == jnp.bfloat16:
        return vectors
    high = vectors.astype(jnp.bfloat16)
    return jnp.concatenate([high, (vectors - high.astype(jnp.float32)).astype(jnp.bfloat16)], 0)


def sweep_kernel(parts, *refs):
    list_refs, tile_refs, vector_refs = refs[:4], refs[4:6], refs[6:9]
    out_refs, (held, total, tiles, sems) = refs[9:13], refs[13:]
    vecs = vector_refs[0].shape[1]

    def copy(k, at):
        span = pl.ds(at * UNROLL, UNROLL)
        place = pl.ds((STARTS[k] + at) * UNROLL, UNROLL)
        return pltpu.make_async_copy(tile_refs[k].at[span], tiles.at[place], sems.at[STARTS[k] + at])

    groups = [lax.div(list_refs[2 * k][COUNT] + (UNROLL - 1), UNROLL) for k in range(len(WINDOWS))]
    for k in range(len(WINDOWS)):

        def fetch(at, _, k=k):
            copy(k, at).start()
            return 0

        lax.fori_loop(0, groups[k], fetch, 0)

    here, there, far = vector_refs
    for k, vectors in enumerate(
        (here[0], there[0], here[1], there[1], here[2], there[2], far[...])
    ):
        both = stacked(vectors)
        for c in range(2):
            held[2 * k + c] = both[:, c * BLOCK : (c + 1) * BLOCK]
    total[...] = jnp.zeros_like(total)

    for k, slots in enumerate(PLACES):

        def step(at, _, k=k, slots=slots, rows_ref=list_refs[2 * k], cols_ref=list_refs[2 * k + 1]):
            copy(k, at).wait()
            terms = []
            for n in range(UNROLL):
                block = cols_ref[UNROLL * at + n]
                slot = 0
                for at_slot, found in enumerate(slots):
                    slot = jnp.where(lax.shift_right_logical(block, 1) == at_slot, found, slot)
                block = 2 * slot + (block & 1)
                tile = tiles[(STARTS[k] + at) * UNROLL + n]
                terms.append(jnp.dot(held[block], tile, preferred_element_type=jnp.float32))
            for n in range(UNROLL):
                total[rows_ref[UNROLL * at + n]] += terms[n]
            return 0

        lax.fori_loop(0, groups[k], step, 0)

    for e in range(N_SUB):
        for r in range(2):
            result = total[2 * e + r, :vecs]
            for part in range(1, parts):
                result = result + total[2 * e + r, part * vecs : (part + 1) * vecs]
            out_refs[e][:, pl.ds(r * BLOCK, BLOCK)] = result


def sweep(near, tiles):
    own = near[0]
    vecs = own.shape[1]
    smem = pl.BlockSpec(memory_space=pltpu.SMEM)
    vmem = pl.BlockSpec(memory_space=pltpu.VMEM)
    parts = 1 if own.dtype == jnp.bfloat16 else 2
    lists = [part for tile in tiles for part in tile[1:]]
    return pl.pallas_call(
        functools.partial(sweep_kernel, parts),
        in_specs=[smem] * 4 + [pl.BlockSpec(memory_space=pl.ANY)] * 2 + [vmem] * 3,
        out_specs=[vmem] * 4,
        out_shape=[jax.ShapeDtypeStruct((vecs, LENGTH), jnp.float32)] * 4,
        scratch_shapes=[
            pltpu.VMEM((14, parts * vecs, BLOCK), jnp.bfloat16),
            pltpu.VMEM((NOBODY + 1, parts * vecs, BLOCK), jnp.float32),
            pltpu.VMEM((GROUPS * UNROLL, BLOCK, BLOCK), jnp.bfloat16),
            pltpu.SemaphoreType.DMA((GROUPS,)),
        ],
        compiler_params=pltpu.CompilerParams(vmem_limit_bytes=SWEEP_LIMIT),
        cost_estimate=pl.CostEstimate(
            flops=50 * 2 * 128 * BLOCK * BLOCK, bytes_accessed=7 * 2**20, transcendentals=0
        ),
    )(*lists, *[tile[0] for tile in tiles], *near)


def exchanged(parts):
    return [parts[0]] + [shifted(parts[e], "sub", -e) for e in range(1, N_SUB)]


def gram_of(image):
    return lax.dot_general(
        image, image, TRANS_B, precision=lax.Precision.HIGHEST, preferred_element_type=jnp.float32
    )


def inverse_factor(gram):
    count = gram.shape[0]
    place = lax.broadcasted_iota(jnp.int32, (count, 1), 0)
    across = lax.broadcasted_iota(jnp.int32, (count, count), 1)
    identity = jnp.where(across == place, 1.0, 0.0)
    joined = jnp.concatenate([gram, identity], 1)
    for k in range(0, count, AT_ONCE):
        columns = [
            jnp.broadcast_to(joined[:, k + n : k + n + 1], joined.shape) for n in range(AT_ONCE)
        ]
        rows = [joined[k + n : k + n + 1, :] for n in range(AT_ONCE)]
        for n in range(AT_ONCE):
            at = slice(k + n, k + n + 1)
            factor = jnp.where(place > k + n, columns[n] * (1.0 / columns[n][at]), 0.0)
            for m in range(n + 1, AT_ONCE):
                columns[m] = columns[m] - factor * columns[m][at]
                rows[m] = rows[m] - factor[k + m : k + m + 1] * rows[n]
            joined = joined - factor * rows[n]
    pivots = jnp.sum(joined[:, :count] * identity, axis=1, keepdims=True)
    diagonal = jnp.sum(gram * identity, axis=1, keepdims=True)
    return joined[:, count:] / jnp.sqrt(pivots), jnp.min(pivots / diagonal)


def exact_dot(left, right):
    return jnp.dot(left, right, precision=lax.Precision.HIGHEST, preferred_element_type=jnp.float32)


def image_of(root_ref, part_refs):
    first, second, third, fourth = (part_ref[...] for part_ref in part_refs)
    return root_ref[...] * ((first + second) + (third + fourth))


def image_kernel(scaled, root_ref, *refs):
    image = image_of(root_ref, refs[:4])
    refs[4][...] = root_ref[...] * image if scaled else image
    refs[5][...] = gram_of(image)


def solve_gram_kernel(gram_ref, image_ref, solved_ref, next_ref):
    image = exact_dot(inverse_factor(gram_ref[...])[0], image_ref[...])
    solved_ref[...] = image
    next_ref[...] = gram_of(image)


def solve_kernel(gram_ref, image_ref, solved_ref):
    solved_ref[...] = exact_dot(inverse_factor(gram_ref[...])[0], image_ref[...])


def solve_both_kernel(grams_ref, image_ref, solved_ref, sound_ref):
    count = image_ref.shape[0]
    first, quality = inverse_factor(grams_ref[:count])
    half = lax.dot_general(
        grams_ref[count:], first, TRANS_B, precision=lax.Precision.HIGHEST,
        preferred_element_type=jnp.float32,
    )
    second, next_quality = inverse_factor(exact_dot(first, half))
    solved_ref[...] = exact_dot(second, exact_dot(first, image_ref[...]))
    sound_ref[0] = jnp.where((quality > 0.05) & (next_quality > 0.001), 1, 0)


def payload_kernel(pairs_ref, data_ref, scale_ref, payload_ref, wide_ref):
    n_space, n_sub = lax.axis_size("space"), lax.axis_size("sub")
    space_at, sub_at = lax.axis_index("space"), lax.axis_index("sub")
    lane = lax.broadcasted_iota(jnp.int32, (1, LENGTH), 1)
    used = jnp.zeros((1, LENGTH), jnp.float32)
    for k in range(pairs_ref.shape[1]):
        row, col = pairs_ref[0, k], pairs_ref[1, k]
        device = lax.shift_right_logical(col, 1)
        hop = lax.rem(lax.div(device, n_sub) - space_at + n_space, n_space)
        across = lax.rem(lax.rem(device, n_sub) - sub_at + n_sub, n_sub)
        place = (((hop - 1) * n_sub + across) * 2 + (row & 1)) * 2 + (col & 1)
        used = jnp.where((lane == place) & (hop > 0), 1.0, used)
    payload_ref[: ROWS - 16] = data_ref[: ROWS - 16]
    wide_ref[: ROWS - 16] = data_ref[: ROWS - 16]
    last = jnp.concatenate(
        [
            data_ref[ROWS - 16 : FEAT].astype(jnp.float32),
            scale_ref[...].astype(jnp.float32).reshape(1, LENGTH),
            used,
            jnp.zeros((ROWS - MASK_ROW - 1, LENGTH), jnp.float32),
        ],
        0,
    ).astype(jnp.bfloat16)
    payload_ref[ROWS - 16 :] = last
    wide_ref[ROWS - 16 : ROWS] = last
    wide_ref[ROWS:] = jnp.zeros((WIDE - ROWS, LENGTH), jnp.bfloat16)


def on_device(trajectories, kernel_scale, start_vectors, pair_list):
    vecs, length = start_vectors.shape
    light = dict(
        cost_estimate=pl.CostEstimate(flops=2**20, bytes_accessed=2**17, transcendentals=0),
        compiler_params=pltpu.CompilerParams(vmem_limit_bytes=SMALL_LIMIT),
    )

    payload, wide = pl.pallas_call(
        payload_kernel,
        in_specs=[pl.BlockSpec(memory_space=pltpu.SMEM)] + [pl.BlockSpec(memory_space=pltpu.VMEM)] * 2,
        out_shape=[jax.ShapeDtypeStruct((rows, length), jnp.bfloat16) for rows in (ROWS, WIDE)],
        **light,
    )(pair_list.T, trajectories, kernel_scale)

    far = lax.ppermute(payload, "space", far_pairs(lax.axis_size("space")))
    ahead, behind = shifted(payload, "space", 2), shifted(payload, "space", -2)
    members = [shifted(wide, "sub", e) for e in range(1, N_SUB)]
    far, ahead, behind, *members = lax.optimization_barrier((far, ahead, behind, *members))
    members = [wide] + members
    there = swapped(jnp.stack([payload, ahead, behind]))
    blocks, rate = row_operands(members)
    listed = jnp.stack([member[MASK_ROW, : REACH * PAIRS] for member in members]).astype(jnp.int32)
    listed = listed.reshape(N_SUB * REACH * PAIRS)

    tiles = []
    carried = payload
    for at, sources in enumerate(((ahead, behind), (there, far))):
        *tile, carried = hop_tiles(
            WINDOWS[at], at == 0, at == len(WINDOWS) - 1, listed, blocks, rate, *sources, carried
        )
        tiles.append(tile)
    degree = carried
    shares = exchanged([degree[e, :1] for e in range(N_SUB)])
    root = lax.rsqrt((shares[0] + shares[1]) + (shares[2] + shares[3]))

    vector_shape = jax.ShapeDtypeStruct((vecs, length), jnp.float32)
    gram_shape = jax.ShapeDtypeStruct((vecs, vecs), jnp.float32)
    def imaged(parts, scaled):
        return pl.pallas_call(
            functools.partial(image_kernel, scaled), out_shape=[vector_shape, gram_shape], **light
        )(root, *exchanged(parts))

    scaled = (root * start_vectors).astype(jnp.bfloat16)
    raw, first_gram = imaged(sweep(space_window(scaled), tiles), True)

    image, second_gram = imaged(sweep(space_window(raw), tiles), False)
    grams = summed(jnp.concatenate([first_gram, second_gram], 0))
    subspace, sound = pl.pallas_call(
        solve_both_kernel,
        in_specs=[pl.BlockSpec(memory_space=pltpu.VMEM)] * 2,
        out_specs=[pl.BlockSpec(memory_space=pltpu.VMEM), pl.BlockSpec(memory_space=pltpu.SMEM)],
        out_shape=[vector_shape, jax.ShapeDtypeStruct((1,), jnp.int32)],
        **light,
    )(grams, image)

    def directly():
        solved, gram = pl.pallas_call(
            solve_gram_kernel, out_shape=[vector_shape, gram_shape], **light
        )(grams[:vecs], image)
        return pl.pallas_call(solve_kernel, out_shape=vector_shape, **light)(summed(gram), solved)

    return lax.cond(sound[0] > 0, lambda: subspace, directly)


def solution(mesh):
    placed = (
        P(None, ("space", "sub")),
        P(("space", "sub")),
        P(None, ("space", "sub")),
        P(("space", "sub"), None),
    )
    return jax.shard_map(
        on_device, mesh=mesh, in_specs=placed, out_specs=P(None, ("space", "sub")), check_vma=False
    )
```

```python
import functools

import jax
import jax.numpy as jnp
from jax import lax
from jax.experimental import pallas as pl
from jax.experimental.pallas import tpu as pltpu
from jax.sharding import PartitionSpec as P

FEAT = 300
BLOCK = 256
LENGTH = 2 * BLOCK
REACH = 3
N_SUB = 4
ROWS = 304
DEPTH = 320
SCALE_ROW = 300
MASK_ROW = 301
PAIRS = 4 * N_SUB
SLOTS = 80
COUNT = SLOTS - 1
NOBODY = 2 * N_SUB
UNROLL = 8
AT_ONCE = 16
HALF = UNROLL // 2
WINDOWS = (((2, 2), (-2, -2)), ((1, -1), (3, 1), (-1, -3), (-3, 3)))
PLACES = ((2, 4, 0), (1, 3, 5, 6))
WIDE = 320
STARTS = (0, 5)
GROUPS = 13
LOG2E = 1.4426950408889634
VMEM_LIMIT = 24 * 1024 * 1024
SWEEP_LIMIT = 24 * 1024 * 1024
SMALL_LIMIT = 4 * 1024 * 1024
TRANS_B = (((1,), (1,)), ((), ()))


def shifted(value, axis, steps):
    count = lax.axis_size(axis)
    return lax.ppermute(value, axis, [((at + steps) % count, at) for at in range(count)])


def far_pairs(count):
    return [(at, (at + (3 if at % 2 else -3)) % count) for at in range(count)]


def swapped(value):
    return lax.ppermute(value, "space", [(at, at ^ 1) for at in range(lax.axis_size("space"))])


def space_window(value):
    far, ahead, behind = lax.optimization_barrier(
        (
            lax.ppermute(value, "space", far_pairs(lax.axis_size("space"))),
            shifted(value, "space", 2),
            shifted(value, "space", -2),
        )
    )
    here = jnp.stack([value, ahead, behind])
    return here, swapped(here), far


def groups_by(key, n_space, n_sub):
    found = {}
    for place in range(n_space * n_sub):
        found.setdefault(key(place // n_sub, place % n_sub), []).append(place)
    return list(found.values())


def summed(value):
    n_space, n_sub = lax.axis_size("space"), lax.axis_size("sub")
    shape = value.shape
    value = value.reshape(-1, 128)
    for key in (lambda s, y: (s // 8, 0), lambda s, y: (s % 8, y)):
        groups = groups_by(key, n_space, n_sub)
        sent = jnp.broadcast_to(value[None], (len(groups[0]),) + value.shape)
        value = jnp.sum(
            lax.all_to_all(sent, ("space", "sub"), 0, 0, axis_index_groups=groups), 0
        )
    return value.reshape(shape)


def pieces(norm):
    high = norm.astype(jnp.bfloat16).astype(jnp.float32)
    rest = norm - high
    middle = rest.astype(jnp.bfloat16).astype(jnp.float32)
    return high, middle, rest - middle


def ones_and_norms(norm, ones_at, norms_at):
    place = lax.broadcasted_iota(jnp.int32, (DEPTH - ROWS, 1), 0)
    tail = jnp.where((place >= ones_at) & (place < ones_at + 3), 1.0, 0.0)
    for k, piece in enumerate(pieces(norm)):
        tail = jnp.where(place == norms_at + k, -piece, tail)
    return tail


def rows_kernel(*refs):
    rows_ref, rate_ref = refs[N_SUB:]
    for e in range(N_SUB):
        wide = refs[e][:FEAT, :].astype(jnp.float32)
        tail = ones_and_norms(jnp.sum(wide * wide, axis=0, keepdims=True), 0, 3)
        tail = tail.astype(jnp.bfloat16)
        rate = LOG2E / refs[e][SCALE_ROW : SCALE_ROW + 1, :].astype(jnp.float32)
        below = lax.broadcasted_iota(jnp.int32, (ROWS, 1), 0) < FEAT
        twice = jnp.where(below, 2.0 * refs[e][:ROWS, :].astype(jnp.float32), 0.0).astype(jnp.bfloat16)
        for r in range(2):
            span = slice(r * BLOCK, (r + 1) * BLOCK)
            rows_ref[2 * e + r, :ROWS] = twice[:, span]
            rows_ref[2 * e + r, ROWS:] = tail[:, span]
            rate_ref[2 * e + r] = jnp.broadcast_to(rate[:, span], (8, BLOCK))


def row_operands(members):
    return pl.pallas_call(
        rows_kernel,
        out_shape=[
            jax.ShapeDtypeStruct((2 * N_SUB, DEPTH, BLOCK), jnp.bfloat16),
            jax.ShapeDtypeStruct((2 * N_SUB, 8, BLOCK), jnp.float32),
        ],
        compiler_params=pltpu.CompilerParams(vmem_limit_bytes=VMEM_LIMIT),
        cost_estimate=pl.CostEstimate(flops=2**22, bytes_accessed=4 * 2**20, transcendentals=0),
    )(*members)


def prepare_columns(data_ref, first, lhs, rate_ref):
    wide = data_ref[...].astype(jnp.float32)
    rate = 1.0 / wide[SCALE_ROW : SCALE_ROW + 1]
    squares = wide[:FEAT] * wide[:FEAT]
    tail = ones_and_norms(jnp.sum(squares, axis=0, keepdims=True), 3, 0)
    full = jnp.concatenate([wide, tail, jnp.zeros((384 - DEPTH, LENGTH), jnp.float32)], 0)
    turned = full.T[:, :DEPTH].astype(jnp.bfloat16)
    rate = jnp.broadcast_to(rate, (128, LENGTH)).T
    for c in range(2):
        lhs[first + c] = turned[c * BLOCK : (c + 1) * BLOCK]
        rate_ref[first + c] = rate[c * BLOCK : (c + 1) * BLOCK]


def list_pairs(hops, mine_ref, theirs, rows_ref, cols_ref, count):
    def member(e, count):
        for k, (hop, bits) in enumerate(zip(hops, theirs)):
            base = (e * REACH + lax.abs(hop) - 1) * PAIRS + lax.rem(N_SUB - e, N_SUB) * 4
            for r in range(2):
                for c in range(2):
                    behind = lax.shift_right_logical(bits, e * 4 + c * 2 + r) & 1
                    used = jnp.where(hop > 0, mine_ref[base + r * 2 + c], behind)
                    rows_ref[count] = e * 2 + r
                    cols_ref[count] = k * 2 + c
                    count = count + used
        return count

    count = lax.fori_loop(0, N_SUB, member, count)
    for k in range(UNROLL + HALF):
        rows_ref[count + k] = NOBODY
        cols_ref[count + k] = 0
    rows_ref[COUNT] = count
    cols_ref[COUNT] = count
    return count


def listed_behind(data_ref, hop):
    lane = lax.broadcasted_iota(jnp.int32, (1, 128), 1) - (lax.abs(hop) - 1) * PAIRS
    weight = lax.shift_left(jnp.ones_like(lane), jnp.clip(lane, 0, PAIRS)).astype(jnp.float32)
    weight = jnp.where((lane >= 0) & (lane < PAIRS), weight, 0.0)
    used = data_ref[MASK_ROW : MASK_ROW + 1, :128].astype(jnp.float32)
    return jnp.sum(used * weight).astype(jnp.int32)


def tile_kernel(windows, first, last, mine_ref, blocks_ref, rate_ref, *refs):
    window_refs, extra_ref, refs = refs[: len(windows)], refs[len(windows)], refs[len(windows) + 1 :]
    odd_place = lax.rem(lax.axis_index("space"), 2) == 1
    hops = [jnp.where(odd_place, odd_hop, even_hop) for even_hop, odd_hop in windows]
    tile_ref, rows_ref, cols_ref, sums_ref, lhs, col, even, odd, made, sems, *held = refs
    total = held[0] if last else sums_ref
    for k, window_ref in enumerate(window_refs):
        prepare_columns(window_ref, 2 * k, lhs, col)
    count = 0
    if first:
        prepare_columns(extra_ref, 2 * len(hops), lhs, col)
        for r in range(2):
            rows_ref[r] = r
            cols_ref[r] = 2 * len(hops) + r
        count = 2
        total[...] = jnp.zeros_like(total)
    else:
        total[...] = extra_ref[...]
    theirs = [listed_behind(ref, hop) for ref, hop in zip(window_refs, hops)]
    count = list_pairs(hops, mine_ref, theirs, rows_ref, cols_ref, jnp.int32(count))

    def products(buffer, base):
        for n in range(HALF):
            row = lax.min(rows_ref[base + n], NOBODY - 1)
            buffer[n] = jnp.dot(
                lhs[cols_ref[base + n]], blocks_ref[row], preferred_element_type=jnp.float32
            )

    def finish(buffer, base):
        for n in range(HALF):
            at = base + n
            row = rows_ref[at]
            rate = col[cols_ref[at]]
            rates = jnp.concatenate([rate, rate], 1) * rate_ref[lax.min(row, NOBODY - 1), :1, :]
            tile = jnp.exp2(buffer[n] * rates).astype(jnp.bfloat16)
            made[at] = tile
            total[row] += jnp.sum(tile.astype(jnp.float32).reshape(BLOCK // 8, 8, BLOCK), axis=0)

    def copy(group):
        span = pl.ds(group * UNROLL, UNROLL)
        return pltpu.make_async_copy(made.at[span], tile_ref.at[span], sems.at[group])

    products(even, 0)

    def step(group, _):
        products(odd, UNROLL * group + HALF)
        finish(even, UNROLL * group)
        products(even, UNROLL * group + UNROLL)
        finish(odd, UNROLL * group + HALF)
        copy(group).start()
        return 0

    groups = lax.div(count + (UNROLL - 1), UNROLL)
    lax.fori_loop(0, groups, step, 0)
    if last:
        for e in range(N_SUB):
            for r in range(2):
                sums = jnp.sum(total[2 * e + r], axis=0, keepdims=True)
                sums_ref[e, :, pl.ds(r * BLOCK, BLOCK)] = jnp.broadcast_to(sums, (8, BLOCK))

    def sent(group, _):
        copy(group).wait()
        return 0

    lax.fori_loop(0, groups, sent, 0)


def hop_tiles(windows, first, last, mine, blocks, rate, sources, extra):
    smem = pl.BlockSpec(memory_space=pltpu.SMEM)
    vmem = pl.BlockSpec(memory_space=pltpu.VMEM)
    columns = 2 * len(windows) + (2 if first else 0)
    slots = len(windows) * PAIRS + (UNROLL if first else 0)
    sums = (NOBODY + 1, 8, BLOCK)
    return pl.pallas_call(
        functools.partial(tile_kernel, windows, first, last),
        in_specs=[smem] + [vmem] * (3 + len(sources)),
        out_specs=[pl.BlockSpec(memory_space=pl.ANY), smem, smem, vmem],
        out_shape=[
            jax.ShapeDtypeStruct((slots, BLOCK, BLOCK), jnp.bfloat16),
            jax.ShapeDtypeStruct((SLOTS,), jnp.int32),
            jax.ShapeDtypeStruct((SLOTS,), jnp.int32),
            jax.ShapeDtypeStruct((N_SUB, 8, LENGTH) if last else sums, jnp.float32),
        ],
        scratch_shapes=[
            pltpu.VMEM((columns, BLOCK, DEPTH), jnp.bfloat16),
            pltpu.VMEM((columns, BLOCK, 128), jnp.float32),
            pltpu.VMEM((HALF, BLOCK, BLOCK), jnp.float32),
            pltpu.VMEM((HALF, BLOCK, BLOCK), jnp.float32),
            pltpu.VMEM((slots, BLOCK, BLOCK), jnp.bfloat16),
            pltpu.SemaphoreType.DMA((slots // UNROLL,)),
        ]
        + ([pltpu.VMEM(sums, jnp.float32)] if last else []),
        compiler_params=pltpu.CompilerParams(vmem_limit_bytes=VMEM_LIMIT),
        cost_estimate=pl.CostEstimate(
            flops=8 * len(windows) * 2 * DEPTH * BLOCK * BLOCK,
            bytes_accessed=7 * 2**20,
            transcendentals=8 * len(windows) * BLOCK * BLOCK,
        ),
    )(mine, blocks, rate, *sources, extra)


def stacked(vectors):
    if vectors.dtype == jnp.bfloat16:
        return vectors
    high = vectors.astype(jnp.bfloat16)
    return jnp.concatenate([high, (vectors - high.astype(jnp.float32)).astype(jnp.bfloat16)], 0)


def sweep_kernel(parts, *refs):
    list_refs, tile_refs, vector_refs = refs[:4], refs[4:6], refs[6:9]
    out_refs, (held, total, tiles, sems) = refs[9:13], refs[13:]
    vecs = vector_refs[0].shape[1]

    def copy(k, at):
        span = pl.ds(at * UNROLL, UNROLL)
        place = pl.ds((STARTS[k] + at) * UNROLL, UNROLL)
        return pltpu.make_async_copy(tile_refs[k].at[span], tiles.at[place], sems.at[STARTS[k] + at])

    groups = [lax.div(list_refs[2 * k][COUNT] + (UNROLL - 1), UNROLL) for k in range(len(WINDOWS))]
    for k in range(len(WINDOWS)):

        def fetch(at, _, k=k):
            copy(k, at).start()
            return 0

        lax.fori_loop(0, groups[k], fetch, 0)

    here, there, far = vector_refs
    for k, vectors in enumerate(
        (here[0], there[0], here[1], there[1], here[2], there[2], far[...])
    ):
        both = stacked(vectors)
        for c in range(2):
            held[2 * k + c] = both[:, c * BLOCK : (c + 1) * BLOCK]
    total[...] = jnp.zeros_like(total)

    for k, slots in enumerate(PLACES):

        def step(at, _, k=k, slots=slots, rows_ref=list_refs[2 * k], cols_ref=list_refs[2 * k + 1]):
            copy(k, at).wait()
            terms = []
            for n in range(UNROLL):
                block = cols_ref[UNROLL * at + n]
                slot = 0
                for at_slot, found in enumerate(slots):
                    slot = jnp.where(lax.shift_right_logical(block, 1) == at_slot, found, slot)
                block = 2 * slot + (block & 1)
                tile = tiles[(STARTS[k] + at) * UNROLL + n]
                terms.append(jnp.dot(held[block], tile, preferred_element_type=jnp.float32))
            for n in range(UNROLL):
                total[rows_ref[UNROLL * at + n]] += terms[n]
            return 0

        lax.fori_loop(0, groups[k], step, 0)

    for e in range(N_SUB):
        for r in range(2):
            result = total[2 * e + r, :vecs]
            for part in range(1, parts):
                result = result + total[2 * e + r, part * vecs : (part + 1) * vecs]
            out_refs[e][:, pl.ds(r * BLOCK, BLOCK)] = result


def sweep(near, tiles):
    own = near[0]
    vecs = own.shape[1]
    smem = pl.BlockSpec(memory_space=pltpu.SMEM)
    vmem = pl.BlockSpec(memory_space=pltpu.VMEM)
    parts = 1 if own.dtype == jnp.bfloat16 else 2
    lists = [part for tile in tiles for part in tile[1:]]
    return pl.pallas_call(
        functools.partial(sweep_kernel, parts),
        in_specs=[smem] * 4 + [pl.BlockSpec(memory_space=pl.ANY)] * 2 + [vmem] * 3,
        out_specs=[vmem] * 4,
        out_shape=[jax.ShapeDtypeStruct((vecs, LENGTH), jnp.float32)] * 4,
        scratch_shapes=[
            pltpu.VMEM((14, parts * vecs, BLOCK), jnp.bfloat16),
            pltpu.VMEM((NOBODY + 1, parts * vecs, BLOCK), jnp.float32),
            pltpu.VMEM((GROUPS * UNROLL, BLOCK, BLOCK), jnp.bfloat16),
            pltpu.SemaphoreType.DMA((GROUPS,)),
        ],
        compiler_params=pltpu.CompilerParams(vmem_limit_bytes=SWEEP_LIMIT),
        cost_estimate=pl.CostEstimate(
            flops=50 * 2 * 128 * BLOCK * BLOCK, bytes_accessed=7 * 2**20, transcendentals=0
        ),
    )(*lists, *[tile[0] for tile in tiles], *near)


def exchanged(parts):
    return [parts[0]] + [shifted(parts[e], "sub", -e) for e in range(1, N_SUB)]


def gram_of(image):
    return lax.dot_general(
        image, image, TRANS_B, precision=lax.Precision.HIGHEST, preferred_element_type=jnp.float32
    )


def inverse_factor(gram):
    count = gram.shape[0]
    place = lax.broadcasted_iota(jnp.int32, (count, 1), 0)
    across = lax.broadcasted_iota(jnp.int32, (count, count), 1)
    identity = jnp.where(across == place, 1.0, 0.0)
    joined = jnp.concatenate([gram, identity], 1)
    for k in range(0, count, AT_ONCE):
        columns = [
            jnp.broadcast_to(joined[:, k + n : k + n + 1], joined.shape) for n in range(AT_ONCE)
        ]
        rows = [joined[k + n : k + n + 1, :] for n in range(AT_ONCE)]
        for n in range(AT_ONCE):
            at = slice(k + n, k + n + 1)
            factor = jnp.where(place > k + n, columns[n] * (1.0 / columns[n][at]), 0.0)
            for m in range(n + 1, AT_ONCE):
                columns[m] = columns[m] - factor * columns[m][at]
                rows[m] = rows[m] - factor[k + m : k + m + 1] * rows[n]
            joined = joined - factor * rows[n]
    pivots = jnp.sum(joined[:, :count] * identity, axis=1, keepdims=True)
    diagonal = jnp.sum(gram * identity, axis=1, keepdims=True)
    return joined[:, count:] / jnp.sqrt(pivots), jnp.min(pivots / diagonal)


def exact_dot(left, right):
    return jnp.dot(left, right, precision=lax.Precision.HIGHEST, preferred_element_type=jnp.float32)


def image_of(root_ref, part_refs):
    first, second, third, fourth = (part_ref[...] for part_ref in part_refs)
    return root_ref[...] * ((first + second) + (third + fourth))


def image_kernel(scaled, root_ref, *refs):
    image = image_of(root_ref, refs[:4])
    refs[4][...] = root_ref[...] * image if scaled else image
    refs[5][...] = gram_of(image)


def solve_gram_kernel(gram_ref, image_ref, solved_ref, next_ref):
    image = exact_dot(inverse_factor(gram_ref[...])[0], image_ref[...])
    solved_ref[...] = image
    next_ref[...] = gram_of(image)


def solve_kernel(gram_ref, image_ref, solved_ref):
    solved_ref[...] = exact_dot(inverse_factor(gram_ref[...])[0], image_ref[...])


def solve_both_kernel(grams_ref, image_ref, solved_ref, sound_ref):
    count = image_ref.shape[0]
    first, quality = inverse_factor(grams_ref[:count])
    half = lax.dot_general(
        grams_ref[count:], first, TRANS_B, precision=lax.Precision.HIGHEST,
        preferred_element_type=jnp.float32,
    )
    second, next_quality = inverse_factor(exact_dot(first, half))
    solved_ref[...] = exact_dot(second, exact_dot(first, image_ref[...]))
    sound_ref[0] = jnp.where((quality > 0.05) & (next_quality > 0.001), 1, 0)


def payload_kernel(pairs_ref, data_ref, scale_ref, payload_ref, wide_ref):
    n_space, n_sub = lax.axis_size("space"), lax.axis_size("sub")
    space_at, sub_at = lax.axis_index("space"), lax.axis_index("sub")
    lane = lax.broadcasted_iota(jnp.int32, (1, LENGTH), 1)
    used = jnp.zeros((1, LENGTH), jnp.float32)
    for k in range(pairs_ref.shape[1]):
        row, col = pairs_ref[0, k], pairs_ref[1, k]
        device = lax.shift_right_logical(col, 1)
        hop = lax.rem(lax.div(device, n_sub) - space_at + n_space, n_space)
        across = lax.rem(lax.rem(device, n_sub) - sub_at + n_sub, n_sub)
        place = (((hop - 1) * n_sub + across) * 2 + (row & 1)) * 2 + (col & 1)
        used = jnp.where((lane == place) & (hop > 0), 1.0, used)
    payload_ref[: ROWS - 16] = data_ref[: ROWS - 16]
    wide_ref[: ROWS - 16] = data_ref[: ROWS - 16]
    last = jnp.concatenate(
        [
            data_ref[ROWS - 16 : FEAT].astype(jnp.float32),
            scale_ref[...].astype(jnp.float32).reshape(1, LENGTH),
            used,
            jnp.zeros((ROWS - MASK_ROW - 1, LENGTH), jnp.float32),
        ],
        0,
    ).astype(jnp.bfloat16)
    payload_ref[ROWS - 16 :] = last
    wide_ref[ROWS - 16 : ROWS] = last
    wide_ref[ROWS:] = jnp.zeros((WIDE - ROWS, LENGTH), jnp.bfloat16)


def on_device(trajectories, kernel_scale, start_vectors, pair_list):
    vecs, length = start_vectors.shape
    light = dict(
        cost_estimate=pl.CostEstimate(flops=2**20, bytes_accessed=2**17, transcendentals=0),
        compiler_params=pltpu.CompilerParams(vmem_limit_bytes=SMALL_LIMIT),
    )

    payload, wide = pl.pallas_call(
        payload_kernel,
        in_specs=[pl.BlockSpec(memory_space=pltpu.SMEM)] + [pl.BlockSpec(memory_space=pltpu.VMEM)] * 2,
        out_shape=[jax.ShapeDtypeStruct((rows, length), jnp.bfloat16) for rows in (ROWS, WIDE)],
        **light,
    )(pair_list.T, trajectories, kernel_scale)

    members = [wide] + [shifted(wide, "sub", e) for e in range(1, N_SUB)]
    ahead, behind = shifted(payload, "space", 2), shifted(payload, "space", -2)
    later, ahead, behind = lax.optimization_barrier((payload, ahead, behind))
    there = swapped(later), swapped(ahead), swapped(behind)
    far = lax.ppermute(later, "space", far_pairs(lax.axis_size("space")))
    blocks, rate = row_operands(members)
    listed = jnp.stack([member[MASK_ROW, : REACH * PAIRS] for member in members]).astype(jnp.int32)
    listed = listed.reshape(N_SUB * REACH * PAIRS)

    tiles = []
    carried = payload
    for at, sources in enumerate(((ahead, behind), (*there, far))):
        *tile, carried = hop_tiles(
            WINDOWS[at], at == 0, at == len(WINDOWS) - 1, listed, blocks, rate, sources, carried
        )
        tiles.append(tile)
    degree = carried
    shares = exchanged([degree[e, :1] for e in range(N_SUB)])
    root = lax.rsqrt((shares[0] + shares[1]) + (shares[2] + shares[3]))

    vector_shape = jax.ShapeDtypeStruct((vecs, length), jnp.float32)
    gram_shape = jax.ShapeDtypeStruct((vecs, vecs), jnp.float32)
    def imaged(parts, scaled):
        return pl.pallas_call(
            functools.partial(image_kernel, scaled), out_shape=[vector_shape, gram_shape], **light
        )(root, *exchanged(parts))

    scaled = (root * start_vectors).astype(jnp.bfloat16)
    raw, first_gram = imaged(sweep(space_window(scaled), tiles), True)

    image, second_gram = imaged(sweep(space_window(raw), tiles), False)
    grams = summed(jnp.concatenate([first_gram, second_gram], 0))
    subspace, sound = pl.pallas_call(
        solve_both_kernel,
        in_specs=[pl.BlockSpec(memory_space=pltpu.VMEM)] * 2,
        out_specs=[pl.BlockSpec(memory_space=pltpu.VMEM), pl.BlockSpec(memory_space=pltpu.SMEM)],
        out_shape=[vector_shape, jax.ShapeDtypeStruct((1,), jnp.int32)],
        **light,
    )(grams, image)

    def directly():
        solved, gram = pl.pallas_call(
            solve_gram_kernel, out_shape=[vector_shape, gram_shape], **light
        )(grams[:vecs], image)
        return pl.pallas_call(solve_kernel, out_shape=vector_shape, **light)(summed(gram), solved)

    return lax.cond(sound[0] > 0, lambda: subspace, directly)


def solution(mesh):
    placed = (
        P(None, ("space", "sub")),
        P(("space", "sub")),
        P(None, ("space", "sub")),
        P(("space", "sub"), None),
    )
    return jax.shard_map(
        on_device, mesh=mesh, in_specs=placed, out_specs=P(None, ("space", "sub")), check_vma=False
    )
```

```python
import functools

import jax
import jax.numpy as jnp
from jax import lax
from jax.experimental import pallas as pl
from jax.experimental.pallas import tpu as pltpu
from jax.sharding import PartitionSpec as P

FEAT = 300
BLOCK = 256
LENGTH = 2 * BLOCK
REACH = 3
N_SUB = 4
ROWS = 304
DEPTH = 320
SCALE_ROW = 300
MASK_ROW = 301
PAIRS = 4 * N_SUB
SLOTS = 80
COUNT = SLOTS - 1
NOBODY = 2 * N_SUB
UNROLL = 8
AT_ONCE = 16
HALF = UNROLL // 2
WINDOWS = (((2, 2), (-2, -2)), ((1, -1), (3, 1), (-1, -3), (-3, 3)))
PLACES = ((2, 4, 0), (1, 3, 5, 6))
WIDE = 320
STARTS = (0, 5)
GROUPS = 13
LOG2E = 1.4426950408889634
VMEM_LIMIT = 24 * 1024 * 1024
SWEEP_LIMIT = 24 * 1024 * 1024
SMALL_LIMIT = 4 * 1024 * 1024
PAYLOAD_LIMIT = 60 * 1024 * 1024
TRANS_B = (((1,), (1,)), ((), ()))


def shifted(value, axis, steps):
    count = lax.axis_size(axis)
    return lax.ppermute(value, axis, [((at + steps) % count, at) for at in range(count)])


def far_pairs(count):
    return [(at, (at + (3 if at % 2 else -3)) % count) for at in range(count)]


def swapped(value):
    return lax.ppermute(value, "space", [(at, at ^ 1) for at in range(lax.axis_size("space"))])


def space_window(value):
    far, ahead, behind = lax.optimization_barrier(
        (
            lax.ppermute(value, "space", far_pairs(lax.axis_size("space"))),
            shifted(value, "space", 2),
            shifted(value, "space", -2),
        )
    )
    here = jnp.stack([value, ahead, behind])
    return here, swapped(here), far


def groups_by(key, n_space, n_sub):
    found = {}
    for place in range(n_space * n_sub):
        found.setdefault(key(place // n_sub, place % n_sub), []).append(place)
    return list(found.values())


def summed(value):
    n_space, n_sub = lax.axis_size("space"), lax.axis_size("sub")
    shape = value.shape
    value = value.reshape(-1, 128)
    for key in (lambda s, y: (s // 8, 0), lambda s, y: (s % 8, y)):
        groups = groups_by(key, n_space, n_sub)
        sent = jnp.broadcast_to(value[None], (len(groups[0]),) + value.shape)
        value = jnp.sum(
            lax.all_to_all(sent, ("space", "sub"), 0, 0, axis_index_groups=groups), 0
        )
    return value.reshape(shape)


def pieces(norm):
    high = norm.astype(jnp.bfloat16).astype(jnp.float32)
    rest = norm - high
    middle = rest.astype(jnp.bfloat16).astype(jnp.float32)
    return high, middle, rest - middle


def ones_and_norms(norm, ones_at, norms_at):
    place = lax.broadcasted_iota(jnp.int32, (DEPTH - ROWS, 1), 0)
    tail = jnp.where((place >= ones_at) & (place < ones_at + 3), 1.0, 0.0)
    for k, piece in enumerate(pieces(norm)):
        tail = jnp.where(place == norms_at + k, -piece, tail)
    return tail


def rows_kernel(*refs):
    rows_ref, rate_ref = refs[N_SUB:]
    for e in range(N_SUB):
        wide = refs[e][:FEAT, :].astype(jnp.float32)
        tail = ones_and_norms(jnp.sum(wide * wide, axis=0, keepdims=True), 0, 3)
        tail = tail.astype(jnp.bfloat16)
        rate = LOG2E / refs[e][SCALE_ROW : SCALE_ROW + 1, :].astype(jnp.float32)
        below = lax.broadcasted_iota(jnp.int32, (ROWS, 1), 0) < FEAT
        twice = jnp.where(below, 2.0 * refs[e][:ROWS, :].astype(jnp.float32), 0.0).astype(jnp.bfloat16)
        for r in range(2):
            span = slice(r * BLOCK, (r + 1) * BLOCK)
            rows_ref[2 * e + r, :ROWS] = twice[:, span]
            rows_ref[2 * e + r, ROWS:] = tail[:, span]
            rate_ref[2 * e + r] = jnp.broadcast_to(rate[:, span], (8, BLOCK))


def row_operands(members):
    return pl.pallas_call(
        rows_kernel,
        out_shape=[
            jax.ShapeDtypeStruct((2 * N_SUB, DEPTH, BLOCK), jnp.bfloat16),
            jax.ShapeDtypeStruct((2 * N_SUB, 8, BLOCK), jnp.float32),
        ],
        compiler_params=pltpu.CompilerParams(vmem_limit_bytes=VMEM_LIMIT),
        cost_estimate=pl.CostEstimate(flops=2**22, bytes_accessed=4 * 2**20, transcendentals=0),
    )(*members)


def prepare_columns(data_ref, first, lhs, rate_ref):
    wide = data_ref[...].astype(jnp.float32)
    rate = 1.0 / wide[SCALE_ROW : SCALE_ROW + 1]
    squares = wide[:FEAT] * wide[:FEAT]
    tail = ones_and_norms(jnp.sum(squares, axis=0, keepdims=True), 3, 0)
    full = jnp.concatenate([wide, tail, jnp.zeros((384 - DEPTH, LENGTH), jnp.float32)], 0)
    turned = full.T[:, :DEPTH].astype(jnp.bfloat16)
    rate = jnp.broadcast_to(rate, (128, LENGTH)).T
    for c in range(2):
        lhs[first + c] = turned[c * BLOCK : (c + 1) * BLOCK]
        rate_ref[first + c] = rate[c * BLOCK : (c + 1) * BLOCK]


def list_pairs(hops, mine_ref, theirs, rows_ref, cols_ref, count):
    def member(e, count):
        for k, (hop, bits) in enumerate(zip(hops, theirs)):
            base = (e * REACH + lax.abs(hop) - 1) * PAIRS + lax.rem(N_SUB - e, N_SUB) * 4
            for r in range(2):
                for c in range(2):
                    behind = lax.shift_right_logical(bits, e * 4 + c * 2 + r) & 1
                    used = jnp.where(hop > 0, mine_ref[base + r * 2 + c], behind)
                    rows_ref[count] = e * 2 + r
                    cols_ref[count] = k * 2 + c
                    count = count + used
        return count

    count = lax.fori_loop(0, N_SUB, member, count)
    for k in range(UNROLL + HALF):
        rows_ref[count + k] = NOBODY
        cols_ref[count + k] = 0
    rows_ref[COUNT] = count
    cols_ref[COUNT] = count
    return count


def listed_behind(data_ref, hop):
    lane = lax.broadcasted_iota(jnp.int32, (1, 128), 1) - (lax.abs(hop) - 1) * PAIRS
    weight = lax.shift_left(jnp.ones_like(lane), jnp.clip(lane, 0, PAIRS)).astype(jnp.float32)
    weight = jnp.where((lane >= 0) & (lane < PAIRS), weight, 0.0)
    used = data_ref[MASK_ROW : MASK_ROW + 1, :128].astype(jnp.float32)
    return jnp.sum(used * weight).astype(jnp.int32)


def tile_kernel(windows, first, last, mine_ref, blocks_ref, rate_ref, *refs):
    window_refs, extra_ref, refs = refs[: len(windows)], refs[len(windows)], refs[len(windows) + 1 :]
    odd_place = lax.rem(lax.axis_index("space"), 2) == 1
    hops = [jnp.where(odd_place, odd_hop, even_hop) for even_hop, odd_hop in windows]
    tile_ref, rows_ref, cols_ref, sums_ref, lhs, col, even, odd, made, sems, *held = refs
    total = held[0] if last else sums_ref
    for k, window_ref in enumerate(window_refs):
        prepare_columns(window_ref, 2 * k, lhs, col)
    count = 0
    if first:
        prepare_columns(extra_ref, 2 * len(hops), lhs, col)
        for r in range(2):
            rows_ref[r] = r
            cols_ref[r] = 2 * len(hops) + r
        count = 2
        total[...] = jnp.zeros_like(total)
    else:
        total[...] = extra_ref[...]
    theirs = [listed_behind(ref, hop) for ref, hop in zip(window_refs, hops)]
    count = list_pairs(hops, mine_ref, theirs, rows_ref, cols_ref, jnp.int32(count))

    def products(buffer, base):
        for n in range(HALF):
            row = lax.min(rows_ref[base + n], NOBODY - 1)
            buffer[n] = jnp.dot(
                lhs[cols_ref[base + n]], blocks_ref[row], preferred_element_type=jnp.float32
            )

    def finish(buffer, base):
        for n in range(HALF):
            at = base + n
            row = rows_ref[at]
            rate = col[cols_ref[at]]
            rates = jnp.concatenate([rate, rate], 1) * rate_ref[lax.min(row, NOBODY - 1), :1, :]
            tile = jnp.exp2(buffer[n] * rates).astype(jnp.bfloat16)
            made[at] = tile
            total[row] += jnp.sum(tile.astype(jnp.float32).reshape(BLOCK // 8, 8, BLOCK), axis=0)

    def copy(group):
        span = pl.ds(group * UNROLL, UNROLL)
        return pltpu.make_async_copy(made.at[span], tile_ref.at[span], sems.at[group])

    products(even, 0)

    def step(group, _):
        products(odd, UNROLL * group + HALF)
        finish(even, UNROLL * group)
        products(even, UNROLL * group + UNROLL)
        finish(odd, UNROLL * group + HALF)
        copy(group).start()
        return 0

    groups = lax.div(count + (UNROLL - 1), UNROLL)
    lax.fori_loop(0, groups, step, 0)
    if last:
        for e in range(N_SUB):
            for r in range(2):
                sums = jnp.sum(total[2 * e + r], axis=0, keepdims=True)
                sums_ref[e, :, pl.ds(r * BLOCK, BLOCK)] = jnp.broadcast_to(sums, (8, BLOCK))

    def sent(group, _):
        copy(group).wait()
        return 0

    lax.fori_loop(0, groups, sent, 0)


def hop_tiles(windows, first, last, mine, blocks, rate, sources, extra):
    smem = pl.BlockSpec(memory_space=pltpu.SMEM)
    vmem = pl.BlockSpec(memory_space=pltpu.VMEM)
    columns = 2 * len(windows) + (2 if first else 0)
    slots = len(windows) * PAIRS + (UNROLL if first else 0)
    sums = (NOBODY + 1, 8, BLOCK)
    return pl.pallas_call(
        functools.partial(tile_kernel, windows, first, last),
        in_specs=[smem] + [vmem] * (3 + len(sources)),
        out_specs=[pl.BlockSpec(memory_space=pl.ANY), smem, smem, vmem],
        out_shape=[
            jax.ShapeDtypeStruct((slots, BLOCK, BLOCK), jnp.bfloat16),
            jax.ShapeDtypeStruct((SLOTS,), jnp.int32),
            jax.ShapeDtypeStruct((SLOTS,), jnp.int32),
            jax.ShapeDtypeStruct((N_SUB, 8, LENGTH) if last else sums, jnp.float32),
        ],
        scratch_shapes=[
            pltpu.VMEM((columns, BLOCK, DEPTH), jnp.bfloat16),
            pltpu.VMEM((columns, BLOCK, 128), jnp.float32),
            pltpu.VMEM((HALF, BLOCK, BLOCK), jnp.float32),
            pltpu.VMEM((HALF, BLOCK, BLOCK), jnp.float32),
            pltpu.VMEM((slots, BLOCK, BLOCK), jnp.bfloat16),
            pltpu.SemaphoreType.DMA((slots // UNROLL,)),
        ]
        + ([pltpu.VMEM(sums, jnp.float32)] if last else []),
        compiler_params=pltpu.CompilerParams(vmem_limit_bytes=VMEM_LIMIT),
        cost_estimate=pl.CostEstimate(
            flops=8 * len(windows) * 2 * DEPTH * BLOCK * BLOCK,
            bytes_accessed=7 * 2**20,
            transcendentals=8 * len(windows) * BLOCK * BLOCK,
        ),
    )(mine, blocks, rate, *sources, extra)


def stacked(vectors):
    if vectors.dtype == jnp.bfloat16:
        return vectors
    high = vectors.astype(jnp.bfloat16)
    return jnp.concatenate([high, (vectors - high.astype(jnp.float32)).astype(jnp.bfloat16)], 0)


def sweep_kernel(parts, *refs):
    list_refs, tile_refs, vector_refs = refs[:4], refs[4:6], refs[6:9]
    out_refs, (held, total, tiles, sems) = refs[9:13], refs[13:]
    vecs = vector_refs[0].shape[1]

    def copy(k, at):
        span = pl.ds(at * UNROLL, UNROLL)
        place = pl.ds((STARTS[k] + at) * UNROLL, UNROLL)
        return pltpu.make_async_copy(tile_refs[k].at[span], tiles.at[place], sems.at[STARTS[k] + at])

    groups = [lax.div(list_refs[2 * k][COUNT] + (UNROLL - 1), UNROLL) for k in range(len(WINDOWS))]
    for k in range(len(WINDOWS)):

        def fetch(at, _, k=k):
            copy(k, at).start()
            return 0

        lax.fori_loop(0, groups[k], fetch, 0)

    here, there, far = vector_refs
    for k, vectors in enumerate(
        (here[0], there[0], here[1], there[1], here[2], there[2], far[...])
    ):
        both = stacked(vectors)
        for c in range(2):
            held[2 * k + c] = both[:, c * BLOCK : (c + 1) * BLOCK]
    total[...] = jnp.zeros_like(total)

    for k, slots in enumerate(PLACES):

        def step(at, _, k=k, slots=slots, rows_ref=list_refs[2 * k], cols_ref=list_refs[2 * k + 1]):
            copy(k, at).wait()
            terms = []
            for n in range(UNROLL):
                block = cols_ref[UNROLL * at + n]
                slot = 0
                for at_slot, found in enumerate(slots):
                    slot = jnp.where(lax.shift_right_logical(block, 1) == at_slot, found, slot)
                block = 2 * slot + (block & 1)
                tile = tiles[(STARTS[k] + at) * UNROLL + n]
                terms.append(jnp.dot(held[block], tile, preferred_element_type=jnp.float32))
            for n in range(UNROLL):
                total[rows_ref[UNROLL * at + n]] += terms[n]
            return 0

        lax.fori_loop(0, groups[k], step, 0)

    for e in range(N_SUB):
        for r in range(2):
            result = total[2 * e + r, :vecs]
            for part in range(1, parts):
                result = result + total[2 * e + r, part * vecs : (part + 1) * vecs]
            out_refs[e][:, pl.ds(r * BLOCK, BLOCK)] = result


def sweep(near, tiles):
    own = near[0]
    vecs = own.shape[1]
    smem = pl.BlockSpec(memory_space=pltpu.SMEM)
    vmem = pl.BlockSpec(memory_space=pltpu.VMEM)
    parts = 1 if own.dtype == jnp.bfloat16 else 2
    lists = [part for tile in tiles for part in tile[1:]]
    return pl.pallas_call(
        functools.partial(sweep_kernel, parts),
        in_specs=[smem] * 4 + [pl.BlockSpec(memory_space=pl.ANY)] * 2 + [vmem] * 3,
        out_specs=[vmem] * 4,
        out_shape=[jax.ShapeDtypeStruct((vecs, LENGTH), jnp.float32)] * 4,
        scratch_shapes=[
            pltpu.VMEM((14, parts * vecs, BLOCK), jnp.bfloat16),
            pltpu.VMEM((NOBODY + 1, parts * vecs, BLOCK), jnp.float32),
            pltpu.VMEM((GROUPS * UNROLL, BLOCK, BLOCK), jnp.bfloat16),
            pltpu.SemaphoreType.DMA((GROUPS,)),
        ],
        compiler_params=pltpu.CompilerParams(vmem_limit_bytes=SWEEP_LIMIT),
        cost_estimate=pl.CostEstimate(
            flops=50 * 2 * 128 * BLOCK * BLOCK, bytes_accessed=7 * 2**20, transcendentals=0
        ),
    )(*lists, *[tile[0] for tile in tiles], *near)


def exchanged(parts):
    return [parts[0]] + [shifted(parts[e], "sub", -e) for e in range(1, N_SUB)]


def gram_of(image):
    return lax.dot_general(
        image, image, TRANS_B, precision=lax.Precision.HIGHEST, preferred_element_type=jnp.float32
    )


def inverse_factor(gram):
    count = gram.shape[0]
    place = lax.broadcasted_iota(jnp.int32, (count, 1), 0)
    across = lax.broadcasted_iota(jnp.int32, (count, count), 1)
    identity = jnp.where(across == place, 1.0, 0.0)
    joined = jnp.concatenate([gram, identity], 1)
    for k in range(0, count, AT_ONCE):
        columns = [
            jnp.broadcast_to(joined[:, k + n : k + n + 1], joined.shape) for n in range(AT_ONCE)
        ]
        rows = [joined[k + n : k + n + 1, :] for n in range(AT_ONCE)]
        for n in range(AT_ONCE):
            at = slice(k + n, k + n + 1)
            factor = jnp.where(place > k + n, columns[n] * (1.0 / columns[n][at]), 0.0)
            for m in range(n + 1, AT_ONCE):
                columns[m] = columns[m] - factor * columns[m][at]
                rows[m] = rows[m] - factor[k + m : k + m + 1] * rows[n]
            joined = joined - factor * rows[n]
    pivots = jnp.sum(joined[:, :count] * identity, axis=1, keepdims=True)
    diagonal = jnp.sum(gram * identity, axis=1, keepdims=True)
    return joined[:, count:] / jnp.sqrt(pivots), jnp.min(pivots / diagonal)


def exact_dot(left, right):
    return jnp.dot(left, right, precision=lax.Precision.HIGHEST, preferred_element_type=jnp.float32)


def image_of(root_ref, part_refs):
    first, second, third, fourth = (part_ref[...] for part_ref in part_refs)
    return root_ref[...] * ((first + second) + (third + fourth))


def image_kernel(scaled, root_ref, *refs):
    image = image_of(root_ref, refs[:4])
    refs[4][...] = root_ref[...] * image if scaled else image
    refs[5][...] = gram_of(image)


def solve_gram_kernel(gram_ref, image_ref, solved_ref, next_ref):
    image = exact_dot(inverse_factor(gram_ref[...])[0], image_ref[...])
    solved_ref[...] = image
    next_ref[...] = gram_of(image)


def solve_kernel(gram_ref, image_ref, solved_ref):
    solved_ref[...] = exact_dot(inverse_factor(gram_ref[...])[0], image_ref[...])


def solve_both_kernel(grams_ref, image_ref, solved_ref, sound_ref):
    count = image_ref.shape[0]
    first, quality = inverse_factor(grams_ref[:count])
    half = lax.dot_general(
        grams_ref[count:], first, TRANS_B, precision=lax.Precision.HIGHEST,
        preferred_element_type=jnp.float32,
    )
    second, next_quality = inverse_factor(exact_dot(first, half))
    solved_ref[...] = exact_dot(second, exact_dot(first, image_ref[...]))
    sound_ref[0] = jnp.where((quality > 0.05) & (next_quality > 0.001), 1, 0)


def payload_kernel(pairs_ref, data_ref, scale_ref, payload_ref, wide_ref):
    n_space, n_sub = lax.axis_size("space"), lax.axis_size("sub")
    space_at, sub_at = lax.axis_index("space"), lax.axis_index("sub")
    lane = lax.broadcasted_iota(jnp.int32, (1, LENGTH), 1)
    used = jnp.zeros((1, LENGTH), jnp.float32)
    for k in range(pairs_ref.shape[1]):
        row, col = pairs_ref[0, k], pairs_ref[1, k]
        device = lax.shift_right_logical(col, 1)
        hop = lax.rem(lax.div(device, n_sub) - space_at + n_space, n_space)
        across = lax.rem(lax.rem(device, n_sub) - sub_at + n_sub, n_sub)
        place = (((hop - 1) * n_sub + across) * 2 + (row & 1)) * 2 + (col & 1)
        used = jnp.where((lane == place) & (hop > 0), 1.0, used)
    payload_ref[: ROWS - 16] = data_ref[: ROWS - 16]
    wide_ref[: ROWS - 16] = data_ref[: ROWS - 16]
    last = jnp.concatenate(
        [
            data_ref[ROWS - 16 : FEAT].astype(jnp.float32),
            scale_ref[...].astype(jnp.float32).reshape(1, LENGTH),
            used,
            jnp.zeros((ROWS - MASK_ROW - 1, LENGTH), jnp.float32),
        ],
        0,
    ).astype(jnp.bfloat16)
    payload_ref[ROWS - 16 :] = last
    wide_ref[ROWS - 16 : ROWS] = last
    wide_ref[ROWS:] = jnp.zeros((WIDE - ROWS, LENGTH), jnp.bfloat16)


def on_device(trajectories, kernel_scale, start_vectors, pair_list):
    vecs, length = start_vectors.shape
    light = dict(
        cost_estimate=pl.CostEstimate(flops=2**20, bytes_accessed=2**17, transcendentals=0),
        compiler_params=pltpu.CompilerParams(vmem_limit_bytes=SMALL_LIMIT),
    )

    payload, wide = pl.pallas_call(
        payload_kernel,
        in_specs=[pl.BlockSpec(memory_space=pltpu.SMEM)] + [pl.BlockSpec(memory_space=pltpu.VMEM)] * 2,
        out_shape=[jax.ShapeDtypeStruct((rows, length), jnp.bfloat16) for rows in (ROWS, WIDE)],
        cost_estimate=light["cost_estimate"],
        compiler_params=pltpu.CompilerParams(vmem_limit_bytes=PAYLOAD_LIMIT),
    )(pair_list.T, trajectories, kernel_scale)

    members = [wide] + [shifted(wide, "sub", e) for e in range(1, N_SUB)]
    ahead, behind = shifted(payload, "space", 2), shifted(payload, "space", -2)
    later, ahead, behind = lax.optimization_barrier((payload, ahead, behind))
    there = swapped(later), swapped(ahead), swapped(behind)
    far = lax.ppermute(later, "space", far_pairs(lax.axis_size("space")))
    blocks, rate = row_operands(members)
    listed = jnp.stack([member[MASK_ROW, : REACH * PAIRS] for member in members]).astype(jnp.int32)
    listed = listed.reshape(N_SUB * REACH * PAIRS)

    tiles = []
    carried = payload
    for at, sources in enumerate(((ahead, behind), (*there, far))):
        *tile, carried = hop_tiles(
            WINDOWS[at], at == 0, at == len(WINDOWS) - 1, listed, blocks, rate, sources, carried
        )
        tiles.append(tile)
    degree = carried
    shares = exchanged([degree[e, :1] for e in range(N_SUB)])
    root = lax.rsqrt((shares[0] + shares[1]) + (shares[2] + shares[3]))

    vector_shape = jax.ShapeDtypeStruct((vecs, length), jnp.float32)
    gram_shape = jax.ShapeDtypeStruct((vecs, vecs), jnp.float32)
    def imaged(parts, scaled):
        return pl.pallas_call(
            functools.partial(image_kernel, scaled), out_shape=[vector_shape, gram_shape], **light
        )(root, *exchanged(parts))

    scaled = (root * start_vectors).astype(jnp.bfloat16)
    raw, first_gram = imaged(sweep(space_window(scaled), tiles), True)

    image, second_gram = imaged(sweep(space_window(raw), tiles), False)
    grams = summed(jnp.concatenate([first_gram, second_gram], 0))
    subspace, sound = pl.pallas_call(
        solve_both_kernel,
        in_specs=[pl.BlockSpec(memory_space=pltpu.VMEM)] * 2,
        out_specs=[pl.BlockSpec(memory_space=pltpu.VMEM), pl.BlockSpec(memory_space=pltpu.SMEM)],
        out_shape=[vector_shape, jax.ShapeDtypeStruct((1,), jnp.int32)],
        **light,
    )(grams, image)

    def directly():
        solved, gram = pl.pallas_call(
            solve_gram_kernel, out_shape=[vector_shape, gram_shape], **light
        )(grams[:vecs], image)
        return pl.pallas_call(solve_kernel, out_shape=vector_shape, **light)(summed(gram), solved)

    return lax.cond(sound[0] > 0, lambda: subspace, directly)


def solution(mesh):
    placed = (
        P(None, ("space", "sub")),
        P(("space", "sub")),
        P(None, ("space", "sub")),
        P(("space", "sub"), None),
    )
    return jax.shard_map(
        on_device, mesh=mesh, in_specs=placed, out_specs=P(None, ("space", "sub")), check_vma=False
    )
```

```python
import functools

import jax
import jax.numpy as jnp
from jax import lax
from jax.experimental import pallas as pl
from jax.experimental.pallas import tpu as pltpu
from jax.sharding import PartitionSpec as P

FEAT = 300
BLOCK = 256
LENGTH = 2 * BLOCK
REACH = 3
N_SUB = 4
ROWS = 304
DEPTH = 320
SCALE_ROW = 300
MASK_ROW = 301
PAIRS = 4 * N_SUB
SLOTS = 80
COUNT = SLOTS - 1
NOBODY = 2 * N_SUB
UNROLL = 8
AT_ONCE = 16
HALF = UNROLL // 2
WINDOWS = (((2, 2), (-2, -2)), ((1, -1), (3, 1), (-1, -3), (-3, 3)))
PLACES = ((2, 4, 0), (1, 3, 5, 6))
WIDE = 320
STARTS = (0, 5)
GROUPS = 13
LOG2E = 1.4426950408889634
VMEM_LIMIT = 24 * 1024 * 1024
SWEEP_LIMIT = 24 * 1024 * 1024
SMALL_LIMIT = 4 * 1024 * 1024
PAYLOAD_LIMIT = 60 * 1024 * 1024
TRANS_B = (((1,), (1,)), ((), ()))


def shifted(value, axis, steps):
    count = lax.axis_size(axis)
    return lax.ppermute(value, axis, [((at + steps) % count, at) for at in range(count)])


def far_pairs(count):
    return [(at, (at + (3 if at % 2 else -3)) % count) for at in range(count)]


def swapped(value):
    return lax.ppermute(value, "space", [(at, at ^ 1) for at in range(lax.axis_size("space"))])


def space_window(value):
    far, ahead, behind = lax.optimization_barrier(
        (
            lax.ppermute(value, "space", far_pairs(lax.axis_size("space"))),
            shifted(value, "space", 2),
            shifted(value, "space", -2),
        )
    )
    here = jnp.stack([value, ahead, behind])
    return here, swapped(here), far


def groups_by(key, n_space, n_sub):
    found = {}
    for place in range(n_space * n_sub):
        found.setdefault(key(place // n_sub, place % n_sub), []).append(place)
    return list(found.values())


def summed(value):
    n_space, n_sub = lax.axis_size("space"), lax.axis_size("sub")
    shape = value.shape
    value = value.reshape(-1, 128)
    for key in (lambda s, y: (s // 8, 0), lambda s, y: (s % 8, y)):
        groups = groups_by(key, n_space, n_sub)
        sent = jnp.broadcast_to(value[None], (len(groups[0]),) + value.shape)
        value = jnp.sum(
            lax.all_to_all(sent, ("space", "sub"), 0, 0, axis_index_groups=groups), 0
        )
    return value.reshape(shape)


def pieces(norm):
    high = norm.astype(jnp.bfloat16).astype(jnp.float32)
    rest = norm - high
    middle = rest.astype(jnp.bfloat16).astype(jnp.float32)
    return high, middle, rest - middle


def ones_and_norms(norm, ones_at, norms_at):
    place = lax.broadcasted_iota(jnp.int32, (DEPTH - ROWS, 1), 0)
    tail = jnp.where((place >= ones_at) & (place < ones_at + 3), 1.0, 0.0)
    for k, piece in enumerate(pieces(norm)):
        tail = jnp.where(place == norms_at + k, -piece, tail)
    return tail


def rows_kernel(*refs):
    rows_ref, rate_ref = refs[N_SUB:]
    for e in range(N_SUB):
        wide = refs[e][:FEAT, :].astype(jnp.float32)
        tail = ones_and_norms(jnp.sum(wide * wide, axis=0, keepdims=True), 0, 3)
        tail = tail.astype(jnp.bfloat16)
        rate = LOG2E / refs[e][SCALE_ROW : SCALE_ROW + 1, :].astype(jnp.float32)
        below = lax.broadcasted_iota(jnp.int32, (ROWS, 1), 0) < FEAT
        twice = jnp.where(below, 2.0 * refs[e][:ROWS, :].astype(jnp.float32), 0.0).astype(jnp.bfloat16)
        for r in range(2):
            span = slice(r * BLOCK, (r + 1) * BLOCK)
            rows_ref[2 * e + r, :ROWS] = twice[:, span]
            rows_ref[2 * e + r, ROWS:] = tail[:, span]
            rate_ref[2 * e + r] = jnp.broadcast_to(rate[:, span], (8, BLOCK))


def row_operands(members):
    return pl.pallas_call(
        rows_kernel,
        out_shape=[
            jax.ShapeDtypeStruct((2 * N_SUB, DEPTH, BLOCK), jnp.bfloat16),
            jax.ShapeDtypeStruct((2 * N_SUB, 8, BLOCK), jnp.float32),
        ],
        compiler_params=pltpu.CompilerParams(vmem_limit_bytes=VMEM_LIMIT),
        cost_estimate=pl.CostEstimate(flops=2**22, bytes_accessed=4 * 2**20, transcendentals=0),
    )(*members)


def prepare_columns(data_ref, first, lhs, rate_ref):
    wide = data_ref[:ROWS, :].astype(jnp.float32)
    rate = 1.0 / wide[SCALE_ROW : SCALE_ROW + 1]
    squares = wide[:FEAT] * wide[:FEAT]
    tail = ones_and_norms(jnp.sum(squares, axis=0, keepdims=True), 3, 0)
    full = jnp.concatenate([wide, tail, jnp.zeros((384 - DEPTH, LENGTH), jnp.float32)], 0)
    turned = full.T[:, :DEPTH].astype(jnp.bfloat16)
    rate = jnp.broadcast_to(rate, (128, LENGTH)).T
    for c in range(2):
        lhs[first + c] = turned[c * BLOCK : (c + 1) * BLOCK]
        rate_ref[first + c] = rate[c * BLOCK : (c + 1) * BLOCK]


def list_pairs(hops, mine_ref, theirs, rows_ref, cols_ref, count):
    def member(e, count):
        for k, (hop, bits) in enumerate(zip(hops, theirs)):
            base = (e * REACH + lax.abs(hop) - 1) * PAIRS + lax.rem(N_SUB - e, N_SUB) * 4
            for r in range(2):
                for c in range(2):
                    behind = lax.shift_right_logical(bits, e * 4 + c * 2 + r) & 1
                    used = jnp.where(hop > 0, mine_ref[base + r * 2 + c], behind)
                    rows_ref[count] = e * 2 + r
                    cols_ref[count] = k * 2 + c
                    count = count + used
        return count

    count = lax.fori_loop(0, N_SUB, member, count)
    for k in range(UNROLL + HALF):
        rows_ref[count + k] = NOBODY
        cols_ref[count + k] = 0
    rows_ref[COUNT] = count
    cols_ref[COUNT] = count
    return count


def listed_behind(data_ref, hop):
    lane = lax.broadcasted_iota(jnp.int32, (1, 128), 1) - (lax.abs(hop) - 1) * PAIRS
    weight = lax.shift_left(jnp.ones_like(lane), jnp.clip(lane, 0, PAIRS)).astype(jnp.float32)
    weight = jnp.where((lane >= 0) & (lane < PAIRS), weight, 0.0)
    used = data_ref[MASK_ROW : MASK_ROW + 1, :128].astype(jnp.float32)
    return jnp.sum(used * weight).astype(jnp.int32)


def tile_kernel(windows, first, last, mine_ref, blocks_ref, rate_ref, *refs):
    window_refs, extra_ref, refs = refs[: len(windows)], refs[len(windows)], refs[len(windows) + 1 :]
    odd_place = lax.rem(lax.axis_index("space"), 2) == 1
    hops = [jnp.where(odd_place, odd_hop, even_hop) for even_hop, odd_hop in windows]
    tile_ref, rows_ref, cols_ref, sums_ref, lhs, col, even, odd, made, sems, *held = refs
    total = held[0] if last else sums_ref
    for k, window_ref in enumerate(window_refs):
        prepare_columns(window_ref, 2 * k, lhs, col)
    count = 0
    if first:
        prepare_columns(extra_ref, 2 * len(hops), lhs, col)
        for r in range(2):
            rows_ref[r] = r
            cols_ref[r] = 2 * len(hops) + r
        count = 2
        total[...] = jnp.zeros_like(total)
    else:
        total[...] = extra_ref[...]
    theirs = [listed_behind(ref, hop) for ref, hop in zip(window_refs, hops)]
    count = list_pairs(hops, mine_ref, theirs, rows_ref, cols_ref, jnp.int32(count))

    def products(buffer, base):
        for n in range(HALF):
            row = lax.min(rows_ref[base + n], NOBODY - 1)
            buffer[n] = jnp.dot(
                lhs[cols_ref[base + n]], blocks_ref[row], preferred_element_type=jnp.float32
            )

    def finish(buffer, base):
        for n in range(HALF):
            at = base + n
            row = rows_ref[at]
            rate = col[cols_ref[at]]
            rates = jnp.concatenate([rate, rate], 1) * rate_ref[lax.min(row, NOBODY - 1), :1, :]
            tile = jnp.exp2(buffer[n] * rates).astype(jnp.bfloat16)
            made[at] = tile
            total[row] += jnp.sum(tile.astype(jnp.float32).reshape(BLOCK // 8, 8, BLOCK), axis=0)

    def copy(group):
        span = pl.ds(group * UNROLL, UNROLL)
        return pltpu.make_async_copy(made.at[span], tile_ref.at[span], sems.at[group])

    products(even, 0)

    def step(group, _):
        products(odd, UNROLL * group + HALF)
        finish(even, UNROLL * group)
        products(even, UNROLL * group + UNROLL)
        finish(odd, UNROLL * group + HALF)
        copy(group).start()
        return 0

    groups = lax.div(count + (UNROLL - 1), UNROLL)
    lax.fori_loop(0, groups, step, 0)
    if last:
        for e in range(N_SUB):
            for r in range(2):
                sums = jnp.sum(total[2 * e + r], axis=0, keepdims=True)
                sums_ref[e, :, pl.ds(r * BLOCK, BLOCK)] = jnp.broadcast_to(sums, (8, BLOCK))

    def sent(group, _):
        copy(group).wait()
        return 0

    lax.fori_loop(0, groups, sent, 0)


def hop_tiles(windows, first, last, mine, blocks, rate, sources, extra):
    smem = pl.BlockSpec(memory_space=pltpu.SMEM)
    vmem = pl.BlockSpec(memory_space=pltpu.VMEM)
    columns = 2 * len(windows) + (2 if first else 0)
    slots = len(windows) * PAIRS + (UNROLL if first else 0)
    sums = (NOBODY + 1, 8, BLOCK)
    return pl.pallas_call(
        functools.partial(tile_kernel, windows, first, last),
        in_specs=[smem] + [vmem] * (3 + len(sources)),
        out_specs=[pl.BlockSpec(memory_space=pl.ANY), smem, smem, vmem],
        out_shape=[
            jax.ShapeDtypeStruct((slots, BLOCK, BLOCK), jnp.bfloat16),
            jax.ShapeDtypeStruct((SLOTS,), jnp.int32),
            jax.ShapeDtypeStruct((SLOTS,), jnp.int32),
            jax.ShapeDtypeStruct((N_SUB, 8, LENGTH) if last else sums, jnp.float32),
        ],
        scratch_shapes=[
            pltpu.VMEM((columns, BLOCK, DEPTH), jnp.bfloat16),
            pltpu.VMEM((columns, BLOCK, 128), jnp.float32),
            pltpu.VMEM((HALF, BLOCK, BLOCK), jnp.float32),
            pltpu.VMEM((HALF, BLOCK, BLOCK), jnp.float32),
            pltpu.VMEM((slots, BLOCK, BLOCK), jnp.bfloat16),
            pltpu.SemaphoreType.DMA((slots // UNROLL,)),
        ]
        + ([pltpu.VMEM(sums, jnp.float32)] if last else []),
        compiler_params=pltpu.CompilerParams(vmem_limit_bytes=VMEM_LIMIT),
        cost_estimate=pl.CostEstimate(
            flops=8 * len(windows) * 2 * DEPTH * BLOCK * BLOCK,
            bytes_accessed=7 * 2**20,
            transcendentals=8 * len(windows) * BLOCK * BLOCK,
        ),
    )(mine, blocks, rate, *sources, extra)


def stacked(vectors):
    if vectors.dtype == jnp.bfloat16:
        return vectors
    high = vectors.astype(jnp.bfloat16)
    return jnp.concatenate([high, (vectors - high.astype(jnp.float32)).astype(jnp.bfloat16)], 0)


def sweep_kernel(parts, *refs):
    list_refs, tile_refs, vector_refs = refs[:4], refs[4:6], refs[6:9]
    out_refs, (held, total, tiles, sems) = refs[9:13], refs[13:]
    vecs = vector_refs[0].shape[1]

    def copy(k, at):
        span = pl.ds(at * UNROLL, UNROLL)
        place = pl.ds((STARTS[k] + at) * UNROLL, UNROLL)
        return pltpu.make_async_copy(tile_refs[k].at[span], tiles.at[place], sems.at[STARTS[k] + at])

    groups = [lax.div(list_refs[2 * k][COUNT] + (UNROLL - 1), UNROLL) for k in range(len(WINDOWS))]
    for k in range(len(WINDOWS)):

        def fetch(at, _, k=k):
            copy(k, at).start()
            return 0

        lax.fori_loop(0, groups[k], fetch, 0)

    here, there, far = vector_refs
    for k, vectors in enumerate(
        (here[0], there[0], here[1], there[1], here[2], there[2], far[...])
    ):
        both = stacked(vectors)
        for c in range(2):
            held[2 * k + c] = both[:, c * BLOCK : (c + 1) * BLOCK]
    total[...] = jnp.zeros_like(total)

    for k, slots in enumerate(PLACES):

        def step(at, _, k=k, slots=slots, rows_ref=list_refs[2 * k], cols_ref=list_refs[2 * k + 1]):
            copy(k, at).wait()
            terms = []
            for n in range(UNROLL):
                block = cols_ref[UNROLL * at + n]
                slot = 0
                for at_slot, found in enumerate(slots):
                    slot = jnp.where(lax.shift_right_logical(block, 1) == at_slot, found, slot)
                block = 2 * slot + (block & 1)
                tile = tiles[(STARTS[k] + at) * UNROLL + n]
                terms.append(jnp.dot(held[block], tile, preferred_element_type=jnp.float32))
            for n in range(UNROLL):
                total[rows_ref[UNROLL * at + n]] += terms[n]
            return 0

        lax.fori_loop(0, groups[k], step, 0)

    for e in range(N_SUB):
        for r in range(2):
            result = total[2 * e + r, :vecs]
            for part in range(1, parts):
                result = result + total[2 * e + r, part * vecs : (part + 1) * vecs]
            out_refs[e][:, pl.ds(r * BLOCK, BLOCK)] = result


def sweep(near, tiles):
    own = near[0]
    vecs = own.shape[1]
    smem = pl.BlockSpec(memory_space=pltpu.SMEM)
    vmem = pl.BlockSpec(memory_space=pltpu.VMEM)
    parts = 1 if own.dtype == jnp.bfloat16 else 2
    lists = [part for tile in tiles for part in tile[1:]]
    return pl.pallas_call(
        functools.partial(sweep_kernel, parts),
        in_specs=[smem] * 4 + [pl.BlockSpec(memory_space=pl.ANY)] * 2 + [vmem] * 3,
        out_specs=[vmem] * 4,
        out_shape=[jax.ShapeDtypeStruct((vecs, LENGTH), jnp.float32)] * 4,
        scratch_shapes=[
            pltpu.VMEM((14, parts * vecs, BLOCK), jnp.bfloat16),
            pltpu.VMEM((NOBODY + 1, parts * vecs, BLOCK), jnp.float32),
            pltpu.VMEM((GROUPS * UNROLL, BLOCK, BLOCK), jnp.bfloat16),
            pltpu.SemaphoreType.DMA((GROUPS,)),
        ],
        compiler_params=pltpu.CompilerParams(vmem_limit_bytes=SWEEP_LIMIT),
        cost_estimate=pl.CostEstimate(
            flops=50 * 2 * 128 * BLOCK * BLOCK, bytes_accessed=7 * 2**20, transcendentals=0
        ),
    )(*lists, *[tile[0] for tile in tiles], *near)


def exchanged(parts):
    return [parts[0]] + [shifted(parts[e], "sub", -e) for e in range(1, N_SUB)]


def gram_of(image):
    return lax.dot_general(
        image, image, TRANS_B, precision=lax.Precision.HIGHEST, preferred_element_type=jnp.float32
    )


def inverse_factor(gram):
    count = gram.shape[0]
    place = lax.broadcasted_iota(jnp.int32, (count, 1), 0)
    across = lax.broadcasted_iota(jnp.int32, (count, count), 1)
    identity = jnp.where(across == place, 1.0, 0.0)
    joined = jnp.concatenate([gram, identity], 1)
    for k in range(0, count, AT_ONCE):
        columns = [
            jnp.broadcast_to(joined[:, k + n : k + n + 1], joined.shape) for n in range(AT_ONCE)
        ]
        rows = [joined[k + n : k + n + 1, :] for n in range(AT_ONCE)]
        for n in range(AT_ONCE):
            at = slice(k + n, k + n + 1)
            factor = jnp.where(place > k + n, columns[n] * (1.0 / columns[n][at]), 0.0)
            for m in range(n + 1, AT_ONCE):
                columns[m] = columns[m] - factor * columns[m][at]
                rows[m] = rows[m] - factor[k + m : k + m + 1] * rows[n]
            joined = joined - factor * rows[n]
    pivots = jnp.sum(joined[:, :count] * identity, axis=1, keepdims=True)
    diagonal = jnp.sum(gram * identity, axis=1, keepdims=True)
    return joined[:, count:] / jnp.sqrt(pivots), jnp.min(pivots / diagonal)


def exact_dot(left, right):
    return jnp.dot(left, right, precision=lax.Precision.HIGHEST, preferred_element_type=jnp.float32)


def image_of(root_ref, part_refs):
    first, second, third, fourth = (part_ref[...] for part_ref in part_refs)
    return root_ref[...] * ((first + second) + (third + fourth))


def image_kernel(scaled, root_ref, *refs):
    image = image_of(root_ref, refs[:4])
    refs[4][...] = root_ref[...] * image if scaled else image
    refs[5][...] = gram_of(image)


def solve_gram_kernel(gram_ref, image_ref, solved_ref, next_ref):
    image = exact_dot(inverse_factor(gram_ref[...])[0], image_ref[...])
    solved_ref[...] = image
    next_ref[...] = gram_of(image)


def solve_kernel(gram_ref, image_ref, solved_ref):
    solved_ref[...] = exact_dot(inverse_factor(gram_ref[...])[0], image_ref[...])


def solve_both_kernel(grams_ref, image_ref, solved_ref, sound_ref):
    count = image_ref.shape[0]
    first, quality = inverse_factor(grams_ref[:count])
    half = lax.dot_general(
        grams_ref[count:], first, TRANS_B, precision=lax.Precision.HIGHEST,
        preferred_element_type=jnp.float32,
    )
    second, next_quality = inverse_factor(exact_dot(first, half))
    solved_ref[...] = exact_dot(second, exact_dot(first, image_ref[...]))
    sound_ref[0] = jnp.where((quality > 0.05) & (next_quality > 0.001), 1, 0)


def payload_kernel(pairs_ref, data_ref, scale_ref, payload_ref, wide_ref):
    n_space, n_sub = lax.axis_size("space"), lax.axis_size("sub")
    space_at, sub_at = lax.axis_index("space"), lax.axis_index("sub")
    lane = lax.broadcasted_iota(jnp.int32, (1, LENGTH), 1)
    used = jnp.zeros((1, LENGTH), jnp.float32)
    for k in range(pairs_ref.shape[1]):
        row, col = pairs_ref[0, k], pairs_ref[1, k]
        device = lax.shift_right_logical(col, 1)
        hop = lax.rem(lax.div(device, n_sub) - space_at + n_space, n_space)
        across = lax.rem(lax.rem(device, n_sub) - sub_at + n_sub, n_sub)
        place = (((hop - 1) * n_sub + across) * 2 + (row & 1)) * 2 + (col & 1)
        used = jnp.where((lane == place) & (hop > 0), 1.0, used)
    payload_ref[: ROWS - 16] = data_ref[: ROWS - 16]
    wide_ref[: ROWS - 16] = data_ref[: ROWS - 16]
    last = jnp.concatenate(
        [
            data_ref[ROWS - 16 : FEAT].astype(jnp.float32),
            scale_ref[...].astype(jnp.float32).reshape(1, LENGTH),
            used,
            jnp.zeros((ROWS - MASK_ROW - 1, LENGTH), jnp.float32),
        ],
        0,
    ).astype(jnp.bfloat16)
    payload_ref[ROWS - 16 :] = last
    wide_ref[ROWS - 16 : ROWS] = last
    wide_ref[ROWS:] = jnp.zeros((WIDE - ROWS, LENGTH), jnp.bfloat16)


def on_device(trajectories, kernel_scale, start_vectors, pair_list):
    vecs, length = start_vectors.shape
    light = dict(
        cost_estimate=pl.CostEstimate(flops=2**20, bytes_accessed=2**17, transcendentals=0),
        compiler_params=pltpu.CompilerParams(vmem_limit_bytes=SMALL_LIMIT),
    )

    payload, wide = pl.pallas_call(
        payload_kernel,
        in_specs=[pl.BlockSpec(memory_space=pltpu.SMEM)] + [pl.BlockSpec(memory_space=pltpu.VMEM)] * 2,
        out_shape=[jax.ShapeDtypeStruct((rows, length), jnp.bfloat16) for rows in (ROWS, WIDE)],
        cost_estimate=light["cost_estimate"],
        compiler_params=pltpu.CompilerParams(vmem_limit_bytes=PAYLOAD_LIMIT),
    )(pair_list.T, trajectories, kernel_scale)

    members = [wide] + [shifted(wide, "sub", e) for e in range(1, N_SUB)]
    ahead, behind = shifted(payload, "space", 2), shifted(payload, "space", -2)
    later, ahead, behind = lax.optimization_barrier((payload, ahead, behind))
    there = swapped(later), swapped(ahead), swapped(behind)
    far = lax.ppermute(later, "space", far_pairs(lax.axis_size("space")))
    blocks, rate = row_operands(members)
    listed = jnp.stack([member[MASK_ROW, : REACH * PAIRS] for member in members]).astype(jnp.int32)
    listed = listed.reshape(N_SUB * REACH * PAIRS)

    tiles = []
    carried = wide
    for at, sources in enumerate(((ahead, behind), (*there, far))):
        *tile, carried = hop_tiles(
            WINDOWS[at], at == 0, at == len(WINDOWS) - 1, listed, blocks, rate, sources, carried
        )
        tiles.append(tile)
    degree = carried
    shares = exchanged([degree[e, :1] for e in range(N_SUB)])
    root = lax.rsqrt((shares[0] + shares[1]) + (shares[2] + shares[3]))

    vector_shape = jax.ShapeDtypeStruct((vecs, length), jnp.float32)
    gram_shape = jax.ShapeDtypeStruct((vecs, vecs), jnp.float32)
    def imaged(parts, scaled):
        return pl.pallas_call(
            functools.partial(image_kernel, scaled), out_shape=[vector_shape, gram_shape], **light
        )(root, *exchanged(parts))

    scaled = (root * start_vectors).astype(jnp.bfloat16)
    raw, first_gram = imaged(sweep(space_window(scaled), tiles), True)

    image, second_gram = imaged(sweep(space_window(raw), tiles), False)
    grams = summed(jnp.concatenate([first_gram, second_gram], 0))
    subspace, sound = pl.pallas_call(
        solve_both_kernel,
        in_specs=[pl.BlockSpec(memory_space=pltpu.VMEM)] * 2,
        out_specs=[pl.BlockSpec(memory_space=pltpu.VMEM), pl.BlockSpec(memory_space=pltpu.SMEM)],
        out_shape=[vector_shape, jax.ShapeDtypeStruct((1,), jnp.int32)],
        **light,
    )(grams, image)

    def directly():
        solved, gram = pl.pallas_call(
            solve_gram_kernel, out_shape=[vector_shape, gram_shape], **light
        )(grams[:vecs], image)
        return pl.pallas_call(solve_kernel, out_shape=vector_shape, **light)(summed(gram), solved)

    return lax.cond(sound[0] > 0, lambda: subspace, directly)


def solution(mesh):
    placed = (
        P(None, ("space", "sub")),
        P(("space", "sub")),
        P(None, ("space", "sub")),
        P(("space", "sub"), None),
    )
    return jax.shard_map(
        on_device, mesh=mesh, in_specs=placed, out_specs=P(None, ("space", "sub")), check_vma=False
    )
```

```python
import functools

import jax
import jax.numpy as jnp
from jax import lax
from jax.experimental import pallas as pl
from jax.experimental.pallas import tpu as pltpu
from jax.sharding import PartitionSpec as P

FEAT = 300
BLOCK = 256
LENGTH = 2 * BLOCK
REACH = 3
N_SUB = 4
ROWS = 304
DEPTH = 320
SCALE_ROW = 300
MASK_ROW = 301
PAIRS = 4 * N_SUB
SLOTS = 80
COUNT = SLOTS - 1
NOBODY = 2 * N_SUB
UNROLL = 8
AT_ONCE = 16
HALF = UNROLL // 2
WINDOWS = (((2, 2), (-2, -2)), ((1, -1), (3, 1), (-1, -3), (-3, 3)))
PLACES = ((2, 4, 0), (1, 3, 5, 6))
WIDE = 320
STARTS = (0, 5)
GROUPS = 13
LOG2E = 1.4426950408889634
VMEM_LIMIT = 24 * 1024 * 1024
SWEEP_LIMIT = 24 * 1024 * 1024
SMALL_LIMIT = 4 * 1024 * 1024
PAYLOAD_LIMIT = 60 * 1024 * 1024
TRANS_B = (((1,), (1,)), ((), ()))


def shifted(value, axis, steps):
    count = lax.axis_size(axis)
    return lax.ppermute(value, axis, [((at + steps) % count, at) for at in range(count)])


def far_pairs(count):
    return [(at, (at + (3 if at % 2 else -3)) % count) for at in range(count)]


def swapped(value):
    return lax.ppermute(value, "space", [(at, at ^ 1) for at in range(lax.axis_size("space"))])


def space_window(value):
    far, ahead, behind = lax.optimization_barrier(
        (
            lax.ppermute(value, "space", far_pairs(lax.axis_size("space"))),
            shifted(value, "space", 2),
            shifted(value, "space", -2),
        )
    )
    here = jnp.stack([value, ahead, behind])
    return here, swapped(here), far


def groups_by(key, n_space, n_sub):
    found = {}
    for place in range(n_space * n_sub):
        found.setdefault(key(place // n_sub, place % n_sub), []).append(place)
    return list(found.values())


def summed(value):
    n_space, n_sub = lax.axis_size("space"), lax.axis_size("sub")
    shape = value.shape
    value = value.reshape(-1, 128)
    for key in (lambda s, y: (s % 8, y), lambda s, y: (s // 8, 0)):
        groups = groups_by(key, n_space, n_sub)
        sent = jnp.broadcast_to(value[None], (len(groups[0]),) + value.shape)
        value = jnp.sum(
            lax.all_to_all(sent, ("space", "sub"), 0, 0, axis_index_groups=groups), 0
        )
    return value.reshape(shape)


def pieces(norm):
    high = norm.astype(jnp.bfloat16).astype(jnp.float32)
    rest = norm - high
    middle = rest.astype(jnp.bfloat16).astype(jnp.float32)
    return high, middle, rest - middle


def ones_and_norms(norm, ones_at, norms_at):
    place = lax.broadcasted_iota(jnp.int32, (DEPTH - ROWS, 1), 0)
    tail = jnp.where((place >= ones_at) & (place < ones_at + 3), 1.0, 0.0)
    for k, piece in enumerate(pieces(norm)):
        tail = jnp.where(place == norms_at + k, -piece, tail)
    return tail


def rows_kernel(*refs):
    rows_ref, rate_ref = refs[N_SUB:]
    for e in range(N_SUB):
        wide = refs[e][:FEAT, :].astype(jnp.float32)
        tail = ones_and_norms(jnp.sum(wide * wide, axis=0, keepdims=True), 0, 3)
        tail = tail.astype(jnp.bfloat16)
        rate = LOG2E / refs[e][SCALE_ROW : SCALE_ROW + 1, :].astype(jnp.float32)
        below = lax.broadcasted_iota(jnp.int32, (ROWS, 1), 0) < FEAT
        twice = jnp.where(below, 2.0 * refs[e][:ROWS, :].astype(jnp.float32), 0.0).astype(jnp.bfloat16)
        for r in range(2):
            span = slice(r * BLOCK, (r + 1) * BLOCK)
            rows_ref[2 * e + r, :ROWS] = twice[:, span]
            rows_ref[2 * e + r, ROWS:] = tail[:, span]
            rate_ref[2 * e + r] = jnp.broadcast_to(rate[:, span], (8, BLOCK))


def row_operands(members):
    return pl.pallas_call(
        rows_kernel,
        out_shape=[
            jax.ShapeDtypeStruct((2 * N_SUB, DEPTH, BLOCK), jnp.bfloat16),
            jax.ShapeDtypeStruct((2 * N_SUB, 8, BLOCK), jnp.float32),
        ],
        compiler_params=pltpu.CompilerParams(vmem_limit_bytes=VMEM_LIMIT),
        cost_estimate=pl.CostEstimate(flops=2**22, bytes_accessed=4 * 2**20, transcendentals=0),
    )(*members)


def prepare_columns(data_ref, first, lhs, rate_ref):
    wide = data_ref[:ROWS, :].astype(jnp.float32)
    rate = 1.0 / wide[SCALE_ROW : SCALE_ROW + 1]
    squares = wide[:FEAT] * wide[:FEAT]
    tail = ones_and_norms(jnp.sum(squares, axis=0, keepdims=True), 3, 0)
    full = jnp.concatenate([wide, tail, jnp.zeros((384 - DEPTH, LENGTH), jnp.float32)], 0)
    turned = full.T[:, :DEPTH].astype(jnp.bfloat16)
    rate = jnp.broadcast_to(rate, (128, LENGTH)).T
    for c in range(2):
        lhs[first + c] = turned[c * BLOCK : (c + 1) * BLOCK]
        rate_ref[first + c] = rate[c * BLOCK : (c + 1) * BLOCK]


def list_pairs(hops, mine_ref, theirs, rows_ref, cols_ref, count):
    def member(e, count):
        for k, (hop, bits) in enumerate(zip(hops, theirs)):
            base = (e * REACH + lax.abs(hop) - 1) * PAIRS + lax.rem(N_SUB - e, N_SUB) * 4
            for r in range(2):
                for c in range(2):
                    behind = lax.shift_right_logical(bits, e * 4 + c * 2 + r) & 1
                    used = jnp.where(hop > 0, mine_ref[base + r * 2 + c], behind)
                    rows_ref[count] = e * 2 + r
                    cols_ref[count] = k * 2 + c
                    count = count + used
        return count

    count = lax.fori_loop(0, N_SUB, member, count)
    for k in range(UNROLL + HALF):
        rows_ref[count + k] = NOBODY
        cols_ref[count + k] = 0
    rows_ref[COUNT] = count
    cols_ref[COUNT] = count
    return count


def listed_behind(data_ref, hop):
    lane = lax.broadcasted_iota(jnp.int32, (1, 128), 1) - (lax.abs(hop) - 1) * PAIRS
    weight = lax.shift_left(jnp.ones_like(lane), jnp.clip(lane, 0, PAIRS)).astype(jnp.float32)
    weight = jnp.where((lane >= 0) & (lane < PAIRS), weight, 0.0)
    used = data_ref[MASK_ROW : MASK_ROW + 1, :128].astype(jnp.float32)
    return jnp.sum(used * weight).astype(jnp.int32)


def tile_kernel(windows, first, last, mine_ref, blocks_ref, rate_ref, *refs):
    window_refs, extra_ref, refs = refs[: len(windows)], refs[len(windows)], refs[len(windows) + 1 :]
    odd_place = lax.rem(lax.axis_index("space"), 2) == 1
    hops = [jnp.where(odd_place, odd_hop, even_hop) for even_hop, odd_hop in windows]
    tile_ref, rows_ref, cols_ref, sums_ref, lhs, col, even, odd, made, sems, *held = refs
    total = held[0] if last else sums_ref
    for k, window_ref in enumerate(window_refs):
        prepare_columns(window_ref, 2 * k, lhs, col)
    count = 0
    if first:
        prepare_columns(extra_ref, 2 * len(hops), lhs, col)
        for r in range(2):
            rows_ref[r] = r
            cols_ref[r] = 2 * len(hops) + r
        count = 2
        total[...] = jnp.zeros_like(total)
    else:
        total[...] = extra_ref[...]
    theirs = [listed_behind(ref, hop) for ref, hop in zip(window_refs, hops)]
    count = list_pairs(hops, mine_ref, theirs, rows_ref, cols_ref, jnp.int32(count))

    def products(buffer, base):
        for n in range(HALF):
            row = lax.min(rows_ref[base + n], NOBODY - 1)
            buffer[n] = jnp.dot(
                lhs[cols_ref[base + n]], blocks_ref[row], preferred_element_type=jnp.float32
            )

    def finish(buffer, base):
        for n in range(HALF):
            at = base + n
            row = rows_ref[at]
            rate = col[cols_ref[at]]
            rates = jnp.concatenate([rate, rate], 1) * rate_ref[lax.min(row, NOBODY - 1), :1, :]
            tile = jnp.exp2(buffer[n] * rates).astype(jnp.bfloat16)
            made[at] = tile
            total[row] += jnp.sum(tile.astype(jnp.float32).reshape(BLOCK // 8, 8, BLOCK), axis=0)

    def copy(group):
        span = pl.ds(group * UNROLL, UNROLL)
        return pltpu.make_async_copy(made.at[span], tile_ref.at[span], sems.at[group])

    products(even, 0)

    def step(group, _):
        products(odd, UNROLL * group + HALF)
        finish(even, UNROLL * group)
        products(even, UNROLL * group + UNROLL)
        finish(odd, UNROLL * group + HALF)
        copy(group).start()
        return 0

    groups = lax.div(count + (UNROLL - 1), UNROLL)
    lax.fori_loop(0, groups, step, 0)
    if last:
        for e in range(N_SUB):
            for r in range(2):
                sums = jnp.sum(total[2 * e + r], axis=0, keepdims=True)
                sums_ref[e, :, pl.ds(r * BLOCK, BLOCK)] = jnp.broadcast_to(sums, (8, BLOCK))

    def sent(group, _):
        copy(group).wait()
        return 0

    lax.fori_loop(0, groups, sent, 0)


def hop_tiles(windows, first, last, mine, blocks, rate, sources, extra):
    smem = pl.BlockSpec(memory_space=pltpu.SMEM)
    vmem = pl.BlockSpec(memory_space=pltpu.VMEM)
    columns = 2 * len(windows) + (2 if first else 0)
    slots = len(windows) * PAIRS + (UNROLL if first else 0)
    sums = (NOBODY + 1, 8, BLOCK)
    return pl.pallas_call(
        functools.partial(tile_kernel, windows, first, last),
        in_specs=[smem] + [vmem] * (3 + len(sources)),
        out_specs=[pl.BlockSpec(memory_space=pl.ANY), smem, smem, vmem],
        out_shape=[
            jax.ShapeDtypeStruct((slots, BLOCK, BLOCK), jnp.bfloat16),
            jax.ShapeDtypeStruct((SLOTS,), jnp.int32),
            jax.ShapeDtypeStruct((SLOTS,), jnp.int32),
            jax.ShapeDtypeStruct((N_SUB, 8, LENGTH) if last else sums, jnp.float32),
        ],
        scratch_shapes=[
            pltpu.VMEM((columns, BLOCK, DEPTH), jnp.bfloat16),
            pltpu.VMEM((columns, BLOCK, 128), jnp.float32),
            pltpu.VMEM((HALF, BLOCK, BLOCK), jnp.float32),
            pltpu.VMEM((HALF, BLOCK, BLOCK), jnp.float32),
            pltpu.VMEM((slots, BLOCK, BLOCK), jnp.bfloat16),
            pltpu.SemaphoreType.DMA((slots // UNROLL,)),
        ]
        + ([pltpu.VMEM(sums, jnp.float32)] if last else []),
        compiler_params=pltpu.CompilerParams(vmem_limit_bytes=VMEM_LIMIT),
        cost_estimate=pl.CostEstimate(
            flops=8 * len(windows) * 2 * DEPTH * BLOCK * BLOCK,
            bytes_accessed=7 * 2**20,
            transcendentals=8 * len(windows) * BLOCK * BLOCK,
        ),
    )(mine, blocks, rate, *sources, extra)


def stacked(vectors):
    if vectors.dtype == jnp.bfloat16:
        return vectors
    high = vectors.astype(jnp.bfloat16)
    return jnp.concatenate([high, (vectors - high.astype(jnp.float32)).astype(jnp.bfloat16)], 0)


def sweep_kernel(parts, *refs):
    list_refs, tile_refs, vector_refs = refs[:4], refs[4:6], refs[6:9]
    out_refs, (held, total, tiles, sems) = refs[9:13], refs[13:]
    vecs = vector_refs[0].shape[1]

    def copy(k, at):
        span = pl.ds(at * UNROLL, UNROLL)
        place = pl.ds((STARTS[k] + at) * UNROLL, UNROLL)
        return pltpu.make_async_copy(tile_refs[k].at[span], tiles.at[place], sems.at[STARTS[k] + at])

    groups = [lax.div(list_refs[2 * k][COUNT] + (UNROLL - 1), UNROLL) for k in range(len(WINDOWS))]
    for k in range(len(WINDOWS)):

        def fetch(at, _, k=k):
            copy(k, at).start()
            return 0

        lax.fori_loop(0, groups[k], fetch, 0)

    here, there, far = vector_refs
    for k, vectors in enumerate(
        (here[0], there[0], here[1], there[1], here[2], there[2], far[...])
    ):
        both = stacked(vectors)
        for c in range(2):
            held[2 * k + c] = both[:, c * BLOCK : (c + 1) * BLOCK]
    total[...] = jnp.zeros_like(total)

    for k, slots in enumerate(PLACES):

        def step(at, _, k=k, slots=slots, rows_ref=list_refs[2 * k], cols_ref=list_refs[2 * k + 1]):
            copy(k, at).wait()
            terms = []
            for n in range(UNROLL):
                block = cols_ref[UNROLL * at + n]
                slot = 0
                for at_slot, found in enumerate(slots):
                    slot = jnp.where(lax.shift_right_logical(block, 1) == at_slot, found, slot)
                block = 2 * slot + (block & 1)
                tile = tiles[(STARTS[k] + at) * UNROLL + n]
                terms.append(jnp.dot(held[block], tile, preferred_element_type=jnp.float32))
            for n in range(UNROLL):
                total[rows_ref[UNROLL * at + n]] += terms[n]
            return 0

        lax.fori_loop(0, groups[k], step, 0)

    for e in range(N_SUB):
        for r in range(2):
            result = total[2 * e + r, :vecs]
            for part in range(1, parts):
                result = result + total[2 * e + r, part * vecs : (part + 1) * vecs]
            out_refs[e][:, pl.ds(r * BLOCK, BLOCK)] = result


def sweep(near, tiles):
    own = near[0]
    vecs = own.shape[1]
    smem = pl.BlockSpec(memory_space=pltpu.SMEM)
    vmem = pl.BlockSpec(memory_space=pltpu.VMEM)
    parts = 1 if own.dtype == jnp.bfloat16 else 2
    lists = [part for tile in tiles for part in tile[1:]]
    return pl.pallas_call(
        functools.partial(sweep_kernel, parts),
        in_specs=[smem] * 4 + [pl.BlockSpec(memory_space=pl.ANY)] * 2 + [vmem] * 3,
        out_specs=[vmem] * 4,
        out_shape=[jax.ShapeDtypeStruct((vecs, LENGTH), jnp.float32)] * 4,
        scratch_shapes=[
            pltpu.VMEM((14, parts * vecs, BLOCK), jnp.bfloat16),
            pltpu.VMEM((NOBODY + 1, parts * vecs, BLOCK), jnp.float32),
            pltpu.VMEM((GROUPS * UNROLL, BLOCK, BLOCK), jnp.bfloat16),
            pltpu.SemaphoreType.DMA((GROUPS,)),
        ],
        compiler_params=pltpu.CompilerParams(vmem_limit_bytes=SWEEP_LIMIT),
        cost_estimate=pl.CostEstimate(
            flops=50 * 2 * 128 * BLOCK * BLOCK, bytes_accessed=7 * 2**20, transcendentals=0
        ),
    )(*lists, *[tile[0] for tile in tiles], *near)


def exchanged(parts):
    return [parts[0]] + [shifted(parts[e], "sub", -e) for e in range(1, N_SUB)]


def gram_of(image):
    return lax.dot_general(
        image, image, TRANS_B, precision=lax.Precision.HIGHEST, preferred_element_type=jnp.float32
    )


def inverse_factor(gram):
    count = gram.shape[0]
    place = lax.broadcasted_iota(jnp.int32, (count, 1), 0)
    across = lax.broadcasted_iota(jnp.int32, (count, count), 1)
    identity = jnp.where(across == place, 1.0, 0.0)
    joined = jnp.concatenate([gram, identity], 1)
    for k in range(0, count, AT_ONCE):
        columns = [
            jnp.broadcast_to(joined[:, k + n : k + n + 1], joined.shape) for n in range(AT_ONCE)
        ]
        rows = [joined[k + n : k + n + 1, :] for n in range(AT_ONCE)]
        for n in range(AT_ONCE):
            at = slice(k + n, k + n + 1)
            factor = jnp.where(place > k + n, columns[n] * (1.0 / columns[n][at]), 0.0)
            for m in range(n + 1, AT_ONCE):
                columns[m] = columns[m] - factor * columns[m][at]
                rows[m] = rows[m] - factor[k + m : k + m + 1] * rows[n]
            joined = joined - factor * rows[n]
    pivots = jnp.sum(joined[:, :count] * identity, axis=1, keepdims=True)
    diagonal = jnp.sum(gram * identity, axis=1, keepdims=True)
    return joined[:, count:] / jnp.sqrt(pivots), jnp.min(pivots / diagonal)


def exact_dot(left, right):
    return jnp.dot(left, right, precision=lax.Precision.HIGHEST, preferred_element_type=jnp.float32)


def image_of(root_ref, part_refs):
    first, second, third, fourth = (part_ref[...] for part_ref in part_refs)
    return root_ref[...] * ((first + second) + (third + fourth))


def image_kernel(scaled, root_ref, *refs):
    image = image_of(root_ref, refs[:4])
    refs[4][...] = root_ref[...] * image if scaled else image
    refs[5][...] = gram_of(image)


def solve_gram_kernel(gram_ref, image_ref, solved_ref, next_ref):
    image = exact_dot(inverse_factor(gram_ref[...])[0], image_ref[...])
    solved_ref[...] = image
    next_ref[...] = gram_of(image)


def solve_kernel(gram_ref, image_ref, solved_ref):
    solved_ref[...] = exact_dot(inverse_factor(gram_ref[...])[0], image_ref[...])


def solve_both_kernel(grams_ref, image_ref, solved_ref, sound_ref):
    count = image_ref.shape[0]
    first, quality = inverse_factor(grams_ref[:count])
    half = lax.dot_general(
        grams_ref[count:], first, TRANS_B, precision=lax.Precision.HIGHEST,
        preferred_element_type=jnp.float32,
    )
    second, next_quality = inverse_factor(exact_dot(first, half))
    solved_ref[...] = exact_dot(second, exact_dot(first, image_ref[...]))
    sound_ref[0] = jnp.where((quality > 0.05) & (next_quality > 0.001), 1, 0)


def payload_kernel(pairs_ref, data_ref, scale_ref, payload_ref, wide_ref):
    n_space, n_sub = lax.axis_size("space"), lax.axis_size("sub")
    space_at, sub_at = lax.axis_index("space"), lax.axis_index("sub")
    lane = lax.broadcasted_iota(jnp.int32, (1, LENGTH), 1)
    used = jnp.zeros((1, LENGTH), jnp.float32)
    for k in range(pairs_ref.shape[1]):
        row, col = pairs_ref[0, k], pairs_ref[1, k]
        device = lax.shift_right_logical(col, 1)
        hop = lax.rem(lax.div(device, n_sub) - space_at + n_space, n_space)
        across = lax.rem(lax.rem(device, n_sub) - sub_at + n_sub, n_sub)
        place = (((hop - 1) * n_sub + across) * 2 + (row & 1)) * 2 + (col & 1)
        used = jnp.where((lane == place) & (hop > 0), 1.0, used)
    payload_ref[: ROWS - 16] = data_ref[: ROWS - 16]
    wide_ref[: ROWS - 16] = data_ref[: ROWS - 16]
    last = jnp.concatenate(
        [
            data_ref[ROWS - 16 : FEAT].astype(jnp.float32),
            scale_ref[...].astype(jnp.float32).reshape(1, LENGTH),
            used,
            jnp.zeros((ROWS - MASK_ROW - 1, LENGTH), jnp.float32),
        ],
        0,
    ).astype(jnp.bfloat16)
    payload_ref[ROWS - 16 :] = last
    wide_ref[ROWS - 16 : ROWS] = last
    wide_ref[ROWS:] = jnp.zeros((WIDE - ROWS, LENGTH), jnp.bfloat16)


def on_device(trajectories, kernel_scale, start_vectors, pair_list):
    vecs, length = start_vectors.shape
    light = dict(
        cost_estimate=pl.CostEstimate(flops=2**20, bytes_accessed=2**17, transcendentals=0),
        compiler_params=pltpu.CompilerParams(vmem_limit_bytes=SMALL_LIMIT),
    )

    payload, wide = pl.pallas_call(
        payload_kernel,
        in_specs=[pl.BlockSpec(memory_space=pltpu.SMEM)] + [pl.BlockSpec(memory_space=pltpu.VMEM)] * 2,
        out_shape=[jax.ShapeDtypeStruct((rows, length), jnp.bfloat16) for rows in (ROWS, WIDE)],
        cost_estimate=light["cost_estimate"],
        compiler_params=pltpu.CompilerParams(vmem_limit_bytes=PAYLOAD_LIMIT),
    )(pair_list.T, trajectories, kernel_scale)

    members = [wide] + [shifted(wide, "sub", e) for e in range(1, N_SUB)]
    ahead, behind = shifted(payload, "space", 2), shifted(payload, "space", -2)
    later, ahead, behind = lax.optimization_barrier((payload, ahead, behind))
    there = swapped(later), swapped(ahead), swapped(behind)
    far = lax.ppermute(later, "space", far_pairs(lax.axis_size("space")))
    blocks, rate = row_operands(members)
    listed = jnp.stack([member[MASK_ROW, : REACH * PAIRS] for member in members]).astype(jnp.int32)
    listed = listed.reshape(N_SUB * REACH * PAIRS)

    tiles = []
    carried = wide
    for at, sources in enumerate(((ahead, behind), (*there, far))):
        *tile, carried = hop_tiles(
            WINDOWS[at], at == 0, at == len(WINDOWS) - 1, listed, blocks, rate, sources, carried
        )
        tiles.append(tile)
    degree = carried
    shares = exchanged([degree[e, :1] for e in range(N_SUB)])
    root = lax.rsqrt((shares[0] + shares[1]) + (shares[2] + shares[3]))

    vector_shape = jax.ShapeDtypeStruct((vecs, length), jnp.float32)
    gram_shape = jax.ShapeDtypeStruct((vecs, vecs), jnp.float32)
    def imaged(parts, scaled):
        return pl.pallas_call(
            functools.partial(image_kernel, scaled), out_shape=[vector_shape, gram_shape], **light
        )(root, *exchanged(parts))

    scaled = (root * start_vectors).astype(jnp.bfloat16)
    raw, first_gram = imaged(sweep(space_window(scaled), tiles), True)

    image, second_gram = imaged(sweep(space_window(raw), tiles), False)
    grams = summed(jnp.concatenate([first_gram, second_gram], 0))
    subspace, sound = pl.pallas_call(
        solve_both_kernel,
        in_specs=[pl.BlockSpec(memory_space=pltpu.VMEM)] * 2,
        out_specs=[pl.BlockSpec(memory_space=pltpu.VMEM), pl.BlockSpec(memory_space=pltpu.SMEM)],
        out_shape=[vector_shape, jax.ShapeDtypeStruct((1,), jnp.int32)],
        **light,
    )(grams, image)

    def directly():
        solved, gram = pl.pallas_call(
            solve_gram_kernel, out_shape=[vector_shape, gram_shape], **light
        )(grams[:vecs], image)
        return pl.pallas_call(solve_kernel, out_shape=vector_shape, **light)(summed(gram), solved)

    return lax.cond(sound[0] > 0, lambda: subspace, directly)


def solution(mesh):
    placed = (
        P(None, ("space", "sub")),
        P(("space", "sub")),
        P(None, ("space", "sub")),
        P(("space", "sub"), None),
    )
    return jax.shard_map(
        on_device, mesh=mesh, in_specs=placed, out_specs=P(None, ("space", "sub")), check_vma=False
    )
```
